128 devices in a mesh: img: 16 (over z, y), txt: 8 (over x, core).
Axes of the slice: x: 4, y: 4, z: 4, core: 2. Of those that a mesh axis runs over, the one named last changes fastest.
Arguments:
- image_emb: bfloat16 [24576, 512], P(('img', 'txt')), may hold values from -8 to 8, as said below
- text_emb: bfloat16 [24576, 512], P(('img', 'txt')), may hold values from -8 to 8
Outputs:
- loss: float32 [], replicated
- grad_image: float32 [24576, 512], P(('img', 'txt'))
- grad_text: float32 [24576, 512], P(('img', 'txt'))
The draws below stay inside these ranges and needn't reach their ends.
Inputs may be any that keep to these rules, and one draw needn't show every extreme that they name: `image_emb`: image row k is, for most k, correlated with text row k.
All inputs are finite; a program needn't handle non-finite values.
Results may differ from the reference program's by a relative error of at most 0.004.
Values may be sent and summed in bfloat16 or wider, within the bound.
No kernel may reach another device: no remote copies, remote signals or barrier semaphores. Data moves between devices by JAX's collectives and lax.ppermute only.
A program may use at most 128 MiB of HBM per device.

```python
import math
import jax
import jax.numpy as jnp
from jax import lax

E = 512
BATCH = 24576


def shared_base(key):
    return jax.random.truncated_normal(key, -4.0, 4.0, (BATCH, E), jnp.float32)


def draw_image_emb(key, part):
    common = shared_base(key)
    values = common / math.sqrt(E)
    return values.astype(jnp.bfloat16)


def draw_text_emb(key, part):
    common = shared_base(key)
    key = jax.random.fold_in(key, 12)
    noise_key = jax.random.fold_in(key, 0)
    noise = jax.random.truncated_normal(noise_key, -4.0, 4.0, (BATCH, E), jnp.float32)
    values = 0.7 * (common + noise) / math.sqrt(E)
    return values.astype(jnp.bfloat16)


def setup_inputs(seed: int = 0) -> dict:
    key_of = jax.random.split(jax.random.key(seed), 3)
    image_emb = draw_image_emb(jax.random.fold_in(key_of[2], 71), 0)
    text_emb = draw_text_emb(jax.random.fold_in(key_of[2], 71), 0)
    return {"image_emb": image_emb, "text_emb": text_emb}


logit_scale = 10.0


def reference(image_emb, text_emb):
    images = image_emb.astype(jnp.float32)
    texts = text_emb.astype(jnp.float32)
    block_rows = math.gcd(BATCH, 512)
    block_count = BATCH // block_rows
    columns = jnp.arange(BATCH, dtype=jnp.int32)

    def block_logits(block_index):
        block_start = (block_index * block_rows).astype(jnp.int32)
        chosen = lax.dynamic_slice_in_dim(images, block_start, block_rows, 0)
        logits = logit_scale * lax.dot_general(chosen, texts, (((1,), (1,)), ((), ())), precision=lax.Precision.HIGHEST)
        return chosen, logits, block_start

    def forward(running, block_index):
        col_max, col_sum, diag_sum = running
        chosen, logits, block_start = block_logits(block_index)
        row_max = jnp.max(logits, axis=1)
        row_lse = row_max + jnp.log(jnp.sum(jnp.exp(logits - row_max[:, None]), axis=1))
        new_max = jnp.maximum(col_max, jnp.max(logits, axis=0))
        col_sum = col_sum * jnp.exp(col_max - new_max) + jnp.sum(jnp.exp(logits - new_max[None, :]), axis=0)
        positive = lax.dynamic_slice_in_dim(texts, block_start, block_rows, 0)
        diag_sum = diag_sum + logit_scale * jnp.sum(chosen * positive)
        return (new_max, col_sum, diag_sum), row_lse

    initial = (jnp.full((BATCH,), -jnp.inf, jnp.float32), jnp.zeros((BATCH,), jnp.float32), jnp.zeros((), jnp.float32))
    (col_max, col_sum, diag_sum), row_lse = lax.scan(forward, initial, jnp.arange(block_count, dtype=jnp.int32))
    row_lse = row_lse.reshape(BATCH)
    col_lse = col_max + jnp.log(col_sum)
    loss = 0.5 * (jnp.sum(row_lse) + jnp.sum(col_lse) - 2.0 * diag_sum) / BATCH

    def backward(text_grad, block_index):
        chosen, logits, block_start = block_logits(block_index)
        lse_rows = lax.dynamic_slice_in_dim(row_lse, block_start, block_rows, 0)
        is_positive = (block_start + jnp.arange(block_rows, dtype=jnp.int32))[:, None] == columns[None, :]
        coeffs = 0.5 * (jnp.exp(logits - lse_rows[:, None]) + jnp.exp(logits - col_lse[None, :])) - is_positive.astype(jnp.float32)
        coeffs = lax.optimization_barrier(coeffs.astype(jnp.bfloat16)).astype(jnp.float32)
        image_grad = logit_scale * jnp.dot(coeffs, texts, precision=lax.Precision.HIGHEST)
        text_grad = text_grad + logit_scale * lax.dot_general(coeffs, chosen, (((0,), (0,)), ((), ())), precision=lax.Precision.HIGHEST)
        return text_grad, image_grad

    text_grad, image_grad = lax.scan(backward, jnp.zeros((BATCH, E), jnp.float32), jnp.arange(block_count, dtype=jnp.int32))
    return loss, image_grad.reshape(BATCH, E), text_grad
```

```python
import functools
import itertools
import math

import jax
import jax.numpy as jnp
from jax import lax
from jax.experimental import pallas as pl
from jax.experimental.pallas import tpu as pltpu
from jax.sharding import Mesh, PartitionSpec as P


logit_scale = 10.0
log2e = 1.4426950408889634
ln2 = 0.6931471805599453
lowest = -1e30
f32 = jnp.float32
bf16 = jnp.bfloat16
AXES = ("z", "y", "x", "c")
SWAP = ((0, 1), (1, 0))
FLIPS = ((0, 0, 1), (0, 1, 0), (1, 0, 0))
IMAGE_PAIR = (1, 0, 3, 2)
TEXT_PAIR = (3, 2, 1, 0)
VMEM = pl.BlockSpec(memory_space=pltpu.VMEM)
SMEM = pl.BlockSpec(memory_space=pltpu.SMEM)


def role_pairs(flip):
    pairs = []
    for z, y, x in itertools.product(range(4), repeat=3):
        for core, pair in ((0, IMAGE_PAIR), (1, TEXT_PAIR)):
            target = [pair[v] if f else v for v, f in zip((z, y, x), flip)]
            source_id = ((z * 4 + y) * 4 + x) * 2 + core
            target_id = ((target[0] * 4 + target[1]) * 4 + target[2]) * 2 + core
            pairs.append((source_id, target_id))
    return pairs


ROLE_PAIRS = [role_pairs(flip) for flip in FLIPS]


def flip_permute(x, dim):
    return lax.ppermute(x, AXES, ROLE_PAIRS[dim % 3])


def core_swap(x):
    return lax.ppermute(x, "c", SWAP)


def call(kernel, name, ins, outs, scratch=(), limit=26, flops=0, moved=0):
    in_specs = [SMEM if i == 0 else VMEM for i in range(len(ins))]
    return pl.pallas_call(
        kernel,
        in_specs=in_specs,
        out_specs=[VMEM] * len(outs),
        out_shape=list(outs),
        scratch_shapes=list(scratch),
        compiler_params=pltpu.CompilerParams(vmem_limit_bytes=limit << 20),
        cost_estimate=pl.CostEstimate(flops=flops, bytes_accessed=moved, transcendentals=0),
        name=name,
    )(*ins)


def held(x):
    return pltpu.with_memory_space_constraint(x, pltpu.VMEM)


def shape(*dims, dtype=f32):
    return jax.ShapeDtypeStruct(dims, dtype)


def forward_kernel(core_ref, image_ref, text_ref, *refs):
    near_x, far_x, near, far = refs[0:3], refs[3:6], refs[6:9], refs[9:12]
    rows_ref, cols_ref = refs[12:14]
    logit_refs = refs[14:17]
    send_ref, keep_ref = refs[17:19]
    core = core_ref[0]
    n = 512

    @pl.when(core == 0)
    def _():
        for q in range(3):
            rows_ref[q * n : q * n + n, :] = far[q][...]
            cols_ref[q * n : q * n + n, :] = near_x[q][...]
            cols_ref[(q + 3) * n : (q + 3) * n + n, :] = far_x[q][...]

    @pl.when(core != 0)
    def _():
        for q in range(3):
            rows_ref[q * n : q * n + n, :] = near_x[q][...]
            cols_ref[q * n : q * n + n, :] = near[q][...]
            cols_ref[(q + 3) * n : (q + 3) * n + n, :] = far[q][...]

    width = cols_ref.shape[0]
    top = jnp.full((1, width), -jnp.inf, f32)
    total = jnp.zeros((1, width), f32)
    row_blocks = []
    for q in range(3):
        logits = lax.dot_general(
            rows_ref[q * n : q * n + n, :], cols_ref[...], (((1,), (1,)), ((), ())), preferred_element_type=f32
        ) * (logit_scale * log2e)
        logit_refs[q][...] = logits
        row_top = jnp.max(logits, axis=1, keepdims=True)
        row_total = jnp.sum(jnp.exp2(logits - row_top), axis=1, keepdims=True)
        row = jnp.broadcast_to(row_top + jnp.log2(row_total), (n, 128)).T[0:1, :]
        row_blocks += [row[:, k * 128 : k * 128 + 128] for k in range(4)]
        new_top = jnp.maximum(top, jnp.max(logits, axis=0, keepdims=True))
        total = total * jnp.exp2(top - new_top) + jnp.sum(jnp.exp2(logits - new_top), axis=0, keepdims=True)
        top = new_top
    col = top + jnp.log2(total)
    positive = logit_scale * jnp.sum(image_ref[...].astype(f32) * text_ref[...].astype(f32))
    extra = jnp.full((8, 128), positive, f32)
    row_part = jnp.concatenate(row_blocks, 0)
    col_part = jnp.concatenate([col[:, k * 128 : k * 128 + 128] for k in range(24)], 0)
    blank = jnp.full((12, 128), lowest, f32)
    is_first = core == 0
    send_ref[0:24, :] = jnp.where(is_first, col_part, jnp.concatenate([row_part, blank], 0))
    keep_ref[0:24, :] = jnp.where(is_first, jnp.concatenate([blank, row_part], 0), col_part)
    send_ref[24:32, :] = extra
    keep_ref[24:32, :] = extra


def join_kernel(order, core_ref, mine_ref, got_ref, out_ref):
    a = mine_ref[0:24, :]
    got = got_ref[...]
    b = jnp.concatenate([got[k : k + 1, :] for k in order], 0)
    top = jnp.maximum(a, b)
    out_ref[0:24, :] = top + jnp.log2(jnp.exp2(a - top) + jnp.exp2(b - top))
    out_ref[24:32, :] = mine_ref[24:32, :] + got_ref[24:32, :]


def flip_order(dim):
    order = []
    for half, q, k in itertools.product(range(2), range(3), range(4)):
        j = (dim - q) % 3
        if j == 2:
            order.append((1 - half) * 12 + q * 4 + k)
        else:
            order.append(half * 12 + q * 4 + (k ^ (1 << j)))
    return order


def coeff_kernel(core_ref, mine_ref, got_ref, cols_ref, *refs):
    logit_refs = refs[0:3]
    coeff_ref = refs[3]
    grad_refs = refs[4:7]
    own_ref, loss_ref = refs[7:9]
    core = core_ref[0]
    is_first = core == 0
    n = 512
    mine = mine_ref[...]
    got = got_ref[...]
    row_lse = jnp.where(is_first, mine[12:24], got[0:12]) + 1.0
    col_lse = jnp.where(is_first, got[0:24], mine[0:24]) + 1.0
    row_lse = jnp.concatenate([row_lse[k : k + 1] for k in range(12)], 1)
    col_lse = jnp.concatenate([col_lse[k : k + 1] for k in range(24)], 1)
    lse_sum = jnp.sum(got[0:24]) * ln2
    loss_ref[...] = jnp.full((8, 128), lse_sum, f32) - jnp.where(is_first, 0.0, 2.0) * got[24:32]
    eye = lax.broadcasted_iota(jnp.int32, (128, 128), 0) == lax.broadcasted_iota(jnp.int32, (128, 128), 1)
    positive = jnp.where(jnp.logical_and(eye, core != 0), 1.0, 0.0)
    for q in range(3):
        row = jnp.broadcast_to(row_lse[:, q * n : q * n + n], (128, n)).T[:, 0:1]
        logits = logit_refs[q][...]
        coeffs = jnp.exp2(logits - row) + jnp.exp2(logits - col_lse)
        coeff_ref[q * n : q * n + n, :] = coeffs.astype(bf16)
        own = slice(q * n, q * n + 128)
        coeff_ref[own, own] = (coeffs[0:128, own] - positive).astype(bf16)
        grad = logit_scale * jnp.dot(coeff_ref[q * n : q * n + n, :], cols_ref[...], preferred_element_type=f32)
        own_ref[q * 128 : q * 128 + 128, :] = grad[0:128, :]
        grad_refs[q][0:128, :] = jnp.where(is_first, grad[0:128, :], 0.0).astype(bf16)
        grad_refs[q][128:n, :] = grad[128:n, :].astype(bf16)


def text_grad(coeff_ref, rows_ref, start):
    return logit_scale * lax.dot_general(
        coeff_ref[:, start : start + 512], rows_ref[...], (((0,), (0,)), ((), ())), preferred_element_type=f32
    )


def far_text_kernel(core_ref, coeff_ref, rows_ref, out_ref):
    for q in range(3):
        out_ref[q * 512 : q * 512 + 512, :] = text_grad(coeff_ref, rows_ref, 1536 + q * 512).astype(bf16)


def near_text_kernel(core_ref, coeff_ref, rows_ref, g0, g1, g2, loss_ref, loss_got, base_ref, send_ref, loss_out):
    core = core_ref[0]
    loss_out[...] = loss_ref[...] + loss_got[...]
    for q, g in enumerate((g0, g1, g2)):
        rows = slice(q * 512, q * 512 + 512)
        grad = text_grad(coeff_ref, rows_ref, q * 512)
        base_ref[rows, :] = jnp.where(core == 0, 0.0, grad)
        send_ref[rows, :] = jnp.where(core == 0, grad.astype(bf16), g[...])


def far_message_kernel(core_ref, g0, g1, g2, text_ref, got_ref, m0, m1, m2):
    core = core_ref[0]
    for q, (g, m) in enumerate(((g0, m0), (g1, m1), (g2, m2))):
        rows = slice(q * 512, q * 512 + 512)
        both = (text_ref[rows, :].astype(f32) + got_ref[rows, :].astype(f32)).astype(bf16)
        m[...] = jnp.where(core == 0, g[...], both)


def near_sum_kernel(core_ref, base_ref, got_ref, r0, r1, r2, loss_ref, loss_got, low_ref, s0, s1, s2, loss_out):
    loss_out[...] = loss_ref[...] + loss_got[...]
    for q, (r, s) in enumerate(((r0, s0), (r1, s1), (r2, s2))):
        rows = slice(q * 512, q * 512 + 512)
        total = base_ref[rows, :] + got_ref[rows, :].astype(f32) + r[...].astype(f32)
        low_ref[q * 256 : q * 256 + 256, :] = total[0:256]
        s[...] = total[256:512].astype(bf16)


def half_sum_kernel(core_ref, low_ref, r0, r1, r2, loss_ref, loss_got, out_ref, s0, s1, s2, loss_out):
    loss_out[...] = loss_ref[...] + loss_got[...]
    for q, (r, s) in enumerate(((r0, s0), (r1, s1), (r2, s2))):
        total = low_ref[q * 256 : q * 256 + 256, :] + r[...].astype(f32)
        out_ref[q * 128 : q * 128 + 128, :] = total[0:128]
        s[...] = total[128:256].astype(bf16)


def last_sum_kernel(core_ref, low_ref, r0, r1, r2, own_ref, loss_ref, keep_ref, send_ref):
    first = core_ref[0] == 0
    for q, r in enumerate((r0, r1, r2)):
        rows = slice(q * 64, q * 64 + 64)
        total = low_ref[q * 128 : q * 128 + 128, :] + r[...].astype(f32)
        keep_ref[rows, :] = jnp.where(first, total[0:64], total[64:128])
        send_ref[rows, :] = jnp.where(first, total[64:128], total[0:64])
        send_ref[192 + q * 64 : 192 + q * 64 + 64, :] = own_ref[q * 128 : q * 128 + 64, :]
    send_ref[384:392, :] = jnp.concatenate([loss_ref[...]] * 4, 1)


def finish_kernel(count, core_ref, keep_ref, got_ref, own_ref, loss_ref, image_out, text_out, loss_out):
    first = core_ref[0] == 0
    for q in range(3):
        rows = slice(q * 64, q * 64 + 64)
        keep = keep_ref[rows, :]
        got = got_ref[rows, :]
        own_mine = own_ref[q * 128 + 64 : q * 128 + 128, :]
        own_got = got_ref[192 + q * 64 : 192 + q * 64 + 64, :]
        image_out[rows, :] = jnp.where(first, keep + own_got, got + own_mine)
        text_out[rows, :] = jnp.where(first, got, keep)
    loss_out[...] = (loss_ref[...] + got_ref[384:392, 0:128]) * (0.5 / count)


def per_device(image_emb, text_emb):
    core = lax.axis_index("c")
    core_id = core.reshape(1).astype(jnp.int32)
    pair_rows, width = image_emb.shape
    count = pair_rows * 128

    swapped = core_swap(jnp.where(core == 0, text_emb, image_emb))
    near = []
    for q in range(3):
        rows = slice(q * 64, q * 64 + 64)
        first = jnp.where(core == 0, image_emb[rows], swapped[rows])
        second = jnp.where(core == 0, swapped[rows], text_emb[rows])
        near.append(jnp.concatenate([first, second], 0))
    for step in range(2):
        got = [flip_permute(near[q], q + step) for q in range(3)]
        near = [jnp.concatenate([a, b], 0) for a, b in zip(near, got)]
    far = [flip_permute(near[q], q + 2) for q in range(3)]
    near_x = [core_swap(a) for a in near]
    far_x = [core_swap(a) for a in far]

    rows, cols, l0, l1, l2, send, keep = call(
        forward_kernel,
        "forward",
        [core_id, image_emb, text_emb, *near_x, *far_x, *near, *far],
        [pltpu.VMEM((1536, width), bf16), pltpu.VMEM((3072, width), bf16)]
        + [pltpu.VMEM((512, 3072), f32)] * 3
        + [shape(32, 128), shape(32, 128)],
        flops=2 * 1536 * 3072 * 512,
    )

    mine = call(functools.partial(join_kernel, list(range(24))), "join", [core_id, keep, core_swap(send)], [shape(32, 128)])[0]
    for dim in range(3):
        got = flip_permute(mine, dim)
        mine = call(functools.partial(join_kernel, flip_order(dim)), "join", [core_id, mine, got], [shape(32, 128)])[0]
    other = core_swap(mine)

    coeffs, g0, g1, g2, own, loss = call(
        coeff_kernel,
        "coeffs",
        [core_id, mine, other, held(cols), held(l0), held(l1), held(l2)],
        [pltpu.VMEM((1536, 3072), bf16)] + [shape(512, width, dtype=bf16)] * 3 + [shape(384, width), shape(8, 128)],
        flops=2 * 1536 * 3072 * 512,
    )
    text_far = call(
        far_text_kernel, "text_far", [core_id, held(coeffs), held(rows)], [shape(1536, width, dtype=bf16)], flops=1536 * 3072 * 512
    )[0]
    text_far_got = core_swap(text_far)
    loss_got = flip_permute(loss, 0)
    base, near_send, loss = call(
        near_text_kernel,
        "text_near",
        [core_id, held(coeffs), held(rows), g0, g1, g2, loss, loss_got],
        [shape(1536, width), shape(1536, width, dtype=bf16), shape(8, 128)],
        flops=1536 * 3072 * 512,
    )
    near_got = core_swap(near_send)
    loss_got = flip_permute(loss, 1)
    messages = call(
        far_message_kernel, "far_message", [core_id, g0, g1, g2, text_far, text_far_got], [shape(512, width, dtype=bf16)] * 3
    )
    got = [flip_permute(messages[q], q + 2) for q in range(3)]
    low, *messages, loss = call(
        near_sum_kernel,
        "near_sum",
        [core_id, base, near_got, *got, loss, loss_got],
        [shape(768, width)] + [shape(256, width, dtype=bf16)] * 3 + [shape(8, 128)],
    )
    got = [flip_permute(messages[q], q + 1) for q in range(3)]
    loss_got = flip_permute(loss, 2)
    low, *messages, loss = call(
        half_sum_kernel,
        "half_sum",
        [core_id, low, *got, loss, loss_got],
        [shape(384, width)] + [shape(128, width, dtype=bf16)] * 3 + [shape(8, 128)],
    )
    got = [flip_permute(messages[q], q) for q in range(3)]
    keep, send = call(
        last_sum_kernel, "last_sum", [core_id, low, *got, own, loss], [shape(192, width), shape(392, width)]
    )
    swapped = core_swap(send)
    grad_image, grad_text, loss = call(
        functools.partial(finish_kernel, count),
        "finish",
        [core_id, keep, swapped, own, loss],
        [shape(192, width), shape(192, width), shape(8, 128)],
    )
    return loss[0, 0], grad_image, grad_text


def solution(mesh):
    fine = Mesh(mesh.devices.reshape(4, 4, 4, 2), AXES)
    return jax.shard_map(
        per_device,
        mesh=fine,
        in_specs=(P(AXES, None), P(AXES, None)),
        out_specs=(P(), P(AXES, None), P(AXES, None)),
        check_vma=False,
    )
```

```python
import functools
import itertools
import math

import jax
import jax.numpy as jnp
from jax import lax
from jax.experimental import pallas as pl
from jax.experimental.pallas import tpu as pltpu
from jax.sharding import Mesh, PartitionSpec as P


logit_scale = 10.0
log2e = 1.4426950408889634
ln2 = 0.6931471805599453
lowest = -1e30
f32 = jnp.float32
bf16 = jnp.bfloat16
AXES = ("z", "y", "x", "c")
SWAP = ((0, 1), (1, 0))
FLIPS = ((0, 0, 1), (0, 1, 0), (1, 0, 0))
IMAGE_PAIR = (1, 0, 3, 2)
TEXT_PAIR = (3, 2, 1, 0)
VMEM = pl.BlockSpec(memory_space=pltpu.VMEM)
SMEM = pl.BlockSpec(memory_space=pltpu.SMEM)


def role_pairs(flip):
    pairs = []
    for z, y, x in itertools.product(range(4), repeat=3):
        for core, pair in ((0, IMAGE_PAIR), (1, TEXT_PAIR)):
            target = [pair[v] if f else v for v, f in zip((z, y, x), flip)]
            source_id = ((z * 4 + y) * 4 + x) * 2 + core
            target_id = ((target[0] * 4 + target[1]) * 4 + target[2]) * 2 + core
            pairs.append((source_id, target_id))
    return pairs


ROLE_PAIRS = [role_pairs(flip) for flip in FLIPS]


def flip_permute(x, dim):
    return lax.ppermute(x, AXES, ROLE_PAIRS[dim % 3])


def core_swap(x):
    return lax.ppermute(x, "c", SWAP)


def call(kernel, name, ins, outs, scratch=(), limit=6, flops=0, moved=0):
    in_specs = [SMEM if i == 0 else VMEM for i in range(len(ins))]
    return pl.pallas_call(
        kernel,
        in_specs=in_specs,
        out_specs=[VMEM] * len(outs),
        out_shape=list(outs),
        scratch_shapes=list(scratch),
        compiler_params=pltpu.CompilerParams(vmem_limit_bytes=limit << 20),
        cost_estimate=pl.CostEstimate(flops=flops, bytes_accessed=moved, transcendentals=0),
        name=name,
    )(*ins)


def held(x):
    return pltpu.with_memory_space_constraint(x, pltpu.VMEM)


def shape(*dims, dtype=f32):
    return jax.ShapeDtypeStruct(dims, dtype)


def forward_kernel(core_ref, image_ref, text_ref, *refs):
    near_x, far_x, near, far = refs[0:3], refs[3:6], refs[6:9], refs[9:12]
    rows_ref, cols_ref = refs[12:14]
    logit_refs = refs[14:17]
    send_ref, keep_ref = refs[17:19]
    core = core_ref[0]
    n = 512

    @pl.when(core == 0)
    def _():
        for q in range(3):
            rows_ref[q * n : q * n + n, :] = far[q][...]
            cols_ref[q * n : q * n + n, :] = near_x[q][...]
            cols_ref[(q + 3) * n : (q + 3) * n + n, :] = far_x[q][...]

    @pl.when(core != 0)
    def _():
        for q in range(3):
            rows_ref[q * n : q * n + n, :] = near_x[q][...]
            cols_ref[q * n : q * n + n, :] = near[q][...]
            cols_ref[(q + 3) * n : (q + 3) * n + n, :] = far[q][...]

    width = cols_ref.shape[0]
    top = jnp.full((1, width), -jnp.inf, f32)
    total = jnp.zeros((1, width), f32)
    row_blocks = []
    for q in range(3):
        logits = lax.dot_general(
            rows_ref[q * n : q * n + n, :], cols_ref[...], (((1,), (1,)), ((), ())), preferred_element_type=f32
        ) * (logit_scale * log2e)
        logit_refs[q][...] = logits
        row_top = jnp.max(logits, axis=1, keepdims=True)
        row_total = jnp.sum(jnp.exp2(logits - row_top), axis=1, keepdims=True)
        row = jnp.broadcast_to(row_top + jnp.log2(row_total), (n, 128)).T[0:1, :]
        row_blocks += [row[:, k * 128 : k * 128 + 128] for k in range(4)]
        new_top = jnp.maximum(top, jnp.max(logits, axis=0, keepdims=True))
        total = total * jnp.exp2(top - new_top) + jnp.sum(jnp.exp2(logits - new_top), axis=0, keepdims=True)
        top = new_top
    col = top + jnp.log2(total)
    positive = logit_scale * jnp.sum(image_ref[...].astype(f32) * text_ref[...].astype(f32))
    extra = jnp.full((8, 128), positive, f32)
    row_part = jnp.concatenate(row_blocks, 0)
    col_part = jnp.concatenate([col[:, k * 128 : k * 128 + 128] for k in range(24)], 0)
    blank = jnp.full((12, 128), lowest, f32)
    is_first = core == 0
    send_ref[0:24, :] = jnp.where(is_first, col_part, jnp.concatenate([row_part, blank], 0))
    keep_ref[0:24, :] = jnp.where(is_first, jnp.concatenate([blank, row_part], 0), col_part)
    send_ref[24:32, :] = extra
    keep_ref[24:32, :] = extra


def join_kernel(order, core_ref, mine_ref, got_ref, out_ref):
    a = mine_ref[0:24, :]
    got = got_ref[...]
    b = jnp.concatenate([got[k : k + 1, :] for k in order], 0)
    top = jnp.maximum(a, b)
    out_ref[0:24, :] = top + jnp.log2(jnp.exp2(a - top) + jnp.exp2(b - top))
    out_ref[24:32, :] = mine_ref[24:32, :] + got_ref[24:32, :]


def flip_order(dim):
    order = []
    for half, q, k in itertools.product(range(2), range(3), range(4)):
        j = (dim - q) % 3
        if j == 2:
            order.append((1 - half) * 12 + q * 4 + k)
        else:
            order.append(half * 12 + q * 4 + (k ^ (1 << j)))
    return order


def coeff_kernel(core_ref, mine_ref, got_ref, cols_ref, *refs):
    logit_refs = refs[0:3]
    coeff_ref = refs[3]
    grad_refs = refs[4:7]
    own_ref, loss_ref = refs[7:9]
    core = core_ref[0]
    is_first = core == 0
    n = 512
    mine = mine_ref[...]
    got = got_ref[...]
    row_lse = jnp.where(is_first, mine[12:24], got[0:12]) + 1.0
    col_lse = jnp.where(is_first, got[0:24], mine[0:24]) + 1.0
    row_lse = jnp.concatenate([row_lse[k : k + 1] for k in range(12)], 1)
    col_lse = jnp.concatenate([col_lse[k : k + 1] for k in range(24)], 1)
    lse_sum = jnp.sum(got[0:24]) * ln2
    loss_ref[...] = jnp.full((8, 128), lse_sum, f32) - jnp.where(is_first, 0.0, 2.0) * got[24:32]
    eye = lax.broadcasted_iota(jnp.int32, (128, 128), 0) == lax.broadcasted_iota(jnp.int32, (128, 128), 1)
    positive = jnp.where(jnp.logical_and(eye, core != 0), 1.0, 0.0)
    for q in range(3):
        row = jnp.broadcast_to(row_lse[:, q * n : q * n + n], (128, n)).T[:, 0:1]
        logits = logit_refs[q][...]
        coeffs = jnp.exp2(logits - row) + jnp.exp2(logits - col_lse)
        coeff_ref[q * n : q * n + n, :] = coeffs.astype(bf16)
        own = slice(q * n, q * n + 128)
        coeff_ref[own, own] = (coeffs[0:128, own] - positive).astype(bf16)
        grad = logit_scale * jnp.dot(coeff_ref[q * n : q * n + n, :], cols_ref[...], preferred_element_type=f32)
        own_ref[q * 128 : q * 128 + 128, :] = grad[0:128, :]
        grad_refs[q][0:128, :] = jnp.where(is_first, grad[0:128, :], 0.0).astype(bf16)
        grad_refs[q][128:n, :] = grad[128:n, :].astype(bf16)


def text_grad(coeff_ref, rows_ref, start):
    return logit_scale * lax.dot_general(
        coeff_ref[:, start : start + 512], rows_ref[...], (((0,), (0,)), ((), ())), preferred_element_type=f32
    )


def far_text_kernel(core_ref, coeff_ref, rows_ref, out_ref):
    for q in range(3):
        out_ref[q * 512 : q * 512 + 512, :] = text_grad(coeff_ref, rows_ref, 1536 + q * 512).astype(bf16)


def near_text_kernel(core_ref, coeff_ref, rows_ref, g0, g1, g2, base_ref, send_ref):
    core = core_ref[0]
    for q, g in enumerate((g0, g1, g2)):
        rows = slice(q * 512, q * 512 + 512)
        grad = text_grad(coeff_ref, rows_ref, q * 512)
        base_ref[rows, :] = jnp.where(core == 0, 0.0, grad)
        send_ref[rows, :] = jnp.where(core == 0, grad.astype(bf16), g[...])


def far_message_kernel(core_ref, g0, g1, g2, text_ref, got_ref, m0, m1, m2):
    core = core_ref[0]
    for q, (g, m) in enumerate(((g0, m0), (g1, m1), (g2, m2))):
        rows = slice(q * 512, q * 512 + 512)
        both = (text_ref[rows, :].astype(f32) + got_ref[rows, :].astype(f32)).astype(bf16)
        m[...] = jnp.where(core == 0, g[...], both)


def near_sum_kernel(core_ref, base_ref, got_ref, r0, r1, r2, loss_ref, loss_got, low_ref, s0, s1, s2, loss_out):
    loss_out[...] = loss_ref[...] + loss_got[...]
    for q, (r, s) in enumerate(((r0, s0), (r1, s1), (r2, s2))):
        rows = slice(q * 512, q * 512 + 512)
        total = base_ref[rows, :] + got_ref[rows, :].astype(f32) + r[...].astype(f32)
        low_ref[q * 256 : q * 256 + 256, :] = total[0:256]
        s[...] = total[256:512].astype(bf16)


def half_sum_kernel(core_ref, low_ref, r0, r1, r2, loss_ref, loss_got, out_ref, s0, s1, s2, loss_out):
    loss_out[...] = loss_ref[...] + loss_got[...]
    for q, (r, s) in enumerate(((r0, s0), (r1, s1), (r2, s2))):
        total = low_ref[q * 256 : q * 256 + 256, :] + r[...].astype(f32)
        out_ref[q * 128 : q * 128 + 128, :] = total[0:128]
        s[...] = total[128:256].astype(bf16)


def last_sum_kernel(core_ref, low_ref, r0, r1, r2, own_ref, loss_ref, loss_got, keep_ref, send_ref, loss_out):
    first = core_ref[0] == 0
    loss = loss_ref[...] + loss_got[...]
    loss_out[...] = loss
    for q, r in enumerate((r0, r1, r2)):
        rows = slice(q * 64, q * 64 + 64)
        total = low_ref[q * 128 : q * 128 + 128, :] + r[...].astype(f32)
        keep_ref[rows, :] = jnp.where(first, total[0:64], total[64:128])
        send_ref[rows, :] = jnp.where(first, total[64:128], total[0:64])
        send_ref[192 + q * 64 : 192 + q * 64 + 64, :] = own_ref[q * 128 : q * 128 + 64, :]
    send_ref[384:392, :] = jnp.concatenate([loss] * 4, 1)


def finish_kernel(count, core_ref, keep_ref, got_ref, own_ref, loss_ref, image_out, text_out, loss_out):
    first = core_ref[0] == 0
    for q in range(3):
        rows = slice(q * 64, q * 64 + 64)
        keep = keep_ref[rows, :]
        got = got_ref[rows, :]
        own_mine = own_ref[q * 128 + 64 : q * 128 + 128, :]
        own_got = got_ref[192 + q * 64 : 192 + q * 64 + 64, :]
        image_out[rows, :] = jnp.where(first, keep + own_got, got + own_mine)
        text_out[rows, :] = jnp.where(first, got, keep)
    loss_out[...] = (loss_ref[0:1, 0:1] + got_ref[384:385, 0:1]) * (0.5 / count)


def per_device(image_emb, text_emb):
    core = lax.axis_index("c")
    core_id = core.reshape(1).astype(jnp.int32)
    pair_rows, width = image_emb.shape
    count = pair_rows * 128

    swapped = core_swap(jnp.where(core == 0, text_emb, image_emb))
    near = []
    for q in range(3):
        rows = slice(q * 64, q * 64 + 64)
        first = jnp.where(core == 0, image_emb[rows], swapped[rows])
        second = jnp.where(core == 0, swapped[rows], text_emb[rows])
        near.append(jnp.concatenate([first, second], 0))
    for step in range(2):
        got = [flip_permute(near[q], q + step) for q in range(3)]
        near = [jnp.concatenate([a, b], 0) for a, b in zip(near, got)]
    far = [flip_permute(near[q], q + 2) for q in range(3)]
    near_x = [core_swap(a) for a in near]
    far_x = [core_swap(a) for a in far]

    rows, cols, l0, l1, l2, send, keep = call(
        forward_kernel,
        "forward",
        [core_id, image_emb, text_emb, *near_x, *far_x, *near, *far],
        [pltpu.VMEM((1536, width), bf16), pltpu.VMEM((3072, width), bf16)]
        + [pltpu.VMEM((512, 3072), f32)] * 3
        + [shape(32, 128), shape(32, 128)],
        flops=2 * 1536 * 3072 * 512,
        limit=12,
    )

    mine = call(functools.partial(join_kernel, list(range(24))), "join", [core_id, keep, core_swap(send)], [shape(32, 128)], limit=2)[0]
    for dim in range(3):
        got = flip_permute(mine, dim)
        mine = call(functools.partial(join_kernel, flip_order(dim)), "join", [core_id, mine, got], [shape(32, 128)], limit=2)[0]
    other = core_swap(mine)

    coeffs, g0, g1, g2, own, loss = call(
        coeff_kernel,
        "coeffs",
        [core_id, mine, other, held(cols), held(l0), held(l1), held(l2)],
        [pltpu.VMEM((1536, 3072), bf16)] + [shape(512, width, dtype=bf16)] * 3 + [shape(384, width), shape(8, 128)],
        flops=2 * 1536 * 3072 * 512,
        limit=8,
    )
    text_far = call(
        far_text_kernel, "text_far", [core_id, held(coeffs), held(rows)], [shape(1536, width, dtype=bf16)], flops=1536 * 3072 * 512
    )[0]
    text_far_got = core_swap(text_far)
    base, near_send = call(
        near_text_kernel,
        "text_near",
        [core_id, held(coeffs), held(rows), g0, g1, g2],
        [shape(1536, width), shape(1536, width, dtype=bf16)],
        flops=1536 * 3072 * 512,
    )
    near_got = core_swap(near_send)
    messages = call(
        far_message_kernel, "far_message", [core_id, g0, g1, g2, text_far, text_far_got], [shape(512, width, dtype=bf16)] * 3
    )
    got = [flip_permute(messages[q], q + 2) for q in range(3)]
    loss_got = flip_permute(loss, 0)
    low, *messages, loss = call(
        near_sum_kernel,
        "near_sum",
        [core_id, base, near_got, *got, loss, loss_got],
        [shape(768, width)] + [shape(256, width, dtype=bf16)] * 3 + [shape(8, 128)],
    )
    got = [flip_permute(messages[q], q + 1) for q in range(3)]
    loss_got = flip_permute(loss, 1)
    low, *messages, loss = call(
        half_sum_kernel,
        "half_sum",
        [core_id, low, *got, loss, loss_got],
        [shape(384, width)] + [shape(128, width, dtype=bf16)] * 3 + [shape(8, 128)],
    )
    got = [flip_permute(messages[q], q) for q in range(3)]
    loss_got = flip_permute(loss, 2)
    keep, send, loss = call(
        last_sum_kernel,
        "last_sum",
        [core_id, low, *got, own, loss, loss_got],
        [shape(192, width), shape(392, width), shape(8, 128)],
    )
    swapped = core_swap(send)
    grad_image, grad_text, loss = call(
        functools.partial(finish_kernel, count),
        "finish",
        [core_id, keep, swapped, own, loss],
        [shape(192, width), shape(192, width), shape(1, 1)],
    )
    return loss.reshape(()), grad_image, grad_text


def solution(mesh):
    fine = Mesh(mesh.devices.reshape(4, 4, 4, 2), AXES)
    return jax.shard_map(
        per_device,
        mesh=fine,
        in_specs=(P(AXES, None), P(AXES, None)),
        out_specs=(P(), P(AXES, None), P(AXES, None)),
        check_vma=False,
    )
```

```python
import functools
import itertools
import math

import jax
import jax.numpy as jnp
from jax import lax
from jax.experimental import pallas as pl
from jax.experimental.pallas import tpu as pltpu
from jax.sharding import Mesh, PartitionSpec as P


logit_scale = 10.0
log2e = 1.4426950408889634
ln2 = 0.6931471805599453
lowest = -1e30
f32 = jnp.float32
bf16 = jnp.bfloat16
AXES = ("z", "y", "x", "c")
SWAP = ((0, 1), (1, 0))
FLIPS = ((0, 0, 1), (0, 1, 0), (1, 0, 0))
IMAGE_PAIR = (1, 0, 3, 2)
TEXT_PAIR = (3, 2, 1, 0)
VMEM = pl.BlockSpec(memory_space=pltpu.VMEM)
SMEM = pl.BlockSpec(memory_space=pltpu.SMEM)


def role_pairs(flip):
    pairs = []
    for z, y, x in itertools.product(range(4), repeat=3):
        for core, pair in ((0, IMAGE_PAIR), (1, TEXT_PAIR)):
            target = [pair[v] if f else v for v, f in zip((z, y, x), flip)]
            source_id = ((z * 4 + y) * 4 + x) * 2 + core
            target_id = ((target[0] * 4 + target[1]) * 4 + target[2]) * 2 + core
            pairs.append((source_id, target_id))
    return pairs


ROLE_PAIRS = [role_pairs(flip) for flip in FLIPS]


def flip_permute(x, dim):
    return lax.ppermute(x, AXES, ROLE_PAIRS[dim % 3])


def core_swap(x):
    return lax.ppermute(x, "c", SWAP)


def call(kernel, name, ins, outs, scratch=(), limit=6, flops=0, moved=0):
    in_specs = [SMEM if i == 0 else VMEM for i in range(len(ins))]
    return pl.pallas_call(
        kernel,
        in_specs=in_specs,
        out_specs=[VMEM] * len(outs),
        out_shape=list(outs),
        scratch_shapes=list(scratch),
        compiler_params=pltpu.CompilerParams(vmem_limit_bytes=limit << 20),
        cost_estimate=pl.CostEstimate(flops=flops, bytes_accessed=moved, transcendentals=0),
        name=name,
    )(*ins)


def held(x):
    return pltpu.with_memory_space_constraint(x, pltpu.VMEM)


def shape(*dims, dtype=f32):
    return jax.ShapeDtypeStruct(dims, dtype)


def forward_kernel(core_ref, image_ref, text_ref, *refs):
    near_x, far_x, near, far = refs[0:3], refs[3:6], refs[6:9], refs[9:12]
    rows_ref, cols_ref = refs[12:14]
    logit_refs = refs[14:17]
    send_ref, keep_ref = refs[17:19]
    core = core_ref[0]
    n = 512

    @pl.when(core == 0)
    def _():
        for q in range(3):
            rows_ref[q * n : q * n + n, :] = far[q][...]
            cols_ref[q * n : q * n + n, :] = near_x[q][...]
            cols_ref[(q + 3) * n : (q + 3) * n + n, :] = far_x[q][...]

    @pl.when(core != 0)
    def _():
        for q in range(3):
            rows_ref[q * n : q * n + n, :] = near_x[q][...]
            cols_ref[q * n : q * n + n, :] = near[q][...]
            cols_ref[(q + 3) * n : (q + 3) * n + n, :] = far[q][...]

    width = cols_ref.shape[0]
    top = jnp.full((1, width), -jnp.inf, f32)
    total = jnp.zeros((1, width), f32)
    row_blocks = []
    for q in range(3):
        logits = lax.dot_general(
            rows_ref[q * n : q * n + n, :], cols_ref[...], (((1,), (1,)), ((), ())), preferred_element_type=f32
        ) * (logit_scale * log2e)
        logit_refs[q][...] = logits
        row_top = jnp.max(logits, axis=1, keepdims=True)
        row_total = jnp.sum(jnp.exp2(logits - row_top), axis=1, keepdims=True)
        row = jnp.broadcast_to(row_top + jnp.log2(row_total), (n, 128)).T[0:1, :]
        row_blocks += [row[:, k * 128 : k * 128 + 128] for k in range(4)]
        new_top = jnp.maximum(top, jnp.max(logits, axis=0, keepdims=True))
        total = total * jnp.exp2(top - new_top) + jnp.sum(jnp.exp2(logits - new_top), axis=0, keepdims=True)
        top = new_top
    col = top + jnp.log2(total)
    positive = logit_scale * jnp.sum(image_ref[...].astype(f32) * text_ref[...].astype(f32))
    extra = jnp.full((8, 128), positive, f32)
    row_part = jnp.concatenate(row_blocks, 0)
    col_part = jnp.concatenate([col[:, k * 128 : k * 128 + 128] for k in range(24)], 0)
    blank = jnp.full((12, 128), lowest, f32)
    is_first = core == 0
    send_ref[0:24, :] = jnp.where(is_first, col_part, jnp.concatenate([row_part, blank], 0))
    keep_ref[0:24, :] = jnp.where(is_first, jnp.concatenate([blank, row_part], 0), col_part)
    send_ref[24:32, :] = extra
    keep_ref[24:32, :] = extra


def join_kernel(order, core_ref, mine_ref, got_ref, out_ref):
    a = mine_ref[0:24, :]
    got = got_ref[...]
    b = jnp.concatenate([got[k : k + 1, :] for k in order], 0)
    top = jnp.maximum(a, b)
    out_ref[0:24, :] = top + jnp.log2(jnp.exp2(a - top) + jnp.exp2(b - top))
    out_ref[24:32, :] = mine_ref[24:32, :] + got_ref[24:32, :]


def flip_order(dim):
    order = []
    for half, q, k in itertools.product(range(2), range(3), range(4)):
        j = (dim - q) % 3
        if j == 2:
            order.append((1 - half) * 12 + q * 4 + k)
        else:
            order.append(half * 12 + q * 4 + (k ^ (1 << j)))
    return order


def coeff_kernel(core_ref, mine_ref, got_ref, cols_ref, *refs):
    logit_refs = refs[0:3]
    coeff_ref = refs[3]
    grad_refs = refs[4:7]
    own_ref, loss_ref = refs[7:9]
    core = core_ref[0]
    is_first = core == 0
    n = 512
    mine = mine_ref[...]
    got = got_ref[...]
    row_lse = jnp.where(is_first, mine[12:24], got[0:12]) + 1.0
    col_lse = jnp.where(is_first, got[0:24], mine[0:24]) + 1.0
    row_lse = jnp.concatenate([row_lse[k : k + 1] for k in range(12)], 1)
    col_lse = jnp.concatenate([col_lse[k : k + 1] for k in range(24)], 1)
    lse_sum = jnp.sum(got[0:24]) * ln2
    loss_ref[...] = jnp.full((8, 128), lse_sum, f32) - jnp.where(is_first, 0.0, 2.0) * got[24:32]
    eye = lax.broadcasted_iota(jnp.int32, (128, 128), 0) == lax.broadcasted_iota(jnp.int32, (128, 128), 1)
    positive = jnp.where(jnp.logical_and(eye, core != 0), 1.0, 0.0)
    for q in range(3):
        row = jnp.broadcast_to(row_lse[:, q * n : q * n + n], (128, n)).T[:, 0:1]
        logits = logit_refs[q][...]
        coeffs = jnp.exp2(logits - row) + jnp.exp2(logits - col_lse)
        coeff_ref[q * n : q * n + n, :] = coeffs.astype(bf16)
        own = slice(q * n, q * n + 128)
        coeff_ref[own, own] = (coeffs[0:128, own] - positive).astype(bf16)
        grad = logit_scale * jnp.dot(coeff_ref[q * n : q * n + n, :], cols_ref[...], preferred_element_type=f32)
        own_ref[q * 128 : q * 128 + 128, :] = grad[0:128, :]
        grad_refs[q][0:128, :] = jnp.where(is_first, grad[0:128, :], 0.0).astype(bf16)
        grad_refs[q][128:n, :] = grad[128:n, :].astype(bf16)


def text_grad(coeff_ref, rows_ref, start):
    return logit_scale * lax.dot_general(
        coeff_ref[:, start : start + 512], rows_ref[...], (((0,), (0,)), ((), ())), preferred_element_type=f32
    )


def far_text_kernel(q, core_ref, coeff_ref, rows_ref, out_ref):
    out_ref[...] = text_grad(coeff_ref, rows_ref, 1536 + q * 512).astype(bf16)


def near_text_kernel(core_ref, coeff_ref, rows_ref, g0, g1, g2, own_ref, after0, after1, after2, base_ref, s0, s1, s2, early_ref, kept_ref):
    first = core_ref[0] == 0
    for q, (g, s) in enumerate(((g0, s0), (g1, s1), (g2, s2))):
        grad = text_grad(coeff_ref, rows_ref, q * 512)
        own = slice(q * 64, q * 64 + 64)
        early_ref[own, :] = own_ref[q * 128 : q * 128 + 64, :]
        early_ref[192 + q * 64 : 192 + q * 64 + 64, :] = grad[0:64, :]
        kept_ref[own, :] = grad[64:128, :]
        base_ref[q * 512 : q * 512 + 128, :] = jnp.zeros((128, grad.shape[1]), f32)
        base_ref[q * 512 + 128 : q * 512 + 512, :] = jnp.where(first, 0.0, grad[128:512, :])
        s[...] = jnp.where(first, grad.astype(bf16), g[...])


def split_terms(x):
    high = x.astype(bf16)
    rest = x - high.astype(f32)
    middle = rest.astype(bf16)
    low = (rest - middle.astype(f32)).astype(bf16)
    pair = [jnp.concatenate([t, t], 0) for t in (high, middle, low)]
    return jnp.concatenate(pair + [jnp.zeros((16, 128), bf16)], 1)


def join_terms(ref, start):
    x = ref[start : start + 16, :].astype(f32)
    return (x[0:8, 0:128] + x[0:8, 128:256]) + x[0:8, 256:384]


def far_message_kernel(core_ref, g, text_ref, got_ref, *refs):
    both = (text_ref[...].astype(f32) + got_ref[...].astype(f32)).astype(bf16)
    refs[-1][0:512, :] = jnp.where(core_ref[0] == 0, g[...], both)
    if len(refs) == 2:
        refs[-1][512:528, :] = split_terms(refs[0][...])


def far_sum_kernel(core_ref, base_ref, r0, r1, r2, loss_ref, total_ref, loss_out):
    loss_out[...] = loss_ref[...] + join_terms(r0, 512)
    for q, r in enumerate((r0, r1, r2)):
        rows = slice(q * 512, q * 512 + 512)
        total_ref[rows, :] = base_ref[rows, :] + r[0:512, :].astype(f32)


def near_sum_kernel(core_ref, total_ref, g0, g1, g2, loss_ref, low_ref, s0, s1, s2):
    s0[256:272, :] = split_terms(loss_ref[...])
    for q, (g, s) in enumerate(((g0, s0), (g1, s1), (g2, s2))):
        rows = slice(q * 512, q * 512 + 512)
        total = total_ref[rows, :] + g[...].astype(f32)
        low_ref[q * 256 : q * 256 + 256, :] = total[0:256]
        s[0:256, :] = total[256:512].astype(bf16)


def half_sum_kernel(core_ref, low_ref, r0, r1, r2, loss_ref, out_ref, s0, s1, s2, loss_out):
    loss = loss_ref[...] + join_terms(r0, 256)
    loss_out[...] = loss
    s0[128:144, :] = split_terms(loss)
    for q, (r, s) in enumerate(((r0, s0), (r1, s1), (r2, s2))):
        total = low_ref[q * 256 : q * 256 + 256, :] + r[0:256, :].astype(f32)
        out_ref[q * 128 : q * 128 + 128, :] = total[0:128]
        s[0:128, :] = total[128:256].astype(bf16)


def last_sum_kernel(core_ref, low_ref, r0, r1, r2, loss_ref, keep_ref, send_ref):
    first = core_ref[0] == 0
    loss = loss_ref[...] + join_terms(r0, 128)
    send_ref[192:200, :] = jnp.concatenate([loss] * 4, 1)
    keep_ref[192:200, :] = jnp.concatenate([loss] * 4, 1)
    for q, r in enumerate((r0, r1, r2)):
        rows = slice(q * 64, q * 64 + 64)
        total = low_ref[q * 128 : q * 128 + 128, :] + r[0:128, :].astype(f32)
        keep_ref[rows, :] = jnp.where(first, total[0:64], total[64:128])
        send_ref[rows, :] = jnp.where(first, total[64:128], total[0:64])


def finish_kernel(count, core_ref, keep_ref, got_ref, own_ref, early_ref, kept_ref, image_out, text_out, loss_out):
    first = core_ref[0] == 0
    for q in range(3):
        rows = slice(q * 64, q * 64 + 64)
        keep = keep_ref[rows, :]
        got = got_ref[rows, :]
        own_image = jnp.where(first, early_ref[rows, :], own_ref[q * 128 + 64 : q * 128 + 128, :])
        own_text = jnp.where(first, early_ref[192 + q * 64 : 192 + q * 64 + 64, :], kept_ref[rows, :])
        image_out[rows, :] = jnp.where(first, keep, got) + own_image
        text_out[rows, :] = jnp.where(first, got, keep) + own_text
    loss_out[...] = (keep_ref[192:193, 0:1] + got_ref[192:193, 0:1]) * (0.5 / count)


def select_kernel(core_ref, image_ref, text_ref, out_ref):
    out_ref[...] = jnp.where(core_ref[0] == 0, text_ref[...], image_ref[...])


def pair_kernel(core_ref, image_ref, text_ref, got_ref, *out_refs):
    first = core_ref[0] == 0
    for q, out in enumerate(out_refs):
        rows = slice(q * 64, q * 64 + 64)
        out[0:64, :] = jnp.where(first, image_ref[rows, :], got_ref[rows, :])
        out[64:128, :] = jnp.where(first, got_ref[rows, :], text_ref[rows, :])


def per_device(image_emb, text_emb):
    core_id = lax.axis_index("c").reshape(1).astype(jnp.int32)
    pair_rows, width = image_emb.shape
    count = pair_rows * 128

    swapped = core_swap(call(select_kernel, "select", [core_id, image_emb, text_emb], [shape(pair_rows, width, dtype=bf16)], limit=4)[0])
    near = call(
        pair_kernel, "pair", [core_id, image_emb, text_emb, swapped], [shape(128, width, dtype=bf16)] * 3, limit=4
    )
    for step in range(2):
        got = [flip_permute(near[q], q + step) for q in range(3)]
        near = [jnp.concatenate([a, b], 0) for a, b in zip(near, got)]
    far = [flip_permute(near[q], q + 2) for q in range(3)]
    near_x = [core_swap(a) for a in near]
    far_x = [core_swap(a) for a in far]

    rows, cols, l0, l1, l2, send, keep = call(
        forward_kernel,
        "forward",
        [core_id, image_emb, text_emb, *near_x, *far_x, *near, *far],
        [pltpu.VMEM((1536, width), bf16), pltpu.VMEM((3072, width), bf16)]
        + [pltpu.VMEM((512, 3072), f32)] * 3
        + [shape(32, 128), shape(32, 128)],
        flops=2 * 1536 * 3072 * 512,
        limit=12,
    )

    mine = call(functools.partial(join_kernel, list(range(24))), "join", [core_id, keep, core_swap(send)], [shape(32, 128)], limit=2)[0]
    for dim in range(3):
        got = flip_permute(mine, dim)
        mine = call(functools.partial(join_kernel, flip_order(dim)), "join", [core_id, mine, got], [shape(32, 128)], limit=2)[0]
    other = core_swap(mine)

    coeffs, g0, g1, g2, own, loss = call(
        coeff_kernel,
        "coeffs",
        [core_id, mine, other, held(cols), held(l0), held(l1), held(l2)],
        [pltpu.VMEM((1536, 3072), bf16)] + [shape(512, width, dtype=bf16)] * 3 + [shape(384, width), shape(8, 128)],
        flops=2 * 1536 * 3072 * 512,
        limit=8,
    )
    messages = []
    for q, g in enumerate((g0, g1, g2)):
        far_grad = call(
            functools.partial(far_text_kernel, q),
            "text_far",
            [core_id, held(coeffs), held(rows)],
            [shape(512, width, dtype=bf16)],
            flops=512 * 3072 * 512,
        )[0]
        ins = [core_id, g, far_grad, core_swap(far_grad)]
        if q == 0:
            ins.append(loss)
        messages.append(call(far_message_kernel, "far_message", ins, [shape(528 if q == 0 else 512, width, dtype=bf16)])[0])
    got = [flip_permute(messages[q], q + 2) for q in range(3)]
    base, *near_send, early, kept = call(
        near_text_kernel,
        "text_near",
        [core_id, held(coeffs), held(rows), g0, g1, g2, own, *messages],
        [shape(1536, width)] + [shape(512, width, dtype=bf16)] * 3 + [shape(384, width), shape(192, width)],
        flops=1536 * 3072 * 512,
    )
    near_got = [core_swap(a) for a in near_send]
    early = core_swap(early)
    total, loss = call(far_sum_kernel, "far_sum", [core_id, base, *got, loss], [shape(1536, width), shape(8, 128)])
    low, *messages = call(
        near_sum_kernel,
        "near_sum",
        [core_id, total, *near_got, loss],
        [shape(768, width)] + [shape(272 if q == 0 else 256, width, dtype=bf16) for q in range(3)],
    )
    got = [flip_permute(messages[q], q + 1) for q in range(3)]
    low, *messages, loss = call(
        half_sum_kernel,
        "half_sum",
        [core_id, low, *got, loss],
        [shape(384, width)] + [shape(144 if q == 0 else 128, width, dtype=bf16) for q in range(3)] + [shape(8, 128)],
    )
    got = [flip_permute(messages[q], q) for q in range(3)]
    keep, send = call(
        last_sum_kernel, "last_sum", [core_id, low, *got, loss], [shape(200, width), shape(200, width)]
    )
    swapped = core_swap(send)
    grad_image, grad_text, loss = call(
        functools.partial(finish_kernel, count),
        "finish",
        [core_id, keep, swapped, own, early, kept],
        [shape(192, width), shape(192, width), shape(1, 1)],
    )
    return loss.reshape(()), grad_image, grad_text


def solution(mesh):
    fine = Mesh(mesh.devices.reshape(4, 4, 4, 2), AXES)
    return jax.shard_map(
        per_device,
        mesh=fine,
        in_specs=(P(AXES, None), P(AXES, None)),
        out_specs=(P(), P(AXES, None), P(AXES, None)),
        check_vma=False,
    )
```

```python
import functools
import itertools
import math

import jax
import jax.numpy as jnp
from jax import lax
from jax.experimental import pallas as pl
from jax.experimental.pallas import tpu as pltpu
from jax.sharding import Mesh, PartitionSpec as P


logit_scale = 10.0
log2e = 1.4426950408889634
ln2 = 0.6931471805599453
lowest = -1e30
f32 = jnp.float32
bf16 = jnp.bfloat16
AXES = ("z", "y", "x", "c")
SWAP = ((0, 1), (1, 0))
FLIPS = ((0, 0, 1), (0, 1, 0), (1, 0, 0))
IMAGE_PAIR = (1, 0, 3, 2)
TEXT_PAIR = (3, 2, 1, 0)
VMEM = pl.BlockSpec(memory_space=pltpu.VMEM)
SMEM = pl.BlockSpec(memory_space=pltpu.SMEM)


def role_pairs(flip):
    pairs = []
    for z, y, x in itertools.product(range(4), repeat=3):
        for core, pair in ((0, IMAGE_PAIR), (1, TEXT_PAIR)):
            target = [pair[v] if f else v for v, f in zip((z, y, x), flip)]
            source_id = ((z * 4 + y) * 4 + x) * 2 + core
            target_id = ((target[0] * 4 + target[1]) * 4 + target[2]) * 2 + core
            pairs.append((source_id, target_id))
    return pairs


ROLE_PAIRS = [role_pairs(flip) for flip in FLIPS]


def flip_permute(x, dim):
    return lax.ppermute(x, AXES, ROLE_PAIRS[dim % 3])


def core_swap(x):
    return lax.ppermute(x, "c", SWAP)


def call(kernel, name, ins, outs, scratch=(), limit=6, flops=0, moved=0):
    in_specs = [SMEM if i == 0 else VMEM for i in range(len(ins))]
    return pl.pallas_call(
        kernel,
        in_specs=in_specs,
        out_specs=[VMEM] * len(outs),
        out_shape=list(outs),
        scratch_shapes=list(scratch),
        compiler_params=pltpu.CompilerParams(vmem_limit_bytes=limit << 20),
        cost_estimate=pl.CostEstimate(flops=flops, bytes_accessed=moved, transcendentals=0),
        name=name,
    )(*ins)


def held(x):
    return pltpu.with_memory_space_constraint(x, pltpu.VMEM)


def shape(*dims, dtype=f32):
    return jax.ShapeDtypeStruct(dims, dtype)


ROW_AT = (0, 768, 1024, 1280, 1536)
COL_AT = (0, 1536, 2048, 2560, 3072)
CONTRACT_LAST = (((1,), (1,)), ((), ()))
CONTRACT_FIRST = (((0,), (0,)), ((), ()))


def log_add(a, b):
    top = jnp.maximum(a, b)
    return top + jnp.log2(jnp.exp2(a - top) + jnp.exp2(b - top))


def lane_blocks(x):
    return [x[:, k : k + 128] for k in range(0, x.shape[1], 128)]


def row_stat(logits):
    top = jnp.max(logits, axis=1, keepdims=True)
    total = jnp.sum(jnp.exp2(logits - top), axis=1, keepdims=True)
    lse = top + jnp.log2(total)
    return jnp.concatenate(lane_blocks(jnp.broadcast_to(lse, (lse.shape[0], 128)).T[0:1, :]), 0)


def column_step(logits, state):
    top = jnp.max(logits, axis=0, keepdims=True)
    if state is None:
        return top, jnp.sum(jnp.exp2(logits - top), axis=0, keepdims=True)
    new_top = jnp.maximum(state[0], top)
    total = state[1] * jnp.exp2(state[0] - new_top) + jnp.sum(jnp.exp2(logits - new_top), axis=0, keepdims=True)
    return new_top, total


def column_stat(state):
    return jnp.concatenate(lane_blocks(state[0] + jnp.log2(state[1])), 0)


def forward_kernel(stage, core_ref, *refs):
    refs = list(refs)
    take = lambda n: [refs.pop(0) for _ in range(n)]
    n = 3 if stage == 0 else 1
    mine, swapped = take(n), take(n)
    rows, cols = take(stage), take(stage)
    row_old, col_old = take(2) if stage else (None, None)
    image_ref, text_ref = take(2) if stage == 3 else (None, None)
    rows_ref, cols_ref, wide_ref = take(3)
    tall_ref = take(1)[0] if stage else None
    first = core_ref[0] == 0

    @pl.when(first)
    def _():
        for i in range(n):
            rows_ref[i * 256 : i * 256 + 256, :] = mine[i][0:256, :]
            cols_ref[i * 512 : i * 512 + 512, :] = swapped[i][...]

    @pl.when(jnp.logical_not(first))
    def _():
        for i in range(n):
            rows_ref[i * 256 : i * 256 + 256, :] = swapped[i][256:512, :]
            cols_ref[i * 512 : i * 512 + 512, :] = mine[i][...]

    def product(a, b):
        return lax.dot_general(a, b, CONTRACT_LAST, preferred_element_type=f32) * (logit_scale * log2e)

    cols = cols + [cols_ref]
    new_rows = []
    state = None
    for block in range(n):
        part = slice(block * 256, block * 256 + 256)
        for p in range(stage + 1):
            wide_ref[part, COL_AT[p] : COL_AT[p + 1]] = product(rows_ref[part, :], cols[p][...])
        logits = wide_ref[part, :]
        new_rows.append(row_stat(logits))
        state = column_step(logits, state)
    col = column_stat(state)
    row = jnp.concatenate(new_rows, 0)
    if stage:
        state = None
        old = []
        for p in range(stage):
            for start in range(0, rows[p].shape[0], 256):
                part = slice(ROW_AT[p] + start, ROW_AT[p] + start + 256)
                tall_ref[part, :] = product(rows[p][start : start + 256, :], cols_ref[...])
                logits = tall_ref[part, :]
                old.append(row_stat(logits))
                state = column_step(logits, state)
        row = jnp.concatenate([log_add(row_old[...], jnp.concatenate(old, 0)), row], 0)
        col = log_add(col, jnp.concatenate([col_old[...], column_stat(state)], 0))
    if stage < 3:
        row_out, col_out = take(2)
        row_out[...] = row
        col_out[...] = col
        return
    send_ref, keep_ref = take(2)
    positive = logit_scale * jnp.sum(image_ref[...].astype(f32) * text_ref[...].astype(f32))
    extra = jnp.full((8, 128), positive, f32)
    blank = jnp.full((2, 128), lowest, f32)
    low_half = jnp.concatenate([x for g in range(6) for x in (row[2 * g : 2 * g + 2], blank)], 0)
    high_half = jnp.concatenate([x for g in range(6) for x in (blank, row[2 * g : 2 * g + 2])], 0)
    send_ref[0:24, :] = jnp.where(first, col, high_half)
    keep_ref[0:24, :] = jnp.where(first, low_half, col)
    send_ref[24:32, :] = extra
    keep_ref[24:32, :] = extra


def join_kernel(order, core_ref, mine_ref, got_ref, out_ref):
    got = got_ref[...]
    out_ref[0:24, :] = log_add(mine_ref[0:24, :], jnp.concatenate([got[k : k + 1, :] for k in order], 0))
    out_ref[24:32, :] = mine_ref[24:32, :] + got_ref[24:32, :]


def flip_order(dim):
    order = []
    for half, q, k in itertools.product(range(2), range(3), range(4)):
        j = (dim - q) % 3
        if j == 2:
            order.append((1 - half) * 12 + q * 4 + k)
        else:
            order.append(half * 12 + q * 4 + (k ^ (1 << j)))
    return order


def tile_lse(first, mine_ref, other_ref):
    mine, other = mine_ref[0:24, :], other_ref[0:24, :]
    row = jnp.where(first, mine, other)
    col = jnp.where(first, other, mine)
    row = [jnp.where(first, row[4 * g + b : 4 * g + b + 1], row[4 * g + b + 2 : 4 * g + b + 3]) for g in range(6) for b in range(2)]
    row = jnp.concatenate(row, 1) + 1.0
    col = jnp.concatenate([col[k : k + 1] for k in range(24)], 1) + 1.0
    return row, col


def coefficients(logits, row, col):
    n = logits.shape[0]
    row = jnp.broadcast_to(row, (128, n)).T[:, 0:1]
    return jnp.exp2(logits - row) + jnp.exp2(logits - col)


def total_of(terms):
    total = terms[0]
    for term in terms[1:]:
        total = total + term
    return logit_scale * total


def times(a, b):
    return jnp.dot(a, b, preferred_element_type=f32)


def transposed_times(a, b):
    return lax.dot_general(a, b, CONTRACT_FIRST, preferred_element_type=f32)


def far_grad_kernel(stage, core_ref, mine_ref, other_ref, *refs):
    refs = list(refs)
    take = lambda n: [refs.pop(0) for _ in range(n)]
    wide_in, tall_in = take(2)
    rows, cols = take(4), take(4)
    wide = [None] * (stage + 1) + take(3 - stage)
    tall = [None] * (stage + 1) + take(3 - stage)
    wide[stage], tall[stage] = take(2)
    kept_ref, send_ref = take(2)
    first = core_ref[0] == 0
    row, col = tile_lse(first, mine_ref, other_ref)
    if stage == 3:
        loss_ref = take(1)[0]
        loss_ref[...] = jnp.sum(other_ref[0:24, :]) * ln2 - jnp.where(first, 0.0, 2.0) * other_ref[24:32, :]
    wide[stage][...] = coefficients(
        wide_in[...], row[:, ROW_AT[stage] : ROW_AT[stage + 1]], col[:, 0 : COL_AT[stage + 1]]
    ).astype(bf16)
    for start in range(0, ROW_AT[stage], 256):
        part = slice(start, start + 256)
        tall[stage][part, :] = coefficients(
            tall_in[part, :], row[:, part], col[:, COL_AT[stage] : COL_AT[stage + 1]]
        ).astype(bf16)
    here = slice(ROW_AT[stage], ROW_AT[stage + 1])
    image = [times(wide[stage][:, COL_AT[p] : COL_AT[p + 1]], cols[p][...]) for p in range(stage + 1)]
    image += [times(tall[p][here, :], cols[p][...]) for p in range(stage + 1, 4)]
    image = total_of(image).astype(bf16)
    here = slice(COL_AT[stage], COL_AT[stage + 1])
    text = [transposed_times(tall[stage][ROW_AT[p] : ROW_AT[p + 1], :], rows[p][...]) for p in range(stage)]
    text += [transposed_times(wide[p][:, here], rows[p][...]) for p in range(stage, 4)]
    text = total_of(text).astype(bf16)
    kept_ref[0:256, :] = jnp.where(first, image, text[0:256])
    send_ref[0:256, :] = jnp.where(first, text[0:256], image)
    kept_ref[256:512, :] = text[256:512]
    send_ref[256:512, :] = text[256:512]


def near_grad_kernel(core_ref, mine_ref, other_ref, *refs):
    refs = list(refs)
    take = lambda n: [refs.pop(0) for _ in range(n)]
    wide_in = take(1)[0]
    rows, cols = take(4), take(4)
    wide, tall = [None] + take(3), [None] + take(3)
    take(3)
    base_ref, *send_refs = take(4)
    early_ref, kept_ref, block_ref = take(3)
    first = core_ref[0] == 0
    row, col = tile_lse(first, mine_ref, other_ref)
    eye = lax.broadcasted_iota(jnp.int32, (128, 128), 0) == lax.broadcasted_iota(jnp.int32, (128, 128), 1)
    positive = jnp.where(jnp.logical_and(eye, first), 1.0, 0.0)
    for q in range(3):
        part = slice(q * 256, q * 256 + 256)
        coeffs = coefficients(wide_in[part, :], row[:, part], col[:, 0:1536])
        block_ref[part, :] = coeffs.astype(bf16)
        own = slice(q * 512, q * 512 + 128)
        block_ref[q * 256 : q * 256 + 128, own] = (coeffs[0:128, own] - positive).astype(bf16)
    for q in range(3):
        part = slice(q * 256, q * 256 + 256)
        image = total_of(
            [times(block_ref[part, :], cols[0][...])] + [times(tall[p][part, :], cols[p][...]) for p in range(1, 4)]
        )
        here = slice(q * 512, q * 512 + 512)
        text = total_of(
            [transposed_times(block_ref[:, here], rows[0][...])]
            + [transposed_times(wide[p][:, here], rows[p][...]) for p in range(1, 4)]
        )
        own, own_text = slice(q * 64, q * 64 + 64), slice(192 + q * 64, 192 + q * 64 + 64)
        kept_ref[own, :] = image[0:64]
        kept_ref[own_text, :] = text[0:64]
        early_ref[own, :] = image[64:128]
        early_ref[own_text, :] = text[64:128]
        at = q * 512
        base_ref[at : at + 128, :] = jnp.where(first, 0.0, text[0:128])
        base_ref[at + 128 : at + 256, :] = jnp.where(first, image[128:256], text[128:256])
        base_ref[at + 256 : at + 512, :] = jnp.where(first, 0.0, text[256:512])
        send = send_refs[q]
        send[0:128, :] = jnp.where(first, 0.0, image[0:128]).astype(bf16)
        send[128:256, :] = jnp.where(first, text[128:256], image[128:256]).astype(bf16)
        send[256:512, :] = text[256:512].astype(bf16)


def split_terms(x):
    high = x.astype(bf16)
    rest = x - high.astype(f32)
    middle = rest.astype(bf16)
    low = (rest - middle.astype(f32)).astype(bf16)
    pair = [jnp.concatenate([t, t], 0) for t in (high, middle, low)]
    return jnp.concatenate(pair + [jnp.zeros((16, 128), bf16)], 1)


def join_terms(ref, start):
    x = ref[start : start + 16, :].astype(f32)
    return (x[0:8, 0:128] + x[0:8, 128:256]) + x[0:8, 256:384]


def far_message_kernel(core_ref, mine_ref, got_ref, *refs):
    first = core_ref[0] == 0
    got = got_ref[...]
    both = (mine_ref[...].astype(f32) + got.astype(f32)).astype(bf16)
    refs[-1][0:256, :] = jnp.where(first, mine_ref[0:256, :], both[0:256])
    refs[-1][256:512, :] = jnp.where(first, got[0:256], both[256:512])
    if len(refs) == 2:
        refs[-1][512:528, :] = split_terms(refs[0][...])


def far_sum_kernel(core_ref, base_ref, r0, r1, r2, loss_ref, total_ref, loss_out):
    loss_out[...] = loss_ref[...] + join_terms(r0, 512)
    for q, r in enumerate((r0, r1, r2)):
        rows = slice(q * 512, q * 512 + 512)
        total_ref[rows, :] = base_ref[rows, :] + r[0:512, :].astype(f32)


def near_sum_kernel(core_ref, total_ref, g0, g1, g2, loss_ref, low_ref, s0, s1, s2):
    first = core_ref[0] == 0
    s0[256:272, :] = split_terms(loss_ref[...])
    for q, (g, s) in enumerate(((g0, s0), (g1, s1), (g2, s2))):
        at = q * 512
        got = g[...].astype(f32)
        low_ref[q * 256 : q * 256 + 256, :] = total_ref[at : at + 256, :] + jnp.where(first, 0.0, got[0:256])
        s[0:256, :] = (total_ref[at + 256 : at + 512, :] + jnp.where(first, got[0:256], got[256:512])).astype(bf16)


def half_sum_kernel(core_ref, low_ref, r0, r1, r2, loss_ref, out_ref, s0, s1, s2, loss_out):
    loss = loss_ref[...] + join_terms(r0, 256)
    loss_out[...] = loss
    s0[128:144, :] = split_terms(loss)
    for q, (r, s) in enumerate(((r0, s0), (r1, s1), (r2, s2))):
        total = low_ref[q * 256 : q * 256 + 256, :] + r[0:256, :].astype(f32)
        out_ref[q * 128 : q * 128 + 128, :] = total[0:128]
        s[0:128, :] = total[128:256].astype(bf16)


def last_sum_kernel(core_ref, low_ref, r0, r1, r2, loss_ref, keep_ref, send_ref):
    first = core_ref[0] == 0
    loss = loss_ref[...] + join_terms(r0, 128)
    send_ref[192:200, :] = jnp.concatenate([loss] * 4, 1)
    keep_ref[192:200, :] = jnp.concatenate([loss] * 4, 1)
    for q, r in enumerate((r0, r1, r2)):
        rows = slice(q * 64, q * 64 + 64)
        total = low_ref[q * 128 : q * 128 + 128, :] + r[0:128, :].astype(f32)
        keep_ref[rows, :] = jnp.where(first, total[0:64], total[64:128])
        send_ref[rows, :] = jnp.where(first, total[64:128], total[0:64])


def finish_kernel(count, core_ref, keep_ref, got_ref, kept_ref, early_ref, image_out, text_out, loss_out):
    first = core_ref[0] == 0
    for q in range(3):
        rows = slice(q * 64, q * 64 + 64)
        keep = keep_ref[rows, :]
        got = got_ref[rows, :]
        text_rows = slice(192 + q * 64, 192 + q * 64 + 64)
        own_image = jnp.where(first, kept_ref[rows, :], early_ref[rows, :])
        own_text = jnp.where(first, kept_ref[text_rows, :], early_ref[text_rows, :])
        image_out[rows, :] = jnp.where(first, keep, got) + own_image
        text_out[rows, :] = jnp.where(first, got, keep) + own_text
    loss_out[...] = (keep_ref[192:193, 0:1] + got_ref[192:193, 0:1]) * (0.5 / count)


def select_kernel(core_ref, image_ref, text_ref, out_ref):
    out_ref[...] = jnp.where(core_ref[0] == 0, text_ref[...], image_ref[...])


def pair_kernel(core_ref, image_ref, text_ref, got_ref, *out_refs):
    first = core_ref[0] == 0
    for q, out in enumerate(out_refs):
        rows = slice(q * 64, q * 64 + 64)
        out[0:64, :] = jnp.where(first, image_ref[rows, :], got_ref[rows, :])
        out[64:128, :] = jnp.where(first, got_ref[rows, :], text_ref[rows, :])


def per_device(image_emb, text_emb):
    core_id = lax.axis_index("c").reshape(1).astype(jnp.int32)
    pair_rows, width = image_emb.shape
    count = pair_rows * 128

    swapped = core_swap(call(select_kernel, "select", [core_id, image_emb, text_emb], [shape(pair_rows, width, dtype=bf16)], limit=4)[0])
    near = call(
        pair_kernel, "pair", [core_id, image_emb, text_emb, swapped], [shape(128, width, dtype=bf16)] * 3, limit=4
    )
    for step in range(2):
        got = [flip_permute(near[q], q + step) for q in range(3)]
        near = [jnp.concatenate([a, b], 0) for a, b in zip(near, got)]
    far = [flip_permute(near[q], q + 2) for q in range(3)]
    near_x = [core_swap(a) for a in near]
    far_x = [core_swap(a) for a in far]

    rows, cols, wide, tall = [], [], [], [None]
    stat = []
    for stage in range(4):
        ins = [core_id] + (near + near_x if stage == 0 else [far[stage - 1], far_x[stage - 1]])
        ins += [held(a) for a in rows + cols] + stat
        if stage == 3:
            ins += [image_emb, text_emb]
        new_rows = 768 if stage == 0 else 256
        new_cols = 1536 if stage == 0 else 512
        outs = [pltpu.VMEM((new_rows, width), bf16), pltpu.VMEM((new_cols, width), bf16)]
        outs.append(pltpu.VMEM((new_rows, COL_AT[stage + 1]), f32))
        if stage:
            outs.append(pltpu.VMEM((ROW_AT[stage], new_cols), f32))
        if stage < 3:
            outs += [shape(ROW_AT[stage + 1] // 128, 128), shape(COL_AT[stage + 1] // 128, 128)]
        else:
            outs += [shape(32, 128), shape(32, 128)]
        area = new_rows * COL_AT[stage + 1] + ROW_AT[stage] * new_cols
        got = call(functools.partial(forward_kernel, stage), "forward", ins, outs, limit=10, flops=2 * area * width)
        rows.append(got[0])
        cols.append(got[1])
        wide.append(got[2])
        if stage:
            tall.append(got[3])
        stat = list(got[-2:])
    send, keep = stat

    mine = call(functools.partial(join_kernel, list(range(24))), "join", [core_id, keep, core_swap(send)], [shape(32, 128)], limit=2)[0]
    for dim in range(3):
        got = flip_permute(mine, dim)
        mine = call(functools.partial(join_kernel, flip_order(dim)), "join", [core_id, mine, got], [shape(32, 128)], limit=2)[0]
    other = core_swap(mine)

    held_rows, held_cols = [held(a) for a in rows], [held(a) for a in cols]
    wide_coeffs, tall_coeffs = [], []
    messages = [None] * 3
    for stage in (3, 2, 1):
        ins = [core_id, mine, other, held(wide[stage]), held(tall[stage]), *held_rows, *held_cols]
        ins += [held(a) for a in wide_coeffs + tall_coeffs]
        outs = [pltpu.VMEM((256, COL_AT[stage + 1]), bf16), pltpu.VMEM((ROW_AT[stage], 512), bf16)]
        outs += [shape(512, width, dtype=bf16)] * 2
        if stage == 3:
            outs.append(shape(8, 128))
        got = call(
            functools.partial(far_grad_kernel, stage),
            "far_grad",
            ins,
            outs,
            limit=10,
            flops=2 * (256 * 3072 + 1536 * 512) * width,
        )
        wide_coeffs.insert(0, got[0])
        tall_coeffs.insert(0, got[1])
        if stage == 3:
            loss = got[4]
        ins = [core_id, got[2], core_swap(got[3])]
        if stage == 1:
            ins.append(loss)
        messages[stage - 1] = call(
            far_message_kernel, "far_message", ins, [shape(528 if stage == 1 else 512, width, dtype=bf16)]
        )[0]
    got = [flip_permute(messages[q], q + 2) for q in range(3)]
    base, *near_send, early, kept = call(
        near_grad_kernel,
        "near_grad",
        [core_id, mine, other, held(wide[0]), *held_rows, *held_cols]
        + [held(a) for a in wide_coeffs + tall_coeffs]
        + messages,
        [shape(1536, width)] + [shape(512, width, dtype=bf16)] * 3 + [shape(384, width), shape(384, width)],
        scratch=[pltpu.VMEM((768, 1536), bf16)],
        limit=10,
        flops=2 * (768 * 3072 + 1536 * 1536) * width,
    )
    near_got = [core_swap(a) for a in near_send]
    early = core_swap(early)
    total, loss = call(far_sum_kernel, "far_sum", [core_id, base, *got, loss], [shape(1536, width), shape(8, 128)])
    low, *messages = call(
        near_sum_kernel,
        "near_sum",
        [core_id, total, *near_got, loss],
        [shape(768, width)] + [shape(272 if q == 0 else 256, width, dtype=bf16) for q in range(3)],
    )
    got = [flip_permute(messages[q], q + 1) for q in range(3)]
    low, *messages, loss = call(
        half_sum_kernel,
        "half_sum",
        [core_id, low, *got, loss],
        [shape(384, width)] + [shape(144 if q == 0 else 128, width, dtype=bf16) for q in range(3)] + [shape(8, 128)],
    )
    got = [flip_permute(messages[q], q) for q in range(3)]
    keep, send = call(
        last_sum_kernel, "last_sum", [core_id, low, *got, loss], [shape(200, width), shape(200, width)]
    )
    swapped = core_swap(send)
    grad_image, grad_text, loss = call(
        functools.partial(finish_kernel, count),
        "finish",
        [core_id, keep, swapped, kept, early],
        [shape(192, width), shape(192, width), shape(1, 1)],
    )
    return loss.reshape(()), grad_image, grad_text


def solution(mesh):
    fine = Mesh(mesh.devices.reshape(4, 4, 4, 2), AXES)
    return jax.shard_map(
        per_device,
        mesh=fine,
        in_specs=(P(AXES, None), P(AXES, None)),
        out_specs=(P(), P(AXES, None), P(AXES, None)),
        check_vma=False,
    )
```

```python
import functools
import itertools
import math

import jax
import jax.numpy as jnp
from jax import lax
from jax.experimental import pallas as pl
from jax.experimental.pallas import tpu as pltpu
from jax.sharding import Mesh, PartitionSpec as P


logit_scale = 10.0
log2e = 1.4426950408889634
ln2 = 0.6931471805599453
lowest = -1e30
f32 = jnp.float32
bf16 = jnp.bfloat16
AXES = ("z", "y", "x", "c")
SWAP = ((0, 1), (1, 0))
FLIPS = ((0, 0, 1), (0, 1, 0), (1, 0, 0))
IMAGE_PAIR = (1, 0, 3, 2)
TEXT_PAIR = (3, 2, 1, 0)
VMEM = pl.BlockSpec(memory_space=pltpu.VMEM)
SMEM = pl.BlockSpec(memory_space=pltpu.SMEM)


def role_pairs(flip):
    pairs = []
    for z, y, x in itertools.product(range(4), repeat=3):
        for core, pair in ((0, IMAGE_PAIR), (1, TEXT_PAIR)):
            target = [pair[v] if f else v for v, f in zip((z, y, x), flip)]
            source_id = ((z * 4 + y) * 4 + x) * 2 + core
            target_id = ((target[0] * 4 + target[1]) * 4 + target[2]) * 2 + core
            pairs.append((source_id, target_id))
    return pairs


ROLE_PAIRS = [role_pairs(flip) for flip in FLIPS]


def flip_permute(x, dim):
    return lax.ppermute(x, AXES, ROLE_PAIRS[dim % 3])


def core_swap(x):
    return lax.ppermute(x, "c", SWAP)


def call(kernel, name, ins, outs, scratch=(), limit=6, flops=0, moved=0):
    in_specs = [SMEM if i == 0 else VMEM for i in range(len(ins))]
    return pl.pallas_call(
        kernel,
        in_specs=in_specs,
        out_specs=[VMEM] * len(outs),
        out_shape=list(outs),
        scratch_shapes=list(scratch),
        compiler_params=pltpu.CompilerParams(vmem_limit_bytes=limit << 20),
        cost_estimate=pl.CostEstimate(flops=flops, bytes_accessed=moved, transcendentals=0),
        name=name,
    )(*ins)


def held(x):
    return pltpu.with_memory_space_constraint(x, pltpu.VMEM)


def shape(*dims, dtype=f32):
    return jax.ShapeDtypeStruct(dims, dtype)


PACKED = 2
ROW_AT = (0, 768, 1024, 1280, 1536)
COL_AT = (0, 1536, 2048, 2560, 3072)
CONTRACT_LAST = (((1,), (1,)), ((), ()))
CONTRACT_FIRST = (((0,), (0,)), ((), ()))


def log_add(a, b):
    top = jnp.maximum(a, b)
    return top + jnp.log2(jnp.exp2(a - top) + jnp.exp2(b - top))


def lane_blocks(x):
    return [x[:, k : k + 128] for k in range(0, x.shape[1], 128)]


def row_stat(logits):
    top = jnp.max(logits, axis=1, keepdims=True)
    total = jnp.sum(jnp.exp2(logits - top), axis=1, keepdims=True)
    lse = top + jnp.log2(total)
    return jnp.concatenate(lane_blocks(jnp.broadcast_to(lse, (lse.shape[0], 128)).T[0:1, :]), 0)


def column_step(logits, state):
    top = jnp.max(logits, axis=0, keepdims=True)
    if state is None:
        return top, jnp.sum(jnp.exp2(logits - top), axis=0, keepdims=True)
    new_top = jnp.maximum(state[0], top)
    total = state[1] * jnp.exp2(state[0] - new_top) + jnp.sum(jnp.exp2(logits - new_top), axis=0, keepdims=True)
    return new_top, total


def column_stat(state):
    return jnp.concatenate(lane_blocks(state[0] + jnp.log2(state[1])), 0)


def forward_kernel(stage, core_ref, *refs):
    refs = list(refs)
    take = lambda n: [refs.pop(0) for _ in range(n)]
    n = 3 if stage == 0 else 1
    mine = take(n)
    if stage == 0:
        packed_ref = take(1)[0]
        swapped = [packed_ref.at[k * 512 : k * 512 + 512] for k in range(PACKED)] + take(3 - PACKED)
    else:
        swapped = take(1)
    rows, cols = take(stage), take(stage)
    row_old, col_old = take(2) if stage else (None, None)
    image_ref, text_ref = take(2) if stage == 3 else (None, None)
    rows_ref, cols_ref, wide_ref = take(3)
    tall_ref = take(1)[0] if stage else None
    first = core_ref[0] == 0

    @pl.when(first)
    def _():
        for i in range(n):
            rows_ref[i * 256 : i * 256 + 256, :] = mine[i][0:256, :]
            cols_ref[i * 512 : i * 512 + 512, :] = swapped[i][...]

    @pl.when(jnp.logical_not(first))
    def _():
        for i in range(n):
            rows_ref[i * 256 : i * 256 + 256, :] = swapped[i][256:512, :]
            cols_ref[i * 512 : i * 512 + 512, :] = mine[i][...]

    def product(a, b):
        return lax.dot_general(a, b, CONTRACT_LAST, preferred_element_type=f32) * (logit_scale * log2e)

    cols = cols + [cols_ref]
    new_rows = []
    state = None
    for block in range(n):
        part = slice(block * 256, block * 256 + 256)
        for p in range(stage + 1):
            wide_ref[part, COL_AT[p] : COL_AT[p + 1]] = product(rows_ref[part, :], cols[p][...])
        logits = wide_ref[part, :]
        new_rows.append(row_stat(logits))
        state = column_step(logits, state)
    col = column_stat(state)
    row = jnp.concatenate(new_rows, 0)
    if stage:
        state = None
        old = []
        for p in range(stage):
            for start in range(0, rows[p].shape[0], 256):
                part = slice(ROW_AT[p] + start, ROW_AT[p] + start + 256)
                tall_ref[part, :] = product(rows[p][start : start + 256, :], cols_ref[...])
                logits = tall_ref[part, :]
                old.append(row_stat(logits))
                state = column_step(logits, state)
        row = jnp.concatenate([log_add(row_old[...], jnp.concatenate(old, 0)), row], 0)
        col = log_add(col, jnp.concatenate([col_old[...], column_stat(state)], 0))
    if stage < 3:
        row_out, col_out = take(2)
        row_out[...] = row
        col_out[...] = col
        return
    send_ref, keep_ref = take(2)
    positive = logit_scale * jnp.sum(image_ref[...].astype(f32) * text_ref[...].astype(f32))
    extra = jnp.full((8, 128), positive, f32)
    blank = jnp.full((2, 128), lowest, f32)
    low_half = jnp.concatenate([x for g in range(6) for x in (row[2 * g : 2 * g + 2], blank)], 0)
    high_half = jnp.concatenate([x for g in range(6) for x in (blank, row[2 * g : 2 * g + 2])], 0)
    send_ref[0:24, :] = jnp.where(first, col, high_half)
    keep_ref[0:24, :] = jnp.where(first, low_half, col)
    send_ref[24:32, :] = extra
    keep_ref[24:32, :] = extra


def pack_kernel(core_ref, *refs):
    for k, ref in enumerate(refs[:-1]):
        refs[-1][k * 512 : k * 512 + 512, :] = ref[...]


def gate_kernel(value_ref, token_ref, out_ref):
    pass


def after(value, token):
    anywhere = pl.BlockSpec(memory_space=pl.ANY)
    return pl.pallas_call(
        gate_kernel,
        in_specs=[anywhere, anywhere],
        out_specs=anywhere,
        out_shape=jax.ShapeDtypeStruct(value.shape, value.dtype),
        input_output_aliases={0: 0},
        name="after",
    )(value, token)


def join_kernel(order, core_ref, mine_ref, got_ref, out_ref):
    got = got_ref[...]
    out_ref[0:24, :] = log_add(mine_ref[0:24, :], jnp.concatenate([got[k : k + 1, :] for k in order], 0))
    out_ref[24:32, :] = mine_ref[24:32, :] + got_ref[24:32, :]


def flip_order(dim):
    order = []
    for half, q, k in itertools.product(range(2), range(3), range(4)):
        j = (dim - q) % 3
        if j == 2:
            order.append((1 - half) * 12 + q * 4 + k)
        else:
            order.append(half * 12 + q * 4 + (k ^ (1 << j)))
    return order


def tile_lse(first, mine_ref, other_ref):
    mine, other = mine_ref[0:24, :], other_ref[0:24, :]
    row = jnp.where(first, mine, other)
    col = jnp.where(first, other, mine)
    row = [jnp.where(first, row[4 * g + b : 4 * g + b + 1], row[4 * g + b + 2 : 4 * g + b + 3]) for g in range(6) for b in range(2)]
    row = jnp.concatenate(row, 1) + 1.0
    col = jnp.concatenate([col[k : k + 1] for k in range(24)], 1) + 1.0
    return row, col


def coefficients(logits, row, col):
    n = logits.shape[0]
    row = jnp.broadcast_to(row, (128, n)).T[:, 0:1]
    return jnp.exp2(logits - row) + jnp.exp2(logits - col)


def total_of(terms):
    total = terms[0]
    for term in terms[1:]:
        total = total + term
    return logit_scale * total


def times(a, b):
    return jnp.dot(a, b, preferred_element_type=f32)


def transposed_times(a, b):
    return lax.dot_general(a, b, CONTRACT_FIRST, preferred_element_type=f32)


def far_grad_kernel(stage, core_ref, mine_ref, other_ref, *refs):
    refs = list(refs)
    take = lambda n: [refs.pop(0) for _ in range(n)]
    wide_in, tall_in = take(2)
    rows, cols = take(4), take(4)
    wide = [None] * (stage + 1) + take(3 - stage)
    tall = [None] * (stage + 1) + take(3 - stage)
    wide[stage], tall[stage] = take(2)
    kept_ref, send_ref = take(2)
    first = core_ref[0] == 0
    row, col = tile_lse(first, mine_ref, other_ref)
    if stage == 3:
        loss_ref = take(1)[0]
        loss_ref[...] = jnp.sum(other_ref[0:24, :]) * ln2 - jnp.where(first, 0.0, 2.0) * other_ref[24:32, :]
    wide[stage][...] = coefficients(
        wide_in[...], row[:, ROW_AT[stage] : ROW_AT[stage + 1]], col[:, 0 : COL_AT[stage + 1]]
    ).astype(bf16)
    for start in range(0, ROW_AT[stage], 256):
        part = slice(start, start + 256)
        tall[stage][part, :] = coefficients(
            tall_in[part, :], row[:, part], col[:, COL_AT[stage] : COL_AT[stage + 1]]
        ).astype(bf16)
    here = slice(ROW_AT[stage], ROW_AT[stage + 1])
    image = [times(wide[stage][:, COL_AT[p] : COL_AT[p + 1]], cols[p][...]) for p in range(stage + 1)]
    image += [times(tall[p][here, :], cols[p][...]) for p in range(stage + 1, 4)]
    image = total_of(image).astype(bf16)
    here = slice(COL_AT[stage], COL_AT[stage + 1])
    text = [transposed_times(tall[stage][ROW_AT[p] : ROW_AT[p + 1], :], rows[p][...]) for p in range(stage)]
    text += [transposed_times(wide[p][:, here], rows[p][...]) for p in range(stage, 4)]
    text = total_of(text).astype(bf16)
    kept_ref[0:256, :] = jnp.where(first, image, text[0:256])
    send_ref[0:256, :] = jnp.where(first, text[0:256], image)
    kept_ref[256:512, :] = text[256:512]
    send_ref[256:512, :] = text[256:512]


def near_grad_kernel(q, core_ref, mine_ref, other_ref, *refs):
    refs = list(refs)
    take = lambda n: [refs.pop(0) for _ in range(n)]
    source_ref = take(1)[0]
    rows, cols = take(4), take(4)
    wide, tall = [None] + take(3), [None] + take(3)
    take(3)
    base_ref, send_ref, own_ref = take(3)
    first = core_ref[0] == 0
    block_ref = source_ref
    if q == 0:
        block_ref = take(1)[0]
        row, col = tile_lse(first, mine_ref, other_ref)
        eye = lax.broadcasted_iota(jnp.int32, (128, 128), 0) == lax.broadcasted_iota(jnp.int32, (128, 128), 1)
        positive = jnp.where(jnp.logical_and(eye, first), 1.0, 0.0)
        for k in range(3):
            part = slice(k * 256, k * 256 + 256)
            coeffs = coefficients(source_ref[part, :], row[:, part], col[:, 0:1536])
            block_ref[part, :] = coeffs.astype(bf16)
            own = slice(k * 512, k * 512 + 128)
            block_ref[k * 256 : k * 256 + 128, own] = (coeffs[0:128, own] - positive).astype(bf16)
    part = slice(q * 256, q * 256 + 256)
    image = total_of(
        [times(block_ref[part, :], cols[0][...])] + [times(tall[p][part, :], cols[p][...]) for p in range(1, 4)]
    )
    here = slice(q * 512, q * 512 + 512)
    text = total_of(
        [transposed_times(block_ref[:, here], rows[0][...])]
        + [transposed_times(wide[p][:, here], rows[p][...]) for p in range(1, 4)]
    )
    own_ref[0:128, :] = image[0:128]
    own_ref[128:256, :] = text[0:128]
    base_ref[0:128, :] = jnp.where(first, 0.0, text[0:128])
    base_ref[128:256, :] = jnp.where(first, image[128:256], text[128:256])
    base_ref[256:512, :] = jnp.where(first, 0.0, text[256:512])
    send_ref[0:128, :] = jnp.where(first, 0.0, image[0:128]).astype(bf16)
    send_ref[128:256, :] = jnp.where(first, text[128:256], image[128:256]).astype(bf16)
    send_ref[256:512, :] = text[256:512].astype(bf16)


def split_terms(x):
    high = x.astype(bf16)
    rest = x - high.astype(f32)
    middle = rest.astype(bf16)
    low = (rest - middle.astype(f32)).astype(bf16)
    pair = [jnp.concatenate([t, t], 0) for t in (high, middle, low)]
    return jnp.concatenate(pair + [jnp.zeros((16, 128), bf16)], 1)


def join_terms(ref, start):
    x = ref[start : start + 16, :].astype(f32)
    return (x[0:8, 0:128] + x[0:8, 128:256]) + x[0:8, 256:384]


def far_message_kernel(core_ref, mine_ref, got_ref, *refs):
    first = core_ref[0] == 0
    got = got_ref[...]
    both = (mine_ref[...].astype(f32) + got.astype(f32)).astype(bf16)
    refs[-1][0:256, :] = jnp.where(first, mine_ref[0:256, :], both[0:256])
    refs[-1][256:512, :] = jnp.where(first, got[0:256], both[256:512])
    if len(refs) == 2:
        refs[-1][512:528, :] = split_terms(refs[0][...])


def far_sum_kernel(core_ref, b0, b1, b2, r0, r1, r2, loss_ref, total_ref, loss_out):
    loss_out[...] = loss_ref[...] + join_terms(r0, 512)
    for q, (b, r) in enumerate(((b0, r0), (b1, r1), (b2, r2))):
        total_ref[q * 512 : q * 512 + 512, :] = b[...] + r[0:512, :].astype(f32)


def near_sum_kernel(core_ref, total_ref, g0, g1, g2, loss_ref, low_ref, s0, s1, s2):
    first = core_ref[0] == 0
    s0[256:272, :] = split_terms(loss_ref[...])
    for q, (g, s) in enumerate(((g0, s0), (g1, s1), (g2, s2))):
        at = q * 512
        got = g[...].astype(f32)
        low_ref[q * 256 : q * 256 + 256, :] = total_ref[at : at + 256, :] + jnp.where(first, 0.0, got[0:256])
        s[0:256, :] = (total_ref[at + 256 : at + 512, :] + jnp.where(first, got[0:256], got[256:512])).astype(bf16)


def half_sum_kernel(core_ref, low_ref, r0, r1, r2, loss_ref, out_ref, s0, s1, s2, loss_out):
    loss = loss_ref[...] + join_terms(r0, 256)
    loss_out[...] = loss
    s0[128:144, :] = split_terms(loss)
    for q, (r, s) in enumerate(((r0, s0), (r1, s1), (r2, s2))):
        total = low_ref[q * 256 : q * 256 + 256, :] + r[0:256, :].astype(f32)
        out_ref[q * 128 : q * 128 + 128, :] = total[0:128]
        s[0:128, :] = total[128:256].astype(bf16)


def last_sum_kernel(core_ref, low_ref, r0, r1, r2, o0, o1, o2, loss_ref, keep_ref, send_ref):
    first = core_ref[0] == 0
    loss = loss_ref[...] + join_terms(r0, 128)
    keep_ref[384:392, :] = jnp.concatenate([loss] * 4, 1)
    send_ref[384:392, :] = jnp.concatenate([loss] * 4, 1)
    for q, (r, own) in enumerate(((r0, o0), (r1, o1), (r2, o2))):
        rows, text_rows = slice(q * 64, q * 64 + 64), slice(192 + q * 64, 192 + q * 64 + 64)
        total = low_ref[q * 128 : q * 128 + 128, :] + r[0:128, :].astype(f32)
        keep_ref[rows, :] = jnp.where(first, total[0:64] + own[0:64, :], total[64:128])
        keep_ref[text_rows, :] = own[128:192, :]
        send_ref[rows, :] = jnp.where(first, total[64:128] + own[64:128, :], total[0:64])
        send_ref[text_rows, :] = own[192:256, :]


def finish_kernel(count, core_ref, keep_ref, got_ref, image_out, text_out, loss_out):
    first = core_ref[0] == 0
    image_out[...] = jnp.where(first, keep_ref[0:192, :], got_ref[0:192, :])
    text_out[...] = jnp.where(
        first, got_ref[0:192, :] + keep_ref[192:384, :], keep_ref[0:192, :] + got_ref[192:384, :]
    )
    loss_out[...] = (keep_ref[384:385, 0:1] + got_ref[384:385, 0:1]) * (0.5 / count)


def select_kernel(core_ref, image_ref, text_ref, out_ref):
    out_ref[...] = jnp.where(core_ref[0] == 0, text_ref[...], image_ref[...])


def pair_kernel(core_ref, image_ref, text_ref, got_ref, *out_refs):
    first = core_ref[0] == 0
    for q, out in enumerate(out_refs):
        rows = slice(q * 64, q * 64 + 64)
        out[0:64, :] = jnp.where(first, image_ref[rows, :], got_ref[rows, :])
        out[64:128, :] = jnp.where(first, got_ref[rows, :], text_ref[rows, :])


def per_device(image_emb, text_emb):
    core_id = lax.axis_index("c").reshape(1).astype(jnp.int32)
    pair_rows, width = image_emb.shape
    count = pair_rows * 128

    swapped = core_swap(call(select_kernel, "select", [core_id, image_emb, text_emb], [shape(pair_rows, width, dtype=bf16)], limit=4)[0])
    near = call(
        pair_kernel, "pair", [core_id, image_emb, text_emb, swapped], [shape(128, width, dtype=bf16)] * 3, limit=4
    )
    for step in range(2):
        got = [flip_permute(near[q], q + step) for q in range(3)]
        near = [jnp.concatenate([a, b], 0) for a, b in zip(near, got)]
    far = [flip_permute(near[q], q + 2) for q in range(3)]
    packed = call(pack_kernel, "pack", [core_id, *near[:PACKED]], [shape(512 * PACKED, width, dtype=bf16)], limit=4)[0]
    near_x = [core_swap(packed)] + [core_swap(a) for a in near[PACKED:]]
    far_x = [None] * 3

    rows, cols, wide, tall = [], [], [], [None]
    stat = []
    for stage in range(4):
        for q in {1: (0, 1, 2)}.get(stage, ()):
            far[q] = after(far[q], stat[0])
            far_x[q] = core_swap(far[q])
        ins = [core_id] + (near + near_x if stage == 0 else [far[stage - 1], far_x[stage - 1]])
        ins += [held(a) for a in rows + cols] + stat
        if stage == 3:
            ins += [image_emb, text_emb]
        new_rows = 768 if stage == 0 else 256
        new_cols = 1536 if stage == 0 else 512
        outs = [pltpu.VMEM((new_rows, width), bf16), pltpu.VMEM((new_cols, width), bf16)]
        outs.append(pltpu.VMEM((new_rows, COL_AT[stage + 1]), f32))
        if stage:
            outs.append(pltpu.VMEM((ROW_AT[stage], new_cols), f32))
        if stage < 3:
            outs += [shape(ROW_AT[stage + 1] // 128, 128), shape(COL_AT[stage + 1] // 128, 128)]
        else:
            outs += [shape(32, 128), shape(32, 128)]
        area = new_rows * COL_AT[stage + 1] + ROW_AT[stage] * new_cols
        got = call(functools.partial(forward_kernel, stage), "forward", ins, outs, limit=10, flops=2 * area * width)
        rows.append(got[0])
        cols.append(got[1])
        wide.append(got[2])
        if stage:
            tall.append(got[3])
        stat = list(got[-2:])
    send, keep = stat

    mine = call(functools.partial(join_kernel, list(range(24))), "join", [core_id, keep, core_swap(send)], [shape(32, 128)], limit=2)[0]
    for dim in range(3):
        got = flip_permute(mine, dim)
        mine = call(functools.partial(join_kernel, flip_order(dim)), "join", [core_id, mine, got], [shape(32, 128)], limit=2)[0]
    other = core_swap(mine)

    held_rows, held_cols = [held(a) for a in rows], [held(a) for a in cols]
    wide_coeffs, tall_coeffs = [], []
    messages = [None] * 3
    for stage in (3, 2, 1):
        ins = [core_id, mine, other, held(wide[stage]), held(tall[stage]), *held_rows, *held_cols]
        ins += [held(a) for a in wide_coeffs + tall_coeffs]
        outs = [pltpu.VMEM((256, COL_AT[stage + 1]), bf16), pltpu.VMEM((ROW_AT[stage], 512), bf16)]
        outs += [shape(512, width, dtype=bf16)] * 2
        if stage == 3:
            outs.append(shape(8, 128))
        got = call(
            functools.partial(far_grad_kernel, stage),
            "far_grad",
            ins,
            outs,
            limit=10,
            flops=2 * (256 * 3072 + 1536 * 512) * width,
        )
        wide_coeffs.insert(0, got[0])
        tall_coeffs.insert(0, got[1])
        if stage == 3:
            loss = got[4]
        ins = [core_id, got[2], core_swap(got[3])]
        if stage == 1:
            ins.append(loss)
        messages[stage - 1] = call(
            far_message_kernel, "far_message", ins, [shape(528 if stage == 1 else 512, width, dtype=bf16)]
        )[0]
    got = [flip_permute(messages[q], q + 2) for q in range(3)]
    bases, near_got, owns = [], [], []
    source = wide[0]
    for q in range(3):
        got_q = call(
            functools.partial(near_grad_kernel, q),
            "near_grad",
            [core_id, mine, other, held(source), *held_rows, *held_cols]
            + [held(a) for a in wide_coeffs + tall_coeffs]
            + messages,
            [shape(512, width), shape(512, width, dtype=bf16), shape(256, width)]
            + ([pltpu.VMEM((768, 1536), bf16)] if q == 0 else []),
            limit=10,
            flops=2 * (256 * 3072 + 1536 * 512) * width,
        )
        bases.append(got_q[0])
        near_got.append(core_swap(got_q[1]))
        owns.append(got_q[2])
        if q == 0:
            source = got_q[3]
    total, loss = call(far_sum_kernel, "far_sum", [core_id, *bases, *got, loss], [shape(1536, width), shape(8, 128)])
    low, *messages = call(
        near_sum_kernel,
        "near_sum",
        [core_id, total, *near_got, loss],
        [shape(768, width)] + [shape(272 if q == 0 else 256, width, dtype=bf16) for q in range(3)],
    )
    got = [flip_permute(messages[q], q + 1) for q in range(3)]
    low, *messages, loss = call(
        half_sum_kernel,
        "half_sum",
        [core_id, low, *got, loss],
        [shape(384, width)] + [shape(144 if q == 0 else 128, width, dtype=bf16) for q in range(3)] + [shape(8, 128)],
    )
    got = [flip_permute(messages[q], q) for q in range(3)]
    keep, send = call(
        last_sum_kernel, "last_sum", [core_id, low, *got, *owns, loss], [shape(392, width), shape(392, width)]
    )
    grad_image, grad_text, loss = call(
        functools.partial(finish_kernel, count),
        "finish",
        [core_id, keep, core_swap(send)],
        [shape(192, width), shape(192, width), shape(1, 1)],
    )
    return loss.reshape(()), grad_image, grad_text


def solution(mesh):
    fine = Mesh(mesh.devices.reshape(4, 4, 4, 2), AXES)
    return jax.shard_map(
        per_device,
        mesh=fine,
        in_specs=(P(AXES, None), P(AXES, None)),
        out_specs=(P(), P(AXES, None), P(AXES, None)),
        check_vma=False,
    )
```

```python
import functools
import itertools
import math

import jax
import jax.numpy as jnp
from jax import lax
from jax.experimental import pallas as pl
from jax.experimental.pallas import tpu as pltpu
from jax.sharding import Mesh, PartitionSpec as P


logit_scale = 10.0
log2e = 1.4426950408889634
ln2 = 0.6931471805599453
lowest = -1e30
f32 = jnp.float32
bf16 = jnp.bfloat16
AXES = ("z", "y", "x", "c")
SWAP = ((0, 1), (1, 0))
FLIPS = ((0, 0, 1), (0, 1, 0), (1, 0, 0))
IMAGE_PAIR = (1, 0, 3, 2)
TEXT_PAIR = (3, 2, 1, 0)
VMEM = pl.BlockSpec(memory_space=pltpu.VMEM)
SMEM = pl.BlockSpec(memory_space=pltpu.SMEM)


def role_pairs(flip):
    pairs = []
    for z, y, x in itertools.product(range(4), repeat=3):
        for core, pair in ((0, IMAGE_PAIR), (1, TEXT_PAIR)):
            target = [pair[v] if f else v for v, f in zip((z, y, x), flip)]
            source_id = ((z * 4 + y) * 4 + x) * 2 + core
            target_id = ((target[0] * 4 + target[1]) * 4 + target[2]) * 2 + core
            pairs.append((source_id, target_id))
    return pairs


ROLE_PAIRS = [role_pairs(flip) for flip in FLIPS]


def flip_permute(x, dim):
    return lax.ppermute(x, AXES, ROLE_PAIRS[dim % 3])


def core_swap(x):
    return lax.ppermute(x, "c", SWAP)


def call(kernel, name, ins, outs, scratch=(), limit=6, flops=0, moved=0):
    in_specs = [SMEM if i == 0 else VMEM for i in range(len(ins))]
    return pl.pallas_call(
        kernel,
        in_specs=in_specs,
        out_specs=[VMEM] * len(outs),
        out_shape=list(outs),
        scratch_shapes=list(scratch),
        compiler_params=pltpu.CompilerParams(vmem_limit_bytes=limit << 20),
        cost_estimate=pl.CostEstimate(flops=flops, bytes_accessed=moved, transcendentals=0),
        name=name,
    )(*ins)


def held(x):
    return pltpu.with_memory_space_constraint(x, pltpu.VMEM)


def shape(*dims, dtype=f32):
    return jax.ShapeDtypeStruct(dims, dtype)


ROW_AT = (0, 768, 1024, 1280, 1536)
COL_AT = (0, 1536, 2048, 2560, 3072)
CONTRACT_LAST = (((1,), (1,)), ((), ()))
CONTRACT_FIRST = (((0,), (0,)), ((), ()))


def log_add(a, b):
    top = jnp.maximum(a, b)
    return top + jnp.log2(jnp.exp2(a - top) + jnp.exp2(b - top))


def lane_blocks(x):
    return [x[:, k : k + 128] for k in range(0, x.shape[1], 128)]


def row_stat(logits):
    top = jnp.max(logits, axis=1, keepdims=True)
    total = jnp.sum(jnp.exp2(logits - top), axis=1, keepdims=True)
    lse = top + jnp.log2(total)
    return jnp.concatenate(lane_blocks(jnp.broadcast_to(lse, (lse.shape[0], 128)).T[0:1, :]), 0)


def column_step(logits, state):
    top = jnp.max(logits, axis=0, keepdims=True)
    if state is None:
        return top, jnp.sum(jnp.exp2(logits - top), axis=0, keepdims=True)
    new_top = jnp.maximum(state[0], top)
    total = state[1] * jnp.exp2(state[0] - new_top) + jnp.sum(jnp.exp2(logits - new_top), axis=0, keepdims=True)
    return new_top, total


def column_stat(state):
    return jnp.concatenate(lane_blocks(state[0] + jnp.log2(state[1])), 0)


def forward_kernel(stage, core_ref, *refs):
    refs = list(refs)
    take = lambda n: [refs.pop(0) for _ in range(n)]
    n = 3 if stage == 0 else 1
    mine = take(n)
    if stage == 0:
        packed_ref = take(1)[0]
        swapped = [packed_ref.at[k * 512 : k * 512 + 512] for k in range(3)]
    else:
        swapped = take(1)
    rows, cols = take(stage), take(stage)
    row_old, col_old = take(2) if stage else (None, None)
    image_ref, text_ref = take(2) if stage == 3 else (None, None)
    rows_ref, cols_ref, wide_ref = take(3)
    tall_ref = take(1)[0] if stage else None
    first = core_ref[0] == 0

    @pl.when(first)
    def _():
        for i in range(n):
            rows_ref[i * 256 : i * 256 + 256, :] = mine[i][0:256, :]
            cols_ref[i * 512 : i * 512 + 512, :] = swapped[i][...]

    @pl.when(jnp.logical_not(first))
    def _():
        for i in range(n):
            rows_ref[i * 256 : i * 256 + 256, :] = swapped[i][256:512, :]
            cols_ref[i * 512 : i * 512 + 512, :] = mine[i][...]

    def product(a, b):
        return lax.dot_general(a, b, CONTRACT_LAST, preferred_element_type=f32) * (logit_scale * log2e)

    cols = cols + [cols_ref]
    new_rows = []
    state = None
    for block in range(n):
        part = slice(block * 256, block * 256 + 256)
        for p in range(stage + 1):
            wide_ref[part, COL_AT[p] : COL_AT[p + 1]] = product(rows_ref[part, :], cols[p][...])
        logits = wide_ref[part, :]
        new_rows.append(row_stat(logits))
        state = column_step(logits, state)
    col = column_stat(state)
    row = jnp.concatenate(new_rows, 0)
    if stage:
        state = None
        old = []
        for p in range(stage):
            for start in range(0, rows[p].shape[0], 256):
                part = slice(ROW_AT[p] + start, ROW_AT[p] + start + 256)
                tall_ref[part, :] = product(rows[p][start : start + 256, :], cols_ref[...])
                logits = tall_ref[part, :]
                old.append(row_stat(logits))
                state = column_step(logits, state)
        row = jnp.concatenate([log_add(row_old[...], jnp.concatenate(old, 0)), row], 0)
        col = log_add(col, jnp.concatenate([col_old[...], column_stat(state)], 0))
    if stage < 3:
        row_out, col_out = take(2)
        row_out[...] = row
        col_out[...] = col
        return
    send_ref, keep_ref = take(2)
    positive = logit_scale * jnp.sum(image_ref[...].astype(f32) * text_ref[...].astype(f32))
    extra = jnp.full((8, 128), positive, f32)
    blank = jnp.full((2, 128), lowest, f32)
    low_half = jnp.concatenate([x for g in range(6) for x in (row[2 * g : 2 * g + 2], blank)], 0)
    high_half = jnp.concatenate([x for g in range(6) for x in (blank, row[2 * g : 2 * g + 2])], 0)
    send_ref[0:24, :] = jnp.where(first, col, high_half)
    keep_ref[0:24, :] = jnp.where(first, low_half, col)
    send_ref[24:32, :] = extra
    keep_ref[24:32, :] = extra


def stack_kernel(core_ref, *refs):
    packed = len(refs) == 10
    for q in range(3):
        a, b, out = refs[q], refs[q + 3], refs[q + 6]
        rows = a.shape[0]
        out[0:rows, :] = a[...]
        out[rows : 2 * rows, :] = b[...]
        if packed:
            refs[9][q * 512 : q * 512 + rows, :] = a[...]
            refs[9][q * 512 + rows : q * 512 + 512, :] = b[...]


def gate_kernel(value_ref, token_ref, out_ref):
    pass


def after(value, token):
    return pl.pallas_call(
        gate_kernel,
        in_specs=[VMEM, VMEM],
        out_specs=VMEM,
        out_shape=pltpu.VMEM(value.shape, value.dtype),
        input_output_aliases={0: 0},
        compiler_params=pltpu.CompilerParams(vmem_limit_bytes=1 << 20),
        name="after",
    )(held(value), token)


def join_kernel(order, core_ref, mine_ref, got_ref, out_ref):
    got = got_ref[...]
    out_ref[0:24, :] = log_add(mine_ref[0:24, :], jnp.concatenate([got[k : k + 1, :] for k in order], 0))
    out_ref[24:32, :] = mine_ref[24:32, :] + got_ref[24:32, :]


def flip_order(dim):
    order = []
    for half, q, k in itertools.product(range(2), range(3), range(4)):
        j = (dim - q) % 3
        if j == 2:
            order.append((1 - half) * 12 + q * 4 + k)
        else:
            order.append(half * 12 + q * 4 + (k ^ (1 << j)))
    return order


def tile_lse(first, mine_ref, other_ref):
    mine, other = mine_ref[0:24, :], other_ref[0:24, :]
    row = jnp.where(first, mine, other)
    col = jnp.where(first, other, mine)
    row = [jnp.where(first, row[4 * g + b : 4 * g + b + 1], row[4 * g + b + 2 : 4 * g + b + 3]) for g in range(6) for b in range(2)]
    row = jnp.concatenate(row, 1) + 1.0
    col = jnp.concatenate([col[k : k + 1] for k in range(24)], 1) + 1.0
    return row, col


def coefficients(logits, row, col):
    n = logits.shape[0]
    row = jnp.broadcast_to(row, (128, n)).T[:, 0:1]
    return jnp.exp2(logits - row) + jnp.exp2(logits - col)


def total_of(terms):
    total = terms[0]
    for term in terms[1:]:
        total = total + term
    return logit_scale * total


def times(a, b):
    return jnp.dot(a, b, preferred_element_type=f32)


def transposed_times(a, b):
    return lax.dot_general(a, b, CONTRACT_FIRST, preferred_element_type=f32)


def far_grad_kernel(stage, core_ref, mine_ref, other_ref, *refs):
    refs = list(refs)
    take = lambda n: [refs.pop(0) for _ in range(n)]
    wide_in, tall_in = take(2)
    rows, cols = take(4), take(4)
    wide = [None] * (stage + 1) + take(3 - stage)
    tall = [None] * (stage + 1) + take(3 - stage)
    wide[stage], tall[stage] = take(2)
    kept_ref, send_ref = take(2)
    first = core_ref[0] == 0
    row, col = tile_lse(first, mine_ref, other_ref)
    if stage == 3:
        loss_ref = take(1)[0]
        loss_ref[...] = jnp.sum(other_ref[0:24, :]) * ln2 - jnp.where(first, 0.0, 2.0) * other_ref[24:32, :]
    wide[stage][...] = coefficients(
        wide_in[...], row[:, ROW_AT[stage] : ROW_AT[stage + 1]], col[:, 0 : COL_AT[stage + 1]]
    ).astype(bf16)
    for start in range(0, ROW_AT[stage], 256):
        part = slice(start, start + 256)
        tall[stage][part, :] = coefficients(
            tall_in[part, :], row[:, part], col[:, COL_AT[stage] : COL_AT[stage + 1]]
        ).astype(bf16)
    here = slice(ROW_AT[stage], ROW_AT[stage + 1])
    image = [times(wide[stage][:, COL_AT[p] : COL_AT[p + 1]], cols[p][...]) for p in range(stage + 1)]
    image += [times(tall[p][here, :], cols[p][...]) for p in range(stage + 1, 4)]
    image = total_of(image).astype(bf16)
    here = slice(COL_AT[stage], COL_AT[stage + 1])
    text = [transposed_times(tall[stage][ROW_AT[p] : ROW_AT[p + 1], :], rows[p][...]) for p in range(stage)]
    text += [transposed_times(wide[p][:, here], rows[p][...]) for p in range(stage, 4)]
    text = total_of(text).astype(bf16)
    kept_ref[0:256, :] = jnp.where(first, image, text[0:256])
    send_ref[0:256, :] = jnp.where(first, text[0:256], image)
    kept_ref[256:512, :] = text[256:512]
    send_ref[256:512, :] = text[256:512]


def near_grad_kernel(q, core_ref, mine_ref, other_ref, *refs):
    refs = list(refs)
    take = lambda n: [refs.pop(0) for _ in range(n)]
    source_ref = take(1)[0]
    rows, cols = take(4), take(4)
    wide, tall = [None] + take(3), [None] + take(3)
    take(3)
    base_ref, send_ref, own_ref = take(3)
    first = core_ref[0] == 0
    block_ref = source_ref
    if q == 0:
        block_ref = take(1)[0]
        row, col = tile_lse(first, mine_ref, other_ref)
        eye = lax.broadcasted_iota(jnp.int32, (128, 128), 0) == lax.broadcasted_iota(jnp.int32, (128, 128), 1)
        positive = jnp.where(jnp.logical_and(eye, first), 1.0, 0.0)
        for k in range(3):
            part = slice(k * 256, k * 256 + 256)
            coeffs = coefficients(source_ref[part, :], row[:, part], col[:, 0:1536])
            block_ref[part, :] = coeffs.astype(bf16)
            own = slice(k * 512, k * 512 + 128)
            block_ref[k * 256 : k * 256 + 128, own] = (coeffs[0:128, own] - positive).astype(bf16)
    part = slice(q * 256, q * 256 + 256)
    image = total_of(
        [times(block_ref[part, :], cols[0][...])] + [times(tall[p][part, :], cols[p][...]) for p in range(1, 4)]
    )
    here = slice(q * 512, q * 512 + 512)
    text = total_of(
        [transposed_times(block_ref[:, here], rows[0][...])]
        + [transposed_times(wide[p][:, here], rows[p][...]) for p in range(1, 4)]
    )
    own_ref[0:128, :] = image[0:128]
    own_ref[128:256, :] = text[0:128]
    base_ref[0:128, :] = jnp.where(first, 0.0, text[0:128])
    base_ref[128:256, :] = jnp.where(first, image[128:256], text[128:256])
    base_ref[256:512, :] = jnp.where(first, 0.0, text[256:512])
    send_ref[0:128, :] = jnp.where(first, 0.0, image[0:128]).astype(bf16)
    send_ref[128:256, :] = jnp.where(first, text[128:256], image[128:256]).astype(bf16)
    send_ref[256:512, :] = text[256:512].astype(bf16)


def split_terms(x):
    high = x.astype(bf16)
    rest = x - high.astype(f32)
    middle = rest.astype(bf16)
    low = (rest - middle.astype(f32)).astype(bf16)
    pair = [jnp.concatenate([t, t], 0) for t in (high, middle, low)]
    return jnp.concatenate(pair + [jnp.zeros((16, 128), bf16)], 1)


def join_terms(ref, start):
    x = ref[start : start + 16, :].astype(f32)
    return (x[0:8, 0:128] + x[0:8, 128:256]) + x[0:8, 256:384]


def far_message_kernel(core_ref, mine_ref, got_ref, *refs):
    first = core_ref[0] == 0
    got = got_ref[...]
    both = (mine_ref[...].astype(f32) + got.astype(f32)).astype(bf16)
    refs[-1][0:256, :] = jnp.where(first, mine_ref[0:256, :], both[0:256])
    refs[-1][256:512, :] = jnp.where(first, got[0:256], both[256:512])
    if len(refs) == 2:
        refs[-1][512:528, :] = split_terms(refs[0][...])


def far_sum_kernel(core_ref, b0, b1, b2, r0, r1, r2, loss_ref, total_ref, loss_out):
    loss_out[...] = loss_ref[...] + join_terms(r0, 512)
    for q, (b, r) in enumerate(((b0, r0), (b1, r1), (b2, r2))):
        total_ref[q * 512 : q * 512 + 512, :] = b[...] + r[0:512, :].astype(f32)


def near_sum_kernel(core_ref, total_ref, g0, g1, g2, loss_ref, low_ref, s0, s1, s2):
    first = core_ref[0] == 0
    s0[256:272, :] = split_terms(loss_ref[...])
    for q, (g, s) in enumerate(((g0, s0), (g1, s1), (g2, s2))):
        at = q * 512
        got = g[...].astype(f32)
        low_ref[q * 256 : q * 256 + 256, :] = total_ref[at : at + 256, :] + jnp.where(first, 0.0, got[0:256])
        s[0:256, :] = (total_ref[at + 256 : at + 512, :] + jnp.where(first, got[0:256], got[256:512])).astype(bf16)


def half_sum_kernel(core_ref, low_ref, r0, r1, r2, loss_ref, out_ref, s0, s1, s2, loss_out):
    loss = loss_ref[...] + join_terms(r0, 256)
    loss_out[...] = loss
    s0[128:144, :] = split_terms(loss)
    for q, (r, s) in enumerate(((r0, s0), (r1, s1), (r2, s2))):
        total = low_ref[q * 256 : q * 256 + 256, :] + r[0:256, :].astype(f32)
        out_ref[q * 128 : q * 128 + 128, :] = total[0:128]
        s[0:128, :] = total[128:256].astype(bf16)


def last_sum_kernel(core_ref, low_ref, r0, r1, r2, o0, o1, o2, loss_ref, keep_ref, send_ref):
    first = core_ref[0] == 0
    loss = loss_ref[...] + join_terms(r0, 128)
    keep_ref[384:392, :] = jnp.concatenate([loss] * 4, 1)
    send_ref[384:392, :] = jnp.concatenate([loss] * 4, 1)
    for q, (r, own) in enumerate(((r0, o0), (r1, o1), (r2, o2))):
        rows, text_rows = slice(q * 64, q * 64 + 64), slice(192 + q * 64, 192 + q * 64 + 64)
        total = low_ref[q * 128 : q * 128 + 128, :] + r[0:128, :].astype(f32)
        keep_ref[rows, :] = jnp.where(first, total[0:64] + own[0:64, :], total[64:128])
        keep_ref[text_rows, :] = own[128:192, :]
        send_ref[rows, :] = jnp.where(first, total[64:128] + own[64:128, :], total[0:64])
        send_ref[text_rows, :] = own[192:256, :]


def finish_kernel(count, core_ref, keep_ref, got_ref, image_out, text_out, loss_out):
    first = core_ref[0] == 0
    image_out[...] = jnp.where(first, keep_ref[0:192, :], got_ref[0:192, :])
    text_out[...] = jnp.where(
        first, got_ref[0:192, :] + keep_ref[192:384, :], keep_ref[0:192, :] + got_ref[192:384, :]
    )
    loss_out[...] = (keep_ref[384:385, 0:1] + got_ref[384:385, 0:1]) * (0.5 / count)


def select_kernel(core_ref, image_ref, text_ref, out_ref):
    out_ref[...] = jnp.where(core_ref[0] == 0, text_ref[...], image_ref[...])


def pair_kernel(core_ref, image_ref, text_ref, got_ref, *out_refs):
    first = core_ref[0] == 0
    for q, out in enumerate(out_refs):
        rows = slice(q * 64, q * 64 + 64)
        out[0:64, :] = jnp.where(first, image_ref[rows, :], got_ref[rows, :])
        out[64:128, :] = jnp.where(first, got_ref[rows, :], text_ref[rows, :])


def per_device(image_emb, text_emb):
    core_id = lax.axis_index("c").reshape(1).astype(jnp.int32)
    pair_rows, width = image_emb.shape
    count = pair_rows * 128

    swapped = core_swap(call(select_kernel, "select", [core_id, image_emb, text_emb], [shape(pair_rows, width, dtype=bf16)], limit=4)[0])
    near = call(
        pair_kernel, "pair", [core_id, image_emb, text_emb, swapped], [shape(128, width, dtype=bf16)] * 3, limit=4
    )
    for step in range(2):
        got = [flip_permute(near[q], q + step) for q in range(3)]
        outs = [shape(256 << step, width, dtype=bf16)] * 3 + [shape(1536, width, dtype=bf16)] * step
        near = call(stack_kernel, "stack", [core_id, *near, *got], outs, limit=2)
    *near, packed = near
    near_x = [core_swap(packed)]
    far = [flip_permute(near[q], q + 2) for q in range(3)]
    far_x = [None] * 3

    rows, cols, wide, tall = [], [], [], [None]
    stat = []
    for stage in range(4):
        for q in {1: (0, 1, 2)}.get(stage, ()):
            far[q] = after(far[q], stat[0])
            far_x[q] = core_swap(far[q])
        ins = [core_id] + (near + near_x if stage == 0 else [far[stage - 1], far_x[stage - 1]])
        ins += [held(a) for a in rows + cols] + stat
        if stage == 3:
            ins += [image_emb, text_emb]
        new_rows = 768 if stage == 0 else 256
        new_cols = 1536 if stage == 0 else 512
        outs = [pltpu.VMEM((new_rows, width), bf16), pltpu.VMEM((new_cols, width), bf16)]
        outs.append(pltpu.VMEM((new_rows, COL_AT[stage + 1]), f32))
        if stage:
            outs.append(pltpu.VMEM((ROW_AT[stage], new_cols), f32))
        if stage < 3:
            outs += [shape(ROW_AT[stage + 1] // 128, 128), shape(COL_AT[stage + 1] // 128, 128)]
        else:
            outs += [shape(32, 128), shape(32, 128)]
        area = new_rows * COL_AT[stage + 1] + ROW_AT[stage] * new_cols
        got = call(functools.partial(forward_kernel, stage), "forward", ins, outs, limit=10, flops=2 * area * width)
        rows.append(got[0])
        cols.append(got[1])
        wide.append(got[2])
        if stage:
            tall.append(got[3])
        stat = list(got[-2:])
    send, keep = stat

    mine = call(functools.partial(join_kernel, list(range(24))), "join", [core_id, keep, core_swap(send)], [shape(32, 128)], limit=2)[0]
    for dim in range(3):
        got = flip_permute(mine, dim)
        mine = call(functools.partial(join_kernel, flip_order(dim)), "join", [core_id, mine, got], [shape(32, 128)], limit=2)[0]
    other = core_swap(mine)

    held_rows, held_cols = [held(a) for a in rows], [held(a) for a in cols]
    wide_coeffs, tall_coeffs = [], []
    messages = [None] * 3
    for stage in (3, 2, 1):
        ins = [core_id, mine, other, held(wide[stage]), held(tall[stage]), *held_rows, *held_cols]
        ins += [held(a) for a in wide_coeffs + tall_coeffs]
        outs = [pltpu.VMEM((256, COL_AT[stage + 1]), bf16), pltpu.VMEM((ROW_AT[stage], 512), bf16)]
        outs += [shape(512, width, dtype=bf16)] * 2
        if stage == 3:
            outs.append(shape(8, 128))
        got = call(
            functools.partial(far_grad_kernel, stage),
            "far_grad",
            ins,
            outs,
            limit=10,
            flops=2 * (256 * 3072 + 1536 * 512) * width,
        )
        wide_coeffs.insert(0, got[0])
        tall_coeffs.insert(0, got[1])
        if stage == 3:
            loss = got[4]
        ins = [core_id, got[2], core_swap(got[3])]
        if stage == 1:
            ins.append(loss)
        messages[stage - 1] = call(
            far_message_kernel, "far_message", ins, [shape(528 if stage == 1 else 512, width, dtype=bf16)]
        )[0]
    got = [flip_permute(messages[q], q + 2) for q in range(3)]
    bases, near_got, owns = [], [], []
    source = wide[0]
    for q in range(3):
        got_q = call(
            functools.partial(near_grad_kernel, q),
            "near_grad",
            [core_id, mine, other, held(source), *held_rows, *held_cols]
            + [held(a) for a in wide_coeffs + tall_coeffs]
            + messages,
            [shape(512, width), shape(512, width, dtype=bf16), shape(256, width)]
            + ([pltpu.VMEM((768, 1536), bf16)] if q == 0 else []),
            limit=10,
            flops=2 * (256 * 3072 + 1536 * 512) * width,
        )
        bases.append(got_q[0])
        near_got.append(core_swap(got_q[1]))
        owns.append(got_q[2])
        if q == 0:
            source = got_q[3]
    total, loss = call(far_sum_kernel, "far_sum", [core_id, *bases, *got, loss], [shape(1536, width), shape(8, 128)])
    low, *messages = call(
        near_sum_kernel,
        "near_sum",
        [core_id, total, *near_got, loss],
        [shape(768, width)] + [shape(272 if q == 0 else 256, width, dtype=bf16) for q in range(3)],
    )
    got = [flip_permute(messages[q], q + 1) for q in range(3)]
    low, *messages, loss = call(
        half_sum_kernel,
        "half_sum",
        [core_id, low, *got, loss],
        [shape(384, width)] + [shape(144 if q == 0 else 128, width, dtype=bf16) for q in range(3)] + [shape(8, 128)],
    )
    got = [flip_permute(messages[q], q) for q in range(3)]
    keep, send = call(
        last_sum_kernel, "last_sum", [core_id, low, *got, *owns, loss], [shape(392, width), shape(392, width)]
    )
    grad_image, grad_text, loss = call(
        functools.partial(finish_kernel, count),
        "finish",
        [core_id, keep, core_swap(send)],
        [shape(192, width), shape(192, width), shape(1, 1)],
    )
    return loss.reshape(()), grad_image, grad_text


def solution(mesh):
    fine = Mesh(mesh.devices.reshape(4, 4, 4, 2), AXES)
    return jax.shard_map(
        per_device,
        mesh=fine,
        in_specs=(P(AXES, None), P(AXES, None)),
        out_specs=(P(), P(AXES, None), P(AXES, None)),
        check_vma=False,
    )
```

```python
import functools
import itertools
import math

import jax
import jax.numpy as jnp
from jax import lax
from jax.experimental import pallas as pl
from jax.experimental.pallas import tpu as pltpu
from jax.sharding import Mesh, PartitionSpec as P


logit_scale = 10.0
log2e = 1.4426950408889634
ln2 = 0.6931471805599453
lowest = -1e30
f32 = jnp.float32
bf16 = jnp.bfloat16
AXES = ("z", "y", "x", "c")
SWAP = ((0, 1), (1, 0))
FLIPS = ((0, 0, 1), (0, 1, 0), (1, 0, 0))
IMAGE_PAIR = (1, 0, 3, 2)
TEXT_PAIR = (3, 2, 1, 0)
VMEM = pl.BlockSpec(memory_space=pltpu.VMEM)
SMEM = pl.BlockSpec(memory_space=pltpu.SMEM)


def role_pairs(flip):
    pairs = []
    for z, y, x in itertools.product(range(4), repeat=3):
        for core, pair in ((0, IMAGE_PAIR), (1, TEXT_PAIR)):
            target = [pair[v] if f else v for v, f in zip((z, y, x), flip)]
            source_id = ((z * 4 + y) * 4 + x) * 2 + core
            target_id = ((target[0] * 4 + target[1]) * 4 + target[2]) * 2 + core
            pairs.append((source_id, target_id))
    return pairs


ROLE_PAIRS = [role_pairs(flip) for flip in FLIPS]


def flip_permute(x, dim):
    return lax.ppermute(x, AXES, ROLE_PAIRS[dim % 3])


def core_swap(x):
    return lax.ppermute(x, "c", SWAP)


def call(kernel, name, ins, outs, scratch=(), limit=6, flops=0, moved=0):
    in_specs = [SMEM if i == 0 else VMEM for i in range(len(ins))]
    return pl.pallas_call(
        kernel,
        in_specs=in_specs,
        out_specs=[VMEM] * len(outs),
        out_shape=list(outs),
        scratch_shapes=list(scratch),
        compiler_params=pltpu.CompilerParams(vmem_limit_bytes=limit << 20),
        cost_estimate=pl.CostEstimate(flops=flops, bytes_accessed=moved, transcendentals=0),
        name=name,
    )(*ins)


def held(x):
    return pltpu.with_memory_space_constraint(x, pltpu.VMEM)


def shape(*dims, dtype=f32):
    return jax.ShapeDtypeStruct(dims, dtype)


ROW_AT = (0, 768, 1024, 1280, 1536)
COL_AT = (0, 1536, 2048, 2560, 3072)
CONTRACT_LAST = (((1,), (1,)), ((), ()))
CONTRACT_FIRST = (((0,), (0,)), ((), ()))


def log_add(a, b):
    top = jnp.maximum(a, b)
    return top + jnp.log2(jnp.exp2(a - top) + jnp.exp2(b - top))


def lane_blocks(x):
    return [x[:, k : k + 128] for k in range(0, x.shape[1], 128)]


def row_stat(logits):
    top = jnp.max(logits, axis=1, keepdims=True)
    total = jnp.sum(jnp.exp2(logits - top), axis=1, keepdims=True)
    lse = top + jnp.log2(total)
    return jnp.concatenate(lane_blocks(jnp.broadcast_to(lse, (lse.shape[0], 128)).T[0:1, :]), 0)


def column_step(logits, state):
    top = jnp.max(logits, axis=0, keepdims=True)
    if state is None:
        return top, jnp.sum(jnp.exp2(logits - top), axis=0, keepdims=True)
    new_top = jnp.maximum(state[0], top)
    total = state[1] * jnp.exp2(state[0] - new_top) + jnp.sum(jnp.exp2(logits - new_top), axis=0, keepdims=True)
    return new_top, total


def column_stat(state):
    return jnp.concatenate(lane_blocks(state[0] + jnp.log2(state[1])), 0)


def forward_kernel(stage, core_ref, *refs):
    refs = list(refs)
    take = lambda n: [refs.pop(0) for _ in range(n)]
    n = 3 if stage == 0 else 1
    mine = take(n)
    if stage == 0:
        packed_ref = take(1)[0]
        swapped = [packed_ref.at[k * 512 : k * 512 + 512] for k in range(3)]
    else:
        swapped = take(1)
    rows, cols = take(stage), take(stage)
    row_old, col_old = take(2) if stage else (None, None)
    image_ref, text_ref = take(2) if stage == 3 else (None, None)
    rows_ref, cols_ref, wide_ref = take(3)
    tall_ref = take(1)[0] if stage else None
    first = core_ref[0] == 0

    @pl.when(first)
    def _():
        for i in range(n):
            rows_ref[i * 256 : i * 256 + 256, :] = mine[i][0:256, :]
            cols_ref[i * 512 : i * 512 + 512, :] = swapped[i][...]

    @pl.when(jnp.logical_not(first))
    def _():
        for i in range(n):
            rows_ref[i * 256 : i * 256 + 256, :] = swapped[i][256:512, :]
            cols_ref[i * 512 : i * 512 + 512, :] = mine[i][...]

    def product(a, b):
        return lax.dot_general(a, b, CONTRACT_LAST, preferred_element_type=f32) * (logit_scale * log2e)

    cols = cols + [cols_ref]
    new_rows = []
    state = None
    for block in range(n):
        part = slice(block * 256, block * 256 + 256)
        for p in range(stage + 1):
            wide_ref[part, COL_AT[p] : COL_AT[p + 1]] = product(rows_ref[part, :], cols[p][...])
        logits = wide_ref[part, :]
        new_rows.append(row_stat(logits))
        state = column_step(logits, state)
    col = column_stat(state)
    row = jnp.concatenate(new_rows, 0)
    if stage:
        state = None
        old = []
        for p in range(stage):
            for start in range(0, rows[p].shape[0], 256):
                part = slice(ROW_AT[p] + start, ROW_AT[p] + start + 256)
                tall_ref[part, :] = product(rows[p][start : start + 256, :], cols_ref[...])
                logits = tall_ref[part, :]
                old.append(row_stat(logits))
                state = column_step(logits, state)
        row = jnp.concatenate([log_add(row_old[...], jnp.concatenate(old, 0)), row], 0)
        col = log_add(col, jnp.concatenate([col_old[...], column_stat(state)], 0))
    if stage < 3:
        row_out, col_out = take(2)
        row_out[...] = row
        col_out[...] = col
        return
    send_ref, keep_ref = take(2)
    positive = logit_scale * jnp.sum(image_ref[...].astype(f32) * text_ref[...].astype(f32))
    extra = jnp.full((8, 128), positive, f32)
    blank = jnp.full((2, 128), lowest, f32)
    low_half = jnp.concatenate([x for g in range(6) for x in (row[2 * g : 2 * g + 2], blank)], 0)
    high_half = jnp.concatenate([x for g in range(6) for x in (blank, row[2 * g : 2 * g + 2])], 0)
    send_ref[0:24, :] = jnp.where(first, col, high_half)
    keep_ref[0:24, :] = jnp.where(first, low_half, col)
    send_ref[24:32, :] = extra
    keep_ref[24:32, :] = extra


def stack_kernel(core_ref, *refs):
    packed = len(refs) == 10
    for q in range(3):
        a, b, out = refs[q], refs[q + 3], refs[q + 6]
        rows = a.shape[0]
        out[0:rows, :] = a[...]
        out[rows : 2 * rows, :] = b[...]
        if packed:
            refs[9][q * 512 : q * 512 + rows, :] = a[...]
            refs[9][q * 512 + rows : q * 512 + 512, :] = b[...]


def gate_kernel(value_ref, token_ref, out_ref):
    pass


def after(value, token):
    return pl.pallas_call(
        gate_kernel,
        in_specs=[VMEM, VMEM],
        out_specs=VMEM,
        out_shape=pltpu.VMEM(value.shape, value.dtype),
        input_output_aliases={0: 0},
        compiler_params=pltpu.CompilerParams(vmem_limit_bytes=1 << 20),
        name="after",
    )(held(value), token)


def join_kernel(order, core_ref, mine_ref, got_ref, out_ref):
    got = got_ref[...]
    out_ref[0:24, :] = log_add(mine_ref[0:24, :], jnp.concatenate([got[k : k + 1, :] for k in order], 0))
    out_ref[24:32, :] = mine_ref[24:32, :] + got_ref[24:32, :]


def flip_order(dim):
    order = []
    for half, q, k in itertools.product(range(2), range(3), range(4)):
        j = (dim - q) % 3
        if j == 2:
            order.append((1 - half) * 12 + q * 4 + k)
        else:
            order.append(half * 12 + q * 4 + (k ^ (1 << j)))
    return order


def tile_lse(first, mine_ref, other_ref):
    mine, other = mine_ref[0:24, :], other_ref[0:24, :]
    row = jnp.where(first, mine, other)
    col = jnp.where(first, other, mine)
    row = [jnp.where(first, row[4 * g + b : 4 * g + b + 1], row[4 * g + b + 2 : 4 * g + b + 3]) for g in range(6) for b in range(2)]
    row = jnp.concatenate(row, 1) + 1.0
    col = jnp.concatenate([col[k : k + 1] for k in range(24)], 1) + 1.0
    return row, col


def coefficients(logits, row, col):
    n = logits.shape[0]
    row = jnp.broadcast_to(row, (128, n)).T[:, 0:1]
    return jnp.exp2(logits - row) + jnp.exp2(logits - col)


def total_of(terms):
    total = terms[0]
    for term in terms[1:]:
        total = total + term
    return logit_scale * total


def times(a, b):
    return jnp.dot(a, b, preferred_element_type=f32)


def transposed_times(a, b):
    return lax.dot_general(a, b, CONTRACT_FIRST, preferred_element_type=f32)


def far_grad_kernel(stage, core_ref, mine_ref, other_ref, *refs):
    refs = list(refs)
    take = lambda n: [refs.pop(0) for _ in range(n)]
    wide_in, tall_in = take(2)
    rows, cols = take(4), take(4)
    wide = [None] * (stage + 1) + take(3 - stage)
    tall = [None] * (stage + 1) + take(3 - stage)
    wide[stage], tall[stage] = take(2)
    kept_ref, send_ref = take(2)
    first = core_ref[0] == 0
    row, col = tile_lse(first, mine_ref, other_ref)
    if stage == 3:
        loss_ref = take(1)[0]
        loss_ref[...] = jnp.sum(other_ref[0:24, :]) * ln2 - jnp.where(first, 0.0, 2.0) * other_ref[24:32, :]
    wide[stage][...] = coefficients(
        wide_in[...], row[:, ROW_AT[stage] : ROW_AT[stage + 1]], col[:, 0 : COL_AT[stage + 1]]
    ).astype(bf16)
    here = slice(ROW_AT[stage], ROW_AT[stage + 1])
    image = [times(wide[stage][:, COL_AT[p] : COL_AT[p + 1]], cols[p][...]) for p in range(stage + 1)]
    image += [times(tall[p][here, :], cols[p][...]) for p in range(stage + 1, 4)]
    image = total_of(image).astype(bf16)
    for start in range(0, ROW_AT[stage], 256):
        part = slice(start, start + 256)
        tall[stage][part, :] = coefficients(
            tall_in[part, :], row[:, part], col[:, COL_AT[stage] : COL_AT[stage + 1]]
        ).astype(bf16)
    here = slice(COL_AT[stage], COL_AT[stage + 1])
    text = [transposed_times(tall[stage][ROW_AT[p] : ROW_AT[p + 1], :], rows[p][...]) for p in range(stage)]
    text += [transposed_times(wide[p][:, here], rows[p][...]) for p in range(stage, 4)]
    text = total_of(text).astype(bf16)
    kept_ref[0:256, :] = jnp.where(first, image, text[0:256])
    send_ref[0:256, :] = jnp.where(first, text[0:256], image)
    kept_ref[256:512, :] = text[256:512]
    send_ref[256:512, :] = text[256:512]


def near_grad_kernel(q, core_ref, mine_ref, other_ref, *refs):
    refs = list(refs)
    take = lambda n: [refs.pop(0) for _ in range(n)]
    source_ref = take(1)[0]
    rows, cols = take(4), take(4)
    wide, tall = [None] + take(3), [None] + take(3)
    take(3)
    base_ref, send_ref, own_ref = take(3)
    first = core_ref[0] == 0
    block_ref = source_ref
    if q == 0:
        block_ref = take(1)[0]
        row, col = tile_lse(first, mine_ref, other_ref)
        eye = lax.broadcasted_iota(jnp.int32, (128, 128), 0) == lax.broadcasted_iota(jnp.int32, (128, 128), 1)
        positive = jnp.where(jnp.logical_and(eye, first), 1.0, 0.0)
    def image_grad():
        part = slice(q * 256, q * 256 + 256)
        terms = [times(block_ref[part, :], cols[0][...])]
        return total_of(terms + [times(tall[p][part, :], cols[p][...]) for p in range(1, 4)])

    if q == 0:
        for k in range(3):
            part = slice(k * 256, k * 256 + 256)
            coeffs = coefficients(source_ref[part, :], row[:, part], col[:, 0:1536])
            block_ref[part, :] = coeffs.astype(bf16)
            own = slice(k * 512, k * 512 + 128)
            block_ref[k * 256 : k * 256 + 128, own] = (coeffs[0:128, own] - positive).astype(bf16)
            if k == 0:
                image = image_grad()
    else:
        image = image_grad()
    here = slice(q * 512, q * 512 + 512)
    text = total_of(
        [transposed_times(block_ref[:, here], rows[0][...])]
        + [transposed_times(wide[p][:, here], rows[p][...]) for p in range(1, 4)]
    )
    own_ref[0:128, :] = image[0:128]
    own_ref[128:256, :] = text[0:128]
    base_ref[0:128, :] = jnp.where(first, 0.0, text[0:128])
    base_ref[128:256, :] = jnp.where(first, image[128:256], text[128:256])
    base_ref[256:512, :] = jnp.where(first, 0.0, text[256:512])
    send_ref[0:128, :] = jnp.where(first, 0.0, image[0:128]).astype(bf16)
    send_ref[128:256, :] = jnp.where(first, text[128:256], image[128:256]).astype(bf16)
    send_ref[256:512, :] = text[256:512].astype(bf16)


def split_terms(x):
    high = x.astype(bf16)
    rest = x - high.astype(f32)
    middle = rest.astype(bf16)
    low = (rest - middle.astype(f32)).astype(bf16)
    pair = [jnp.concatenate([t, t], 0) for t in (high, middle, low)]
    return jnp.concatenate(pair + [jnp.zeros((16, 128), bf16)], 1)


def join_terms(ref, start):
    x = ref[start : start + 16, :].astype(f32)
    return (x[0:8, 0:128] + x[0:8, 128:256]) + x[0:8, 256:384]


def far_message_kernel(core_ref, mine_ref, got_ref, *refs):
    first = core_ref[0] == 0
    got = got_ref[...]
    both = (mine_ref[...].astype(f32) + got.astype(f32)).astype(bf16)
    refs[-1][0:256, :] = jnp.where(first, mine_ref[0:256, :], both[0:256])
    refs[-1][256:512, :] = jnp.where(first, got[0:256], both[256:512])
    if len(refs) == 2:
        refs[-1][512:528, :] = split_terms(refs[0][...])


def far_sum_kernel(core_ref, b0, b1, b2, r0, r1, r2, loss_ref, total_ref, loss_out):
    loss_out[...] = loss_ref[...] + join_terms(r0, 512)
    for q, (b, r) in enumerate(((b0, r0), (b1, r1), (b2, r2))):
        total_ref[q * 512 : q * 512 + 512, :] = b[...] + r[0:512, :].astype(f32)


def near_sum_kernel(core_ref, total_ref, g0, g1, g2, loss_ref, low_ref, s0, s1, s2):
    first = core_ref[0] == 0
    s0[256:272, :] = split_terms(loss_ref[...])
    for q, (g, s) in enumerate(((g0, s0), (g1, s1), (g2, s2))):
        at = q * 512
        got = g[...].astype(f32)
        low_ref[q * 256 : q * 256 + 256, :] = total_ref[at : at + 256, :] + jnp.where(first, 0.0, got[0:256])
        s[0:256, :] = (total_ref[at + 256 : at + 512, :] + jnp.where(first, got[0:256], got[256:512])).astype(bf16)


def half_sum_kernel(core_ref, low_ref, r0, r1, r2, loss_ref, out_ref, s0, s1, s2, loss_out):
    loss = loss_ref[...] + join_terms(r0, 256)
    loss_out[...] = loss
    s0[128:144, :] = split_terms(loss)
    for q, (r, s) in enumerate(((r0, s0), (r1, s1), (r2, s2))):
        total = low_ref[q * 256 : q * 256 + 256, :] + r[0:256, :].astype(f32)
        out_ref[q * 128 : q * 128 + 128, :] = total[0:128]
        s[0:128, :] = total[128:256].astype(bf16)


def last_sum_kernel(core_ref, low_ref, r0, r1, r2, o0, o1, o2, loss_ref, keep_ref, send_ref):
    first = core_ref[0] == 0
    loss = loss_ref[...] + join_terms(r0, 128)
    keep_ref[384:392, :] = jnp.concatenate([loss] * 4, 1)
    send_ref[384:392, :] = jnp.concatenate([loss] * 4, 1)
    for q, (r, own) in enumerate(((r0, o0), (r1, o1), (r2, o2))):
        rows, text_rows = slice(q * 64, q * 64 + 64), slice(192 + q * 64, 192 + q * 64 + 64)
        total = low_ref[q * 128 : q * 128 + 128, :] + r[0:128, :].astype(f32)
        keep_ref[rows, :] = jnp.where(first, total[0:64] + own[0:64, :], total[64:128])
        keep_ref[text_rows, :] = own[128:192, :]
        send_ref[rows, :] = jnp.where(first, total[64:128] + own[64:128, :], total[0:64])
        send_ref[text_rows, :] = own[192:256, :]


def finish_kernel(count, core_ref, keep_ref, got_ref, image_out, text_out, loss_out):
    first = core_ref[0] == 0
    image_out[...] = jnp.where(first, keep_ref[0:192, :], got_ref[0:192, :])
    text_out[...] = jnp.where(
        first, got_ref[0:192, :] + keep_ref[192:384, :], keep_ref[0:192, :] + got_ref[192:384, :]
    )
    loss_out[...] = (keep_ref[384:385, 0:1] + got_ref[384:385, 0:1]) * (0.5 / count)


def pair_kernel(core_ref, image_ref, text_ref, image_got, text_got, *out_refs):
    first = core_ref[0] == 0
    for q, out in enumerate(out_refs):
        rows = slice(q * 64, q * 64 + 64)
        out[0:64, :] = jnp.where(first, image_ref[rows, :], text_got[rows, :])
        out[64:128, :] = jnp.where(first, image_got[rows, :], text_ref[rows, :])


def per_device(image_emb, text_emb):
    core_id = lax.axis_index("c").reshape(1).astype(jnp.int32)
    pair_rows, width = image_emb.shape
    count = pair_rows * 128

    got = [core_swap(image_emb), core_swap(text_emb)]
    near = call(
        pair_kernel, "pair", [core_id, image_emb, text_emb, *got], [shape(128, width, dtype=bf16)] * 3, limit=4
    )
    for step in range(2):
        got = [flip_permute(near[q], q + step) for q in range(3)]
        outs = [shape(256 << step, width, dtype=bf16)] * 3 + [shape(1536, width, dtype=bf16)] * step
        near = call(stack_kernel, "stack", [core_id, *near, *got], outs, limit=2)
    *near, packed = near
    near_x = [core_swap(packed)]
    far = [flip_permute(near[q], q + 2) for q in range(3)]
    far_x = [None] * 3

    rows, cols, wide, tall = [], [], [], [None]
    stat = []
    for stage in range(4):
        for q in {1: (0, 1, 2)}.get(stage, ()):
            far[q] = after(far[q], stat[0])
            far_x[q] = core_swap(far[q])
        ins = [core_id] + (near + near_x if stage == 0 else [far[stage - 1], far_x[stage - 1]])
        ins += [held(a) for a in rows + cols] + stat
        if stage == 3:
            ins += [image_emb, text_emb]
        new_rows = 768 if stage == 0 else 256
        new_cols = 1536 if stage == 0 else 512
        outs = [pltpu.VMEM((new_rows, width), bf16), pltpu.VMEM((new_cols, width), bf16)]
        outs.append(pltpu.VMEM((new_rows, COL_AT[stage + 1]), f32))
        if stage:
            outs.append(pltpu.VMEM((ROW_AT[stage], new_cols), f32))
        if stage < 3:
            outs += [shape(ROW_AT[stage + 1] // 128, 128), shape(COL_AT[stage + 1] // 128, 128)]
        else:
            outs += [shape(32, 128), shape(32, 128)]
        area = new_rows * COL_AT[stage + 1] + ROW_AT[stage] * new_cols
        got = call(functools.partial(forward_kernel, stage), "forward", ins, outs, limit=10, flops=2 * area * width)
        rows.append(got[0])
        cols.append(got[1])
        wide.append(got[2])
        if stage:
            tall.append(got[3])
        stat = list(got[-2:])
    send, keep = stat

    mine = call(functools.partial(join_kernel, list(range(24))), "join", [core_id, keep, core_swap(send)], [shape(32, 128)], limit=2)[0]
    for dim in range(3):
        got = flip_permute(mine, dim)
        mine = call(functools.partial(join_kernel, flip_order(dim)), "join", [core_id, mine, got], [shape(32, 128)], limit=2)[0]
    other = core_swap(mine)

    held_rows, held_cols = [held(a) for a in rows], [held(a) for a in cols]
    wide_coeffs, tall_coeffs = [], []
    messages = [None] * 3
    for stage in (3, 2, 1):
        ins = [core_id, mine, other, held(wide[stage]), held(tall[stage]), *held_rows, *held_cols]
        ins += [held(a) for a in wide_coeffs + tall_coeffs]
        outs = [pltpu.VMEM((256, COL_AT[stage + 1]), bf16), pltpu.VMEM((ROW_AT[stage], 512), bf16)]
        outs += [shape(512, width, dtype=bf16)] * 2
        if stage == 3:
            outs.append(shape(8, 128))
        got = call(
            functools.partial(far_grad_kernel, stage),
            "far_grad",
            ins,
            outs,
            limit=10,
            flops=2 * (256 * 3072 + 1536 * 512) * width,
        )
        wide_coeffs.insert(0, got[0])
        tall_coeffs.insert(0, got[1])
        if stage == 3:
            loss = got[4]
        ins = [core_id, got[2], core_swap(got[3])]
        if stage == 1:
            ins.append(loss)
        messages[stage - 1] = call(
            far_message_kernel, "far_message", ins, [shape(528 if stage == 1 else 512, width, dtype=bf16)]
        )[0]
    got = [flip_permute(messages[q], q + 2) for q in range(3)]
    bases, near_got, owns = [], [], []
    source = wide[0]
    for q in range(3):
        got_q = call(
            functools.partial(near_grad_kernel, q),
            "near_grad",
            [core_id, mine, other, held(source), *held_rows, *held_cols]
            + [held(a) for a in wide_coeffs + tall_coeffs]
            + messages,
            [shape(512, width), shape(512, width, dtype=bf16), shape(256, width)]
            + ([pltpu.VMEM((768, 1536), bf16)] if q == 0 else []),
            limit=10,
            flops=2 * (256 * 3072 + 1536 * 512) * width,
        )
        bases.append(got_q[0])
        near_got.append(core_swap(got_q[1]))
        owns.append(got_q[2])
        if q == 0:
            source = got_q[3]
    total, loss = call(far_sum_kernel, "far_sum", [core_id, *bases, *got, loss], [shape(1536, width), shape(8, 128)])
    low, *messages = call(
        near_sum_kernel,
        "near_sum",
        [core_id, total, *near_got, loss],
        [shape(768, width)] + [shape(272 if q == 0 else 256, width, dtype=bf16) for q in range(3)],
    )
    got = [flip_permute(messages[q], q + 1) for q in range(3)]
    low, *messages, loss = call(
        half_sum_kernel,
        "half_sum",
        [core_id, low, *got, loss],
        [shape(384, width)] + [shape(144 if q == 0 else 128, width, dtype=bf16) for q in range(3)] + [shape(8, 128)],
    )
    got = [flip_permute(messages[q], q) for q in range(3)]
    keep, send = call(
        last_sum_kernel, "last_sum", [core_id, low, *got, *owns, loss], [shape(392, width), shape(392, width)]
    )
    grad_image, grad_text, loss = call(
        functools.partial(finish_kernel, count),
        "finish",
        [core_id, keep, core_swap(send)],
        [shape(192, width), shape(192, width), shape(1, 1)],
    )
    return loss.reshape(()), grad_image, grad_text


def solution(mesh):
    fine = Mesh(mesh.devices.reshape(4, 4, 4, 2), AXES)
    return jax.shard_map(
        per_device,
        mesh=fine,
        in_specs=(P(AXES, None), P(AXES, None)),
        out_specs=(P(), P(AXES, None), P(AXES, None)),
        check_vma=False,
    )
```

```python
import functools
import itertools
import math

import jax
import jax.numpy as jnp
from jax import lax
from jax.experimental import pallas as pl
from jax.experimental.pallas import tpu as pltpu
from jax.sharding import Mesh, PartitionSpec as P


logit_scale = 10.0
log2e = 1.4426950408889634
ln2 = 0.6931471805599453
lowest = -1e30
f32 = jnp.float32
bf16 = jnp.bfloat16
AXES = ("z", "y", "x", "c")
SWAP = ((0, 1), (1, 0))
FLIPS = ((0, 0, 1), (0, 1, 0), (1, 0, 0))
IMAGE_PAIR = (1, 0, 3, 2)
TEXT_PAIR = (3, 2, 1, 0)
VMEM = pl.BlockSpec(memory_space=pltpu.VMEM)
SMEM = pl.BlockSpec(memory_space=pltpu.SMEM)


def role_pairs(flip):
    pairs = []
    for z, y, x in itertools.product(range(4), repeat=3):
        for core, pair in ((0, IMAGE_PAIR), (1, TEXT_PAIR)):
            target = [pair[v] if f else v for v, f in zip((z, y, x), flip)]
            source_id = ((z * 4 + y) * 4 + x) * 2 + core
            target_id = ((target[0] * 4 + target[1]) * 4 + target[2]) * 2 + core
            pairs.append((source_id, target_id))
    return pairs


ROLE_PAIRS = [role_pairs(flip) for flip in FLIPS]


def flip_permute(x, dim):
    return lax.ppermute(x, AXES, ROLE_PAIRS[dim % 3])


def core_swap(x):
    return lax.ppermute(x, "c", SWAP)


def call(kernel, name, ins, outs, scratch=(), limit=6, flops=0, moved=0):
    in_specs = [SMEM if i == 0 else VMEM for i in range(len(ins))]
    return pl.pallas_call(
        kernel,
        in_specs=in_specs,
        out_specs=[VMEM] * len(outs),
        out_shape=list(outs),
        scratch_shapes=list(scratch),
        compiler_params=pltpu.CompilerParams(vmem_limit_bytes=limit << 20),
        cost_estimate=pl.CostEstimate(flops=flops, bytes_accessed=moved, transcendentals=0),
        name=name,
    )(*ins)


def held(x):
    return pltpu.with_memory_space_constraint(x, pltpu.VMEM)


def shape(*dims, dtype=f32):
    return jax.ShapeDtypeStruct(dims, dtype)


CONTRACT_LAST = (((1,), (1,)), ((), ()))
CONTRACT_FIRST = (((0,), (0,)), ((), ()))


def log_add(a, b):
    top = jnp.maximum(a, b)
    return top + jnp.log2(jnp.exp2(a - top) + jnp.exp2(b - top))


def lane_blocks(x):
    return [x[:, k : k + 128] for k in range(0, x.shape[1], 128)]


def row_stat(logits):
    top = jnp.max(logits, axis=1, keepdims=True)
    total = jnp.sum(jnp.exp2(logits - top), axis=1, keepdims=True)
    lse = top + jnp.log2(total)
    return jnp.concatenate(lane_blocks(jnp.broadcast_to(lse, (lse.shape[0], 128)).T[0:1, :]), 0)


def column_step(logits, state):
    top = jnp.max(logits, axis=0, keepdims=True)
    if state is None:
        return top, jnp.sum(jnp.exp2(logits - top), axis=0, keepdims=True)
    new_top = jnp.maximum(state[0], top)
    total = state[1] * jnp.exp2(state[0] - new_top) + jnp.sum(jnp.exp2(logits - new_top), axis=0, keepdims=True)
    return new_top, total


def column_stat(state):
    return jnp.concatenate(lane_blocks(state[0] + jnp.log2(state[1])), 0)


def product(a, b):
    return lax.dot_general(a, b, CONTRACT_LAST, preferred_element_type=f32) * (logit_scale * log2e)


def place(first, mine, swapped, rows_ref, cols_ref):
    @pl.when(first)
    def _():
        for q in range(3):
            rows_ref[q * 256 : q * 256 + 256, :] = mine[q][0:256, :]
            cols_ref[q * 512 : q * 512 + 512, :] = swapped[q][...]

    @pl.when(jnp.logical_not(first))
    def _():
        for q in range(3):
            rows_ref[q * 256 : q * 256 + 256, :] = swapped[q][256:512, :]
            cols_ref[q * 512 : q * 512 + 512, :] = mine[q][...]


def near_kernel(core_ref, m0, m1, m2, packed_ref, rows_ref, cols_ref, logit_ref, row_out, col_out):
    swapped = [packed_ref.at[q * 512 : q * 512 + 512] for q in range(3)]
    place(core_ref[0] == 0, (m0, m1, m2), swapped, rows_ref, cols_ref)
    rows, state = [], None
    for q in range(3):
        part = slice(q * 256, q * 256 + 256)
        logit_ref[part, :] = product(rows_ref[part, :], cols_ref[...])
        logits = logit_ref[part, :]
        rows.append(row_stat(logits))
        state = column_step(logits, state)
    row_out[...] = jnp.concatenate(rows, 0)
    col_out[...] = column_stat(state)


def far_kernel(core_ref, *refs):
    mine, swapped = refs[0:3], refs[3:6]
    near_rows, near_cols, row_old, col_old, image_ref, text_ref = refs[6:12]
    rows_ref, cols_ref, *wide_refs = refs[12:17]
    tall_ref, send_ref, keep_ref = refs[17:20]
    first = core_ref[0] == 0
    place(first, mine, swapped, rows_ref, cols_ref)
    new, state = [], None
    for q, wide in enumerate(wide_refs):
        part = slice(q * 256, q * 256 + 256)
        wide[:, 0:1536] = product(rows_ref[part, :], near_cols[...])
        wide[:, 1536:3072] = product(rows_ref[part, :], cols_ref[...])
        logits = wide[...]
        new.append(row_stat(logits))
        state = column_step(logits, state)
    old, tall_state = [], None
    for q in range(3):
        part = slice(q * 256, q * 256 + 256)
        tall_ref[part, :] = product(near_rows[part, :], cols_ref[...])
        logits = tall_ref[part, :]
        old.append(row_stat(logits))
        tall_state = column_step(logits, tall_state)
    row = jnp.concatenate([log_add(row_old[...], jnp.concatenate(old, 0))] + new, 0)
    col = log_add(column_stat(state), jnp.concatenate([col_old[...], column_stat(tall_state)], 0))
    positive = logit_scale * jnp.sum(image_ref[...].astype(f32) * text_ref[...].astype(f32))
    extra = jnp.full((8, 128), positive, f32)
    blank = jnp.full((2, 128), lowest, f32)
    low_half = jnp.concatenate([x for g in range(6) for x in (row[2 * g : 2 * g + 2], blank)], 0)
    high_half = jnp.concatenate([x for g in range(6) for x in (blank, row[2 * g : 2 * g + 2])], 0)
    send_ref[0:24, :] = jnp.where(first, col, high_half)
    keep_ref[0:24, :] = jnp.where(first, low_half, col)
    send_ref[24:32, :] = extra
    keep_ref[24:32, :] = extra


def stack_kernel(core_ref, *refs):
    packed = len(refs) == 10
    for q in range(3):
        a, b, out = refs[q], refs[q + 3], refs[q + 6]
        rows = a.shape[0]
        out[0:rows, :] = a[...]
        out[rows : 2 * rows, :] = b[...]
        if packed:
            refs[9][q * 512 : q * 512 + rows, :] = a[...]
            refs[9][q * 512 + rows : q * 512 + 512, :] = b[...]


def gate_kernel(value_ref, token_ref, out_ref):
    pass


def after(value, token):
    return pl.pallas_call(
        gate_kernel,
        in_specs=[VMEM, VMEM],
        out_specs=VMEM,
        out_shape=pltpu.VMEM(value.shape, value.dtype),
        input_output_aliases={0: 0},
        compiler_params=pltpu.CompilerParams(vmem_limit_bytes=1 << 20),
        name="after",
    )(held(value), token)


def join_kernel(order, core_ref, mine_ref, got_ref, out_ref):
    got = got_ref[...]
    out_ref[0:24, :] = log_add(mine_ref[0:24, :], jnp.concatenate([got[k : k + 1, :] for k in order], 0))
    out_ref[24:32, :] = mine_ref[24:32, :] + got_ref[24:32, :]


def flip_order(dim):
    order = []
    for half, q, k in itertools.product(range(2), range(3), range(4)):
        j = (dim - q) % 3
        if j == 2:
            order.append((1 - half) * 12 + q * 4 + k)
        else:
            order.append(half * 12 + q * 4 + (k ^ (1 << j)))
    return order


def tile_lse(first, mine_ref, other_ref):
    mine, other = mine_ref[0:24, :], other_ref[0:24, :]
    row = jnp.where(first, mine, other)
    col = jnp.where(first, other, mine)
    row = [jnp.where(first, row[4 * g + b : 4 * g + b + 1], row[4 * g + b + 2 : 4 * g + b + 3]) for g in range(6) for b in range(2)]
    row = jnp.concatenate(row, 1) + 1.0
    col = jnp.concatenate([col[k : k + 1] for k in range(24)], 1) + 1.0
    return row, col


def coefficients(logits, row, col):
    n = logits.shape[0]
    row = jnp.broadcast_to(row, (128, n)).T[:, 0:1]
    return jnp.exp2(logits - row) + jnp.exp2(logits - col)


def total_of(terms):
    total = terms[0]
    for term in terms[1:]:
        total = total + term
    return logit_scale * total


def times(a, b):
    return jnp.dot(a, b, preferred_element_type=f32)


def transposed_times(a, b):
    return lax.dot_general(a, b, CONTRACT_FIRST, preferred_element_type=f32)


def coeff_kernel(core_ref, mine_ref, other_ref, *refs):
    near_ref, tall_ref, *wide_refs = refs[0:5]
    near_cols, far_cols = refs[5:7]
    coeff_ref, *grad_refs = refs[7:14]
    own_ref, loss_ref = refs[14:16]
    first = core_ref[0] == 0
    row, col = tile_lse(first, mine_ref, other_ref)
    loss_ref[...] = jnp.sum(other_ref[0:24, :]) * ln2 - jnp.where(first, 0.0, 2.0) * other_ref[24:32, :]
    eye = lax.broadcasted_iota(jnp.int32, (128, 128), 0) == lax.broadcasted_iota(jnp.int32, (128, 128), 1)
    positive = jnp.where(jnp.logical_and(eye, first), 1.0, 0.0)
    for g in range(6):
        part = slice(g * 256, g * 256 + 256)
        if g < 3:
            coeffs = coefficients(near_ref[part, :], row[:, part], col[:, 0:1536])
            coeff_ref[part, 0:1536] = coeffs.astype(bf16)
            own = slice(g * 512, g * 512 + 128)
            coeff_ref[g * 256 : g * 256 + 128, own] = (coeffs[0:128, own] - positive).astype(bf16)
            coeff_ref[part, 1536:3072] = coefficients(tall_ref[part, :], row[:, part], col[:, 1536:3072]).astype(bf16)
        else:
            coeff_ref[part, :] = coefficients(wide_refs[g - 3][...], row[:, part], col).astype(bf16)
        grad = total_of(
            [times(coeff_ref[part, 0:1536], near_cols[...]), times(coeff_ref[part, 1536:3072], far_cols[...])]
        )
        grad_refs[g][...] = grad.astype(bf16)
        if g < 3:
            own_ref[g * 128 : g * 128 + 128, :] = grad[0:128, :]


def text_grad(coeff_ref, near_rows, far_rows, start):
    here = slice(start, start + 512)
    return total_of(
        [
            transposed_times(coeff_ref[0:768, here], near_rows[...]),
            transposed_times(coeff_ref[768:1536, here], far_rows[...]),
        ]
    )


def far_text_kernel(q, core_ref, coeff_ref, near_rows, far_rows, image_ref, kept_ref, send_ref):
    first = core_ref[0] == 0
    text = text_grad(coeff_ref, near_rows, far_rows, 1536 + q * 512).astype(bf16)
    image = image_ref[...]
    kept_ref[0:256, :] = jnp.where(first, image, text[0:256])
    send_ref[0:256, :] = jnp.where(first, text[0:256], image)
    kept_ref[256:512, :] = text[256:512]
    send_ref[256:512, :] = text[256:512]


def near_text_kernel(q, core_ref, coeff_ref, near_rows, far_rows, image_ref, own_image, a0, a1, a2, base_ref, send_ref, own_ref):
    first = core_ref[0] == 0
    text = text_grad(coeff_ref, near_rows, far_rows, q * 512)
    image = image_ref[...].astype(f32)
    own_ref[0:128, :] = own_image[q * 128 : q * 128 + 128, :]
    own_ref[128:256, :] = text[0:128]
    base_ref[0:128, :] = jnp.where(first, 0.0, text[0:128])
    base_ref[128:256, :] = jnp.where(first, image[128:256], text[128:256])
    base_ref[256:512, :] = jnp.where(first, 0.0, text[256:512])
    send_ref[0:128, :] = jnp.where(first, 0.0, image[0:128]).astype(bf16)
    send_ref[128:256, :] = jnp.where(first, text[128:256], image[128:256]).astype(bf16)
    send_ref[256:512, :] = text[256:512].astype(bf16)


def split_terms(x):
    high = x.astype(bf16)
    rest = x - high.astype(f32)
    middle = rest.astype(bf16)
    low = (rest - middle.astype(f32)).astype(bf16)
    pair = [jnp.concatenate([t, t], 0) for t in (high, middle, low)]
    return jnp.concatenate(pair + [jnp.zeros((16, 128), bf16)], 1)


def join_terms(ref, start):
    x = ref[start : start + 16, :].astype(f32)
    return (x[0:8, 0:128] + x[0:8, 128:256]) + x[0:8, 256:384]


def far_message_kernel(core_ref, mine_ref, got_ref, *refs):
    first = core_ref[0] == 0
    got = got_ref[...]
    both = (mine_ref[...].astype(f32) + got.astype(f32)).astype(bf16)
    refs[-1][0:256, :] = jnp.where(first, mine_ref[0:256, :], both[0:256])
    refs[-1][256:512, :] = jnp.where(first, got[0:256], both[256:512])
    if len(refs) == 2:
        refs[-1][512:528, :] = split_terms(refs[0][...])


def far_sum_kernel(core_ref, b0, b1, b2, r0, r1, r2, loss_ref, total_ref, loss_out):
    loss_out[...] = loss_ref[...] + join_terms(r0, 512)
    for q, (b, r) in enumerate(((b0, r0), (b1, r1), (b2, r2))):
        total_ref[q * 512 : q * 512 + 512, :] = b[...] + r[0:512, :].astype(f32)


def near_sum_kernel(core_ref, total_ref, g0, g1, g2, loss_ref, low_ref, s0, s1, s2):
    first = core_ref[0] == 0
    s0[256:272, :] = split_terms(loss_ref[...])
    for q, (g, s) in enumerate(((g0, s0), (g1, s1), (g2, s2))):
        at = q * 512
        got = g[...].astype(f32)
        low_ref[q * 256 : q * 256 + 256, :] = total_ref[at : at + 256, :] + jnp.where(first, 0.0, got[0:256])
        s[0:256, :] = (total_ref[at + 256 : at + 512, :] + jnp.where(first, got[0:256], got[256:512])).astype(bf16)


def half_sum_kernel(core_ref, low_ref, r0, r1, r2, loss_ref, out_ref, s0, s1, s2, loss_out):
    loss = loss_ref[...] + join_terms(r0, 256)
    loss_out[...] = loss
    s0[128:144, :] = split_terms(loss)
    for q, (r, s) in enumerate(((r0, s0), (r1, s1), (r2, s2))):
        total = low_ref[q * 256 : q * 256 + 256, :] + r[0:256, :].astype(f32)
        out_ref[q * 128 : q * 128 + 128, :] = total[0:128]
        s[0:128, :] = total[128:256].astype(bf16)


def last_sum_kernel(core_ref, low_ref, r0, r1, r2, o0, o1, o2, loss_ref, keep_ref, send_ref):
    first = core_ref[0] == 0
    loss = loss_ref[...] + join_terms(r0, 128)
    keep_ref[384:392, :] = jnp.concatenate([loss] * 4, 1)
    send_ref[384:392, :] = jnp.concatenate([loss] * 4, 1)
    for q, (r, own) in enumerate(((r0, o0), (r1, o1), (r2, o2))):
        rows, text_rows = slice(q * 64, q * 64 + 64), slice(192 + q * 64, 192 + q * 64 + 64)
        total = low_ref[q * 128 : q * 128 + 128, :] + r[0:128, :].astype(f32)
        keep_ref[rows, :] = jnp.where(first, total[0:64] + own[0:64, :], total[64:128])
        keep_ref[text_rows, :] = own[128:192, :]
        send_ref[rows, :] = jnp.where(first, total[64:128] + own[64:128, :], total[0:64])
        send_ref[text_rows, :] = own[192:256, :]


def finish_kernel(count, core_ref, keep_ref, got_ref, image_out, text_out, loss_out):
    first = core_ref[0] == 0
    image_out[...] = jnp.where(first, keep_ref[0:192, :], got_ref[0:192, :])
    text_out[...] = jnp.where(
        first, got_ref[0:192, :] + keep_ref[192:384, :], keep_ref[0:192, :] + got_ref[192:384, :]
    )
    loss_out[...] = (keep_ref[384:385, 0:1] + got_ref[384:385, 0:1]) * (0.5 / count)


def pair_kernel(core_ref, image_hbm, text_hbm, image_got, text_got, o0, o1, o2, image_ref, text_ref, sems):
    copies = [
        pltpu.make_async_copy(image_hbm, image_ref, sems.at[0]),
        pltpu.make_async_copy(text_hbm, text_ref, sems.at[1]),
    ]
    for copy in copies:
        copy.start()
    for copy in copies:
        copy.wait()
    first = core_ref[0] == 0
    for q, out in enumerate((o0, o1, o2)):
        rows = slice(q * 64, q * 64 + 64)
        out[0:64, :] = jnp.where(first, image_ref[rows, :], text_got[rows, :])
        out[64:128, :] = jnp.where(first, image_got[rows, :], text_ref[rows, :])


def pair(core_id, image_emb, text_emb, image_got, text_got):
    rows, width = image_emb.shape
    anywhere = pl.BlockSpec(memory_space=pl.ANY)
    return pl.pallas_call(
        pair_kernel,
        in_specs=[SMEM, anywhere, anywhere, VMEM, VMEM],
        out_specs=[VMEM] * 3,
        out_shape=[shape(128, width, dtype=bf16)] * 3,
        scratch_shapes=[pltpu.VMEM((rows, width), bf16)] * 2 + [pltpu.SemaphoreType.DMA((2,))],
        compiler_params=pltpu.CompilerParams(vmem_limit_bytes=4 << 20),
        name="pair",
    )(
        core_id,
        pltpu.with_memory_space_constraint(image_emb, pltpu.HBM),
        pltpu.with_memory_space_constraint(text_emb, pltpu.HBM),
        image_got,
        text_got,
    )


def per_device(image_emb, text_emb):
    core_id = lax.axis_index("c").reshape(1).astype(jnp.int32)
    pair_rows, width = image_emb.shape
    count = pair_rows * 128

    got = [core_swap(image_emb), core_swap(text_emb)]
    near = pair(core_id, image_emb, text_emb, *got)
    for step in range(2):
        got = [flip_permute(near[q], q + step) for q in range(3)]
        outs = [shape(256 << step, width, dtype=bf16)] * 3 + [shape(1536, width, dtype=bf16)] * step
        near = call(stack_kernel, "stack", [core_id, *near, *got], outs, limit=2)
    *near, packed = near
    near_x = [core_swap(packed)]
    far = [flip_permute(near[q], q + 2) for q in range(3)]

    near_rows, near_cols, near_logits, row, col = call(
        near_kernel,
        "near",
        [core_id, *near, *near_x],
        [pltpu.VMEM((768, width), bf16), pltpu.VMEM((1536, width), bf16), pltpu.VMEM((768, 1536), f32)]
        + [shape(6, 128), shape(12, 128)],
        limit=10,
        flops=2 * 768 * 1536 * width,
    )
    far = [after(a, row) for a in far]
    far_x = [core_swap(a) for a in far]
    far_rows, far_cols, *logits, send, keep = call(
        far_kernel,
        "far",
        [core_id, *far, *far_x, held(near_rows), held(near_cols), row, col, image_emb, text_emb],
        [pltpu.VMEM((768, width), bf16), pltpu.VMEM((1536, width), bf16)]
        + [pltpu.VMEM((256, 3072), f32)] * 3
        + [pltpu.VMEM((768, 1536), f32), shape(32, 128), shape(32, 128)],
        limit=10,
        flops=2 * 768 * 4608 * width,
    )
    *wide_logits, tall_logits = logits

    mine = call(functools.partial(join_kernel, list(range(24))), "join", [core_id, keep, core_swap(send)], [shape(32, 128)], limit=2)[0]
    for dim in range(3):
        got = flip_permute(mine, dim)
        mine = call(functools.partial(join_kernel, flip_order(dim)), "join", [core_id, mine, got], [shape(32, 128)], limit=2)[0]
    other = core_swap(mine)

    held_rows = [held(near_rows), held(far_rows)]
    coeffs, *image_grads, own_image, loss = call(
        coeff_kernel,
        "coeffs",
        [core_id, mine, other]
        + [held(a) for a in (near_logits, tall_logits, *wide_logits, near_cols, far_cols)],
        [pltpu.VMEM((1536, 3072), bf16)] + [shape(256, width, dtype=bf16)] * 6 + [shape(384, width), shape(8, 128)],
        limit=10,
        flops=2 * 1536 * 3072 * width,
    )
    messages = []
    for q in range(3):
        kept, send = call(
            functools.partial(far_text_kernel, q),
            "far_text",
            [core_id, held(coeffs), *held_rows, image_grads[3 + q]],
            [shape(512, width, dtype=bf16)] * 2,
            limit=6,
            flops=2 * 1536 * 512 * width,
        )
        ins = [core_id, kept, core_swap(send)] + ([loss] if q == 0 else [])
        outs = [shape(528 if q == 0 else 512, width, dtype=bf16)]
        messages.append(call(far_message_kernel, "far_message", ins, outs)[0])
    got = [flip_permute(messages[q], q + 2) for q in range(3)]
    bases, near_got, owns = [], [], []
    for q in range(3):
        base, send, own = call(
            functools.partial(near_text_kernel, q),
            "near_text",
            [core_id, held(coeffs), *held_rows, image_grads[q], own_image, *messages],
            [shape(512, width), shape(512, width, dtype=bf16), shape(256, width)],
            limit=6,
            flops=2 * 1536 * 512 * width,
        )
        bases.append(base)
        near_got.append(core_swap(send))
        owns.append(own)
    total, loss = call(far_sum_kernel, "far_sum", [core_id, *bases, *got, loss], [shape(1536, width), shape(8, 128)])
    low, *messages = call(
        near_sum_kernel,
        "near_sum",
        [core_id, total, *near_got, loss],
        [shape(768, width)] + [shape(272 if q == 0 else 256, width, dtype=bf16) for q in range(3)],
    )
    got = [flip_permute(messages[q], q + 1) for q in range(3)]
    low, *messages, loss = call(
        half_sum_kernel,
        "half_sum",
        [core_id, low, *got, loss],
        [shape(384, width)] + [shape(144 if q == 0 else 128, width, dtype=bf16) for q in range(3)] + [shape(8, 128)],
    )
    got = [flip_permute(messages[q], q) for q in range(3)]
    keep, send = call(
        last_sum_kernel, "last_sum", [core_id, low, *got, *owns, loss], [shape(392, width), shape(392, width)]
    )
    grad_image, grad_text, loss = call(
        functools.partial(finish_kernel, count),
        "finish",
        [core_id, keep, core_swap(send)],
        [shape(192, width), shape(192, width), shape(1, 1)],
    )
    return loss.reshape(()), grad_image, grad_text


def solution(mesh):
    fine = Mesh(mesh.devices.reshape(4, 4, 4, 2), AXES)
    return jax.shard_map(
        per_device,
        mesh=fine,
        in_specs=(P(AXES, None), P(AXES, None)),
        out_specs=(P(), P(AXES, None), P(AXES, None)),
        check_vma=False,
    )
```

```python
import functools
import itertools
import math

import jax
import jax.numpy as jnp
from jax import lax
from jax.experimental import pallas as pl
from jax.experimental.pallas import tpu as pltpu
from jax.sharding import Mesh, PartitionSpec as P


logit_scale = 10.0
log2e = 1.4426950408889634
ln2 = 0.6931471805599453
lowest = -1e30
f32 = jnp.float32
bf16 = jnp.bfloat16
AXES = ("z", "y", "x", "c")
SWAP = ((0, 1), (1, 0))
FLIPS = ((0, 0, 1), (0, 1, 0), (1, 0, 0))
INNER, OUTER = (1, 0, 3, 2), (3, 2, 1, 0)
IMAGE_PAIRS = (INNER, OUTER, INNER)
TEXT_PAIRS = (OUTER, INNER, OUTER)
VMEM = pl.BlockSpec(memory_space=pltpu.VMEM)
SMEM = pl.BlockSpec(memory_space=pltpu.SMEM)


def role_pairs(flip):
    pairs = []
    for z, y, x in itertools.product(range(4), repeat=3):
        for core, pairs_of in ((0, IMAGE_PAIRS), (1, TEXT_PAIRS)):
            target = [pair[v] if f else v for v, f, pair in zip((z, y, x), flip, pairs_of)]
            source_id = ((z * 4 + y) * 4 + x) * 2 + core
            target_id = ((target[0] * 4 + target[1]) * 4 + target[2]) * 2 + core
            pairs.append((source_id, target_id))
    return pairs


ROLE_PAIRS = [role_pairs(flip) for flip in FLIPS]


def flip_permute(x, dim):
    return lax.ppermute(x, AXES, ROLE_PAIRS[dim % 3])


def core_swap(x):
    return lax.ppermute(x, "c", SWAP)


def call(kernel, name, ins, outs, scratch=(), limit=6, flops=0, moved=0):
    in_specs = [SMEM if i == 0 else VMEM for i in range(len(ins))]
    return pl.pallas_call(
        kernel,
        in_specs=in_specs,
        out_specs=[VMEM] * len(outs),
        out_shape=list(outs),
        scratch_shapes=list(scratch),
        compiler_params=pltpu.CompilerParams(vmem_limit_bytes=limit << 20),
        cost_estimate=pl.CostEstimate(flops=flops, bytes_accessed=moved, transcendentals=0),
        name=name,
    )(*ins)


def held(x):
    return pltpu.with_memory_space_constraint(x, pltpu.VMEM)


def shape(*dims, dtype=f32):
    return jax.ShapeDtypeStruct(dims, dtype)


CONTRACT_LAST = (((1,), (1,)), ((), ()))
CONTRACT_FIRST = (((0,), (0,)), ((), ()))


def log_add(a, b):
    top = jnp.maximum(a, b)
    return top + jnp.log2(jnp.exp2(a - top) + jnp.exp2(b - top))


def lane_blocks(x):
    return [x[:, k : k + 128] for k in range(0, x.shape[1], 128)]


def row_stat(logits):
    top = jnp.max(logits, axis=1, keepdims=True)
    total = jnp.sum(jnp.exp2(logits - top), axis=1, keepdims=True)
    lse = top + jnp.log2(total)
    return jnp.concatenate(lane_blocks(jnp.broadcast_to(lse, (lse.shape[0], 128)).T[0:1, :]), 0)


def column_step(logits, state):
    top = jnp.max(logits, axis=0, keepdims=True)
    if state is None:
        return top, jnp.sum(jnp.exp2(logits - top), axis=0, keepdims=True)
    new_top = jnp.maximum(state[0], top)
    total = state[1] * jnp.exp2(state[0] - new_top) + jnp.sum(jnp.exp2(logits - new_top), axis=0, keepdims=True)
    return new_top, total


def column_stat(state):
    return jnp.concatenate(lane_blocks(state[0] + jnp.log2(state[1])), 0)


def product(a, b):
    return lax.dot_general(a, b, CONTRACT_LAST, preferred_element_type=f32) * (logit_scale * log2e)


def place(first, mine, swapped, rows_ref, cols_ref):
    @pl.when(first)
    def _():
        for q in range(3):
            rows_ref[q * 256 : q * 256 + 256, :] = mine[q][0:256, :]
            cols_ref[q * 512 : q * 512 + 512, :] = swapped[q][...]

    @pl.when(jnp.logical_not(first))
    def _():
        for q in range(3):
            rows_ref[q * 256 : q * 256 + 256, :] = swapped[q][256:512, :]
            cols_ref[q * 512 : q * 512 + 512, :] = mine[q][...]


def near_kernel(core_ref, m0, m1, m2, packed_ref, rows_ref, cols_ref, logit_ref, row_out, col_out):
    swapped = [packed_ref.at[q * 512 : q * 512 + 512] for q in range(3)]
    place(core_ref[0] == 0, (m0, m1, m2), swapped, rows_ref, cols_ref)
    rows, state = [], None
    for q in range(3):
        part = slice(q * 256, q * 256 + 256)
        logit_ref[part, :] = product(rows_ref[part, :], cols_ref[...])
        logits = logit_ref[part, :]
        rows.append(row_stat(logits))
        state = column_step(logits, state)
    row_out[...] = jnp.concatenate(rows, 0)
    col_out[...] = column_stat(state)


def far_kernel(core_ref, *refs):
    mine, swapped = refs[0:3], refs[3:6]
    near_rows, near_cols, row_old, col_old, image_ref, text_ref = refs[6:12]
    rows_ref, cols_ref, *wide_refs = refs[12:17]
    tall_ref, send_ref, keep_ref = refs[17:20]
    first = core_ref[0] == 0
    place(first, mine, swapped, rows_ref, cols_ref)
    new, state = [], None
    for q, wide in enumerate(wide_refs):
        part = slice(q * 256, q * 256 + 256)
        wide[:, 0:1536] = product(rows_ref[part, :], near_cols[...])
        wide[:, 1536:3072] = product(rows_ref[part, :], cols_ref[...])
        logits = wide[...]
        new.append(row_stat(logits))
        state = column_step(logits, state)
    old, tall_state = [], None
    for q in range(3):
        part = slice(q * 256, q * 256 + 256)
        tall_ref[part, :] = product(near_rows[part, :], cols_ref[...])
        logits = tall_ref[part, :]
        old.append(row_stat(logits))
        tall_state = column_step(logits, tall_state)
    row = jnp.concatenate([log_add(row_old[...], jnp.concatenate(old, 0))] + new, 0)
    col = log_add(column_stat(state), jnp.concatenate([col_old[...], column_stat(tall_state)], 0))
    positive = logit_scale * jnp.sum(image_ref[...].astype(f32) * text_ref[...].astype(f32))
    extra = jnp.full((8, 128), positive, f32)
    blank = jnp.full((2, 128), lowest, f32)
    low_half = jnp.concatenate([x for g in range(6) for x in (row[2 * g : 2 * g + 2], blank)], 0)
    high_half = jnp.concatenate([x for g in range(6) for x in (blank, row[2 * g : 2 * g + 2])], 0)
    send_ref[0:24, :] = jnp.where(first, col, high_half)
    keep_ref[0:24, :] = jnp.where(first, low_half, col)
    send_ref[24:32, :] = extra
    keep_ref[24:32, :] = extra


def stack_kernel(core_ref, *refs):
    packed = len(refs) == 10
    for q in range(3):
        a, b, out = refs[q], refs[q + 3], refs[q + 6]
        rows = a.shape[0]
        out[0:rows, :] = a[...]
        out[rows : 2 * rows, :] = b[...]
        if packed:
            refs[9][q * 512 : q * 512 + rows, :] = a[...]
            refs[9][q * 512 + rows : q * 512 + 512, :] = b[...]


def gate_kernel(value_ref, token_ref, out_ref):
    pass


def after(value, token):
    return pl.pallas_call(
        gate_kernel,
        in_specs=[VMEM, VMEM],
        out_specs=VMEM,
        out_shape=pltpu.VMEM(value.shape, value.dtype),
        input_output_aliases={0: 0},
        compiler_params=pltpu.CompilerParams(vmem_limit_bytes=1 << 20),
        name="after",
    )(held(value), token)


def join_kernel(order, core_ref, mine_ref, got_ref, out_ref):
    got = got_ref[...]
    out_ref[0:24, :] = log_add(mine_ref[0:24, :], jnp.concatenate([got[k : k + 1, :] for k in order], 0))
    out_ref[24:32, :] = mine_ref[24:32, :] + got_ref[24:32, :]


def flip_order(dim):
    order = []
    for half, q, k in itertools.product(range(2), range(3), range(4)):
        j = (dim - q) % 3
        if j == 2:
            order.append((1 - half) * 12 + q * 4 + k)
        else:
            order.append(half * 12 + q * 4 + (k ^ (1 << j)))
    return order


def tile_lse(first, mine_ref, other_ref):
    mine, other = mine_ref[0:24, :], other_ref[0:24, :]
    row = jnp.where(first, mine, other)
    col = jnp.where(first, other, mine)
    row = [jnp.where(first, row[4 * g + b : 4 * g + b + 1], row[4 * g + b + 2 : 4 * g + b + 3]) for g in range(6) for b in range(2)]
    row = jnp.concatenate(row, 1) + 1.0
    col = jnp.concatenate([col[k : k + 1] for k in range(24)], 1) + 1.0
    return row, col


def coefficients(logits, row, col):
    n = logits.shape[0]
    row = jnp.broadcast_to(row, (128, n)).T[:, 0:1]
    return jnp.exp2(logits - row) + jnp.exp2(logits - col)


def total_of(terms):
    total = terms[0]
    for term in terms[1:]:
        total = total + term
    return logit_scale * total


def times(a, b):
    return jnp.dot(a, b, preferred_element_type=f32)


def transposed_times(a, b):
    return lax.dot_general(a, b, CONTRACT_FIRST, preferred_element_type=f32)


def coeff_kernel(core_ref, mine_ref, other_ref, *refs):
    near_ref, tall_ref, *wide_refs = refs[0:5]
    near_cols, far_cols = refs[5:7]
    coeff_ref, *grad_refs = refs[7:14]
    own_ref, loss_ref = refs[14:16]
    first = core_ref[0] == 0
    row, col = tile_lse(first, mine_ref, other_ref)
    loss_ref[...] = jnp.sum(other_ref[0:24, :]) * ln2 - jnp.where(first, 0.0, 2.0) * other_ref[24:32, :]
    eye = lax.broadcasted_iota(jnp.int32, (128, 128), 0) == lax.broadcasted_iota(jnp.int32, (128, 128), 1)
    positive = jnp.where(jnp.logical_and(eye, first), 1.0, 0.0)
    for g in range(6):
        part = slice(g * 256, g * 256 + 256)
        if g < 3:
            coeffs = coefficients(near_ref[part, :], row[:, part], col[:, 0:1536])
            coeff_ref[part, 0:1536] = coeffs.astype(bf16)
            own = slice(g * 512, g * 512 + 128)
            coeff_ref[g * 256 : g * 256 + 128, own] = (coeffs[0:128, own] - positive).astype(bf16)
            coeff_ref[part, 1536:3072] = coefficients(tall_ref[part, :], row[:, part], col[:, 1536:3072]).astype(bf16)
        else:
            coeff_ref[part, :] = coefficients(wide_refs[g - 3][...], row[:, part], col).astype(bf16)
        grad = total_of(
            [times(coeff_ref[part, 0:1536], near_cols[...]), times(coeff_ref[part, 1536:3072], far_cols[...])]
        )
        grad_refs[g][...] = grad.astype(bf16)
        if g < 3:
            own_ref[g * 128 : g * 128 + 128, :] = grad[0:128, :]


def text_grad(coeff_ref, near_rows, far_rows, start):
    here = slice(start, start + 512)
    return total_of(
        [
            transposed_times(coeff_ref[0:768, here], near_rows[...]),
            transposed_times(coeff_ref[768:1536, here], far_rows[...]),
        ]
    )


def far_text_kernel(q, core_ref, coeff_ref, near_rows, far_rows, image_ref, kept_ref, send_ref):
    first = core_ref[0] == 0
    text = text_grad(coeff_ref, near_rows, far_rows, 1536 + q * 512).astype(bf16)
    image = image_ref[...]
    kept_ref[0:256, :] = jnp.where(first, image, text[0:256])
    send_ref[0:256, :] = jnp.where(first, text[0:256], image)
    kept_ref[256:512, :] = text[256:512]
    send_ref[256:512, :] = text[256:512]


def near_text_kernel(q, core_ref, coeff_ref, near_rows, far_rows, image_ref, own_image, a0, a1, a2, base_ref, send_ref, own_ref):
    first = core_ref[0] == 0
    text = text_grad(coeff_ref, near_rows, far_rows, q * 512)
    image = image_ref[...].astype(f32)
    own_ref[0:128, :] = own_image[q * 128 : q * 128 + 128, :]
    own_ref[128:256, :] = text[0:128]
    base_ref[0:128, :] = jnp.where(first, 0.0, text[0:128])
    base_ref[128:256, :] = jnp.where(first, image[128:256], text[128:256])
    base_ref[256:512, :] = jnp.where(first, 0.0, text[256:512])
    send_ref[0:128, :] = jnp.where(first, 0.0, image[0:128]).astype(bf16)
    send_ref[128:256, :] = jnp.where(first, text[128:256], image[128:256]).astype(bf16)
    send_ref[256:512, :] = text[256:512].astype(bf16)


def split_terms(x):
    high = x.astype(bf16)
    rest = x - high.astype(f32)
    middle = rest.astype(bf16)
    low = (rest - middle.astype(f32)).astype(bf16)
    pair = [jnp.concatenate([t, t], 0) for t in (high, middle, low)]
    return jnp.concatenate(pair + [jnp.zeros((16, 128), bf16)], 1)


def join_terms(ref, start):
    x = ref[start : start + 16, :].astype(f32)
    return (x[0:8, 0:128] + x[0:8, 128:256]) + x[0:8, 256:384]


def far_message_kernel(core_ref, mine_ref, got_ref, *refs):
    first = core_ref[0] == 0
    got = got_ref[...]
    both = (mine_ref[...].astype(f32) + got.astype(f32)).astype(bf16)
    refs[-1][0:256, :] = jnp.where(first, mine_ref[0:256, :], both[0:256])
    refs[-1][256:512, :] = jnp.where(first, got[0:256], both[256:512])
    if len(refs) == 2:
        refs[-1][512:528, :] = split_terms(refs[0][...])


def far_sum_kernel(core_ref, b0, b1, b2, r0, r1, r2, loss_ref, total_ref, loss_out):
    loss_out[...] = loss_ref[...] + join_terms(r0, 512)
    for q, (b, r) in enumerate(((b0, r0), (b1, r1), (b2, r2))):
        total_ref[q * 512 : q * 512 + 512, :] = b[...] + r[0:512, :].astype(f32)


def near_sum_kernel(core_ref, total_ref, g0, g1, g2, loss_ref, low_ref, s0, s1, s2):
    first = core_ref[0] == 0
    s0[256:272, :] = split_terms(loss_ref[...])
    for q, (g, s) in enumerate(((g0, s0), (g1, s1), (g2, s2))):
        at = q * 512
        got = g[...].astype(f32)
        low_ref[q * 256 : q * 256 + 256, :] = total_ref[at : at + 256, :] + jnp.where(first, 0.0, got[0:256])
        s[0:256, :] = (total_ref[at + 256 : at + 512, :] + jnp.where(first, got[0:256], got[256:512])).astype(bf16)


def half_sum_kernel(core_ref, low_ref, r0, r1, r2, loss_ref, out_ref, s0, s1, s2, loss_out):
    loss = loss_ref[...] + join_terms(r0, 256)
    loss_out[...] = loss
    s0[128:144, :] = split_terms(loss)
    for q, (r, s) in enumerate(((r0, s0), (r1, s1), (r2, s2))):
        total = low_ref[q * 256 : q * 256 + 256, :] + r[0:256, :].astype(f32)
        out_ref[q * 128 : q * 128 + 128, :] = total[0:128]
        s[0:128, :] = total[128:256].astype(bf16)


def last_sum_kernel(core_ref, low_ref, r0, r1, r2, o0, o1, o2, loss_ref, keep_ref, send_ref):
    first = core_ref[0] == 0
    loss = loss_ref[...] + join_terms(r0, 128)
    keep_ref[384:392, :] = jnp.concatenate([loss] * 4, 1)
    send_ref[384:392, :] = jnp.concatenate([loss] * 4, 1)
    for q, (r, own) in enumerate(((r0, o0), (r1, o1), (r2, o2))):
        rows, text_rows = slice(q * 64, q * 64 + 64), slice(192 + q * 64, 192 + q * 64 + 64)
        total = low_ref[q * 128 : q * 128 + 128, :] + r[0:128, :].astype(f32)
        keep_ref[rows, :] = jnp.where(first, total[0:64] + own[0:64, :], total[64:128])
        keep_ref[text_rows, :] = own[128:192, :]
        send_ref[rows, :] = jnp.where(first, total[64:128] + own[64:128, :], total[0:64])
        send_ref[text_rows, :] = own[192:256, :]


def finish_kernel(count, core_ref, keep_ref, got_ref, image_out, text_out, loss_out):
    first = core_ref[0] == 0
    image_out[...] = jnp.where(first, keep_ref[0:192, :], got_ref[0:192, :])
    text_out[...] = jnp.where(
        first, got_ref[0:192, :] + keep_ref[192:384, :], keep_ref[0:192, :] + got_ref[192:384, :]
    )
    loss_out[...] = (keep_ref[384:385, 0:1] + got_ref[384:385, 0:1]) * (0.5 / count)


def pair_kernel(core_ref, image_hbm, text_hbm, image_got, text_got, o0, o1, o2, image_ref, text_ref, sems):
    copies = [
        pltpu.make_async_copy(image_hbm, image_ref, sems.at[0]),
        pltpu.make_async_copy(text_hbm, text_ref, sems.at[1]),
    ]
    for copy in copies:
        copy.start()
    for copy in copies:
        copy.wait()
    first = core_ref[0] == 0
    for q, out in enumerate((o0, o1, o2)):
        rows = slice(q * 64, q * 64 + 64)
        out[0:64, :] = jnp.where(first, image_ref[rows, :], text_got[rows, :])
        out[64:128, :] = jnp.where(first, image_got[rows, :], text_ref[rows, :])


def pair(core_id, image_emb, text_emb, image_got, text_got):
    rows, width = image_emb.shape
    anywhere = pl.BlockSpec(memory_space=pl.ANY)
    return pl.pallas_call(
        pair_kernel,
        in_specs=[SMEM, anywhere, anywhere, VMEM, VMEM],
        out_specs=[VMEM] * 3,
        out_shape=[shape(128, width, dtype=bf16)] * 3,
        scratch_shapes=[pltpu.VMEM((rows, width), bf16)] * 2 + [pltpu.SemaphoreType.DMA((2,))],
        compiler_params=pltpu.CompilerParams(vmem_limit_bytes=4 << 20),
        name="pair",
    )(
        core_id,
        pltpu.with_memory_space_constraint(image_emb, pltpu.HBM),
        pltpu.with_memory_space_constraint(text_emb, pltpu.HBM),
        image_got,
        text_got,
    )


def per_device(image_emb, text_emb):
    core_id = lax.axis_index("c").reshape(1).astype(jnp.int32)
    pair_rows, width = image_emb.shape
    count = pair_rows * 128

    got = [core_swap(image_emb), core_swap(text_emb)]
    near = pair(core_id, image_emb, text_emb, *got)
    for step in range(2):
        got = [flip_permute(near[q], q + step) for q in range(3)]
        outs = [shape(256 << step, width, dtype=bf16)] * 3 + [shape(1536, width, dtype=bf16)] * step
        near = call(stack_kernel, "stack", [core_id, *near, *got], outs, limit=2)
    *near, packed = near
    near_x = [core_swap(packed)]
    far = [flip_permute(near[q], q + 2) for q in range(3)]

    near_rows, near_cols, near_logits, row, col = call(
        near_kernel,
        "near",
        [core_id, *near, *near_x],
        [pltpu.VMEM((768, width), bf16), pltpu.VMEM((1536, width), bf16), pltpu.VMEM((768, 1536), f32)]
        + [shape(6, 128), shape(12, 128)],
        limit=10,
        flops=2 * 768 * 1536 * width,
    )
    far = [after(a, row) for a in far]
    far_x = [core_swap(a) for a in far]
    far_rows, far_cols, *logits, send, keep = call(
        far_kernel,
        "far",
        [core_id, *far, *far_x, held(near_rows), held(near_cols), row, col, image_emb, text_emb],
        [pltpu.VMEM((768, width), bf16), pltpu.VMEM((1536, width), bf16)]
        + [pltpu.VMEM((256, 3072), f32)] * 3
        + [pltpu.VMEM((768, 1536), f32), shape(32, 128), shape(32, 128)],
        limit=10,
        flops=2 * 768 * 4608 * width,
    )
    *wide_logits, tall_logits = logits

    mine = call(functools.partial(join_kernel, list(range(24))), "join", [core_id, keep, core_swap(send)], [shape(32, 128)], limit=2)[0]
    for dim in range(3):
        got = flip_permute(mine, dim)
        mine = call(functools.partial(join_kernel, flip_order(dim)), "join", [core_id, mine, got], [shape(32, 128)], limit=2)[0]
    other = core_swap(mine)

    held_rows = [held(near_rows), held(far_rows)]
    coeffs, *image_grads, own_image, loss = call(
        coeff_kernel,
        "coeffs",
        [core_id, mine, other]
        + [held(a) for a in (near_logits, tall_logits, *wide_logits, near_cols, far_cols)],
        [pltpu.VMEM((1536, 3072), bf16)] + [shape(256, width, dtype=bf16)] * 6 + [shape(384, width), shape(8, 128)],
        limit=10,
        flops=2 * 1536 * 3072 * width,
    )
    messages = []
    for q in range(3):
        kept, send = call(
            functools.partial(far_text_kernel, q),
            "far_text",
            [core_id, held(coeffs), *held_rows, image_grads[3 + q]],
            [shape(512, width, dtype=bf16)] * 2,
            limit=6,
            flops=2 * 1536 * 512 * width,
        )
        ins = [core_id, kept, core_swap(send)] + ([loss] if q == 0 else [])
        outs = [shape(528 if q == 0 else 512, width, dtype=bf16)]
        messages.append(call(far_message_kernel, "far_message", ins, outs)[0])
    got = [flip_permute(messages[q], q + 2) for q in range(3)]
    bases, near_got, owns = [], [], []
    for q in range(3):
        base, send, own = call(
            functools.partial(near_text_kernel, q),
            "near_text",
            [core_id, held(coeffs), *held_rows, image_grads[q], own_image, *messages],
            [shape(512, width), shape(512, width, dtype=bf16), shape(256, width)],
            limit=6,
            flops=2 * 1536 * 512 * width,
        )
        bases.append(base)
        near_got.append(core_swap(send))
        owns.append(own)
    total, loss = call(far_sum_kernel, "far_sum", [core_id, *bases, *got, loss], [shape(1536, width), shape(8, 128)])
    low, *messages = call(
        near_sum_kernel,
        "near_sum",
        [core_id, total, *near_got, loss],
        [shape(768, width)] + [shape(272 if q == 0 else 256, width, dtype=bf16) for q in range(3)],
    )
    got = [flip_permute(messages[q], q + 1) for q in range(3)]
    low, *messages, loss = call(
        half_sum_kernel,
        "half_sum",
        [core_id, low, *got, loss],
        [shape(384, width)] + [shape(144 if q == 0 else 128, width, dtype=bf16) for q in range(3)] + [shape(8, 128)],
    )
    got = [flip_permute(messages[q], q) for q in range(3)]
    keep, send = call(
        last_sum_kernel, "last_sum", [core_id, low, *got, *owns, loss], [shape(392, width), shape(392, width)]
    )
    grad_image, grad_text, loss = call(
        functools.partial(finish_kernel, count),
        "finish",
        [core_id, keep, core_swap(send)],
        [shape(192, width), shape(192, width), shape(1, 1)],
    )
    return loss.reshape(()), grad_image, grad_text


def solution(mesh):
    fine = Mesh(mesh.devices.reshape(4, 4, 4, 2), AXES)
    return jax.shard_map(
        per_device,
        mesh=fine,
        in_specs=(P(AXES, None), P(AXES, None)),
        out_specs=(P(), P(AXES, None), P(AXES, None)),
        check_vma=False,
    )
```

```python
import functools
import itertools
import math

import jax
import jax.numpy as jnp
from jax import lax
from jax.experimental import pallas as pl
from jax.experimental.pallas import tpu as pltpu
from jax.sharding import Mesh, PartitionSpec as P


logit_scale = 10.0
log2e = 1.4426950408889634
ln2 = 0.6931471805599453
lowest = -1e30
f32 = jnp.float32
bf16 = jnp.bfloat16
AXES = ("z", "y", "x", "c")
SWAP = ((0, 1), (1, 0))
FLIPS = ((0, 0, 1), (0, 1, 0), (1, 0, 0))
IMAGE_PAIR = (1, 0, 3, 2)
TEXT_PAIR = (3, 2, 1, 0)
VMEM = pl.BlockSpec(memory_space=pltpu.VMEM)
SMEM = pl.BlockSpec(memory_space=pltpu.SMEM)


def role_pairs(flip):
    pairs = []
    for z, y, x in itertools.product(range(4), repeat=3):
        for core, pair in ((0, IMAGE_PAIR), (1, TEXT_PAIR)):
            target = [pair[v] if f else v for v, f in zip((z, y, x), flip)]
            source_id = ((z * 4 + y) * 4 + x) * 2 + core
            target_id = ((target[0] * 4 + target[1]) * 4 + target[2]) * 2 + core
            pairs.append((source_id, target_id))
    return pairs


ROLE_PAIRS = [role_pairs(flip) for flip in FLIPS]


def flip_permute(x, dim):
    return lax.ppermute(x, AXES, ROLE_PAIRS[dim % 3])


def core_swap(x):
    return lax.ppermute(x, "c", SWAP)


def call(kernel, name, ins, outs, scratch=(), limit=6, flops=0, moved=0):
    in_specs = [SMEM if i == 0 else VMEM for i in range(len(ins))]
    return pl.pallas_call(
        kernel,
        in_specs=in_specs,
        out_specs=[VMEM] * len(outs),
        out_shape=list(outs),
        scratch_shapes=list(scratch),
        compiler_params=pltpu.CompilerParams(vmem_limit_bytes=limit << 20),
        cost_estimate=pl.CostEstimate(flops=flops, bytes_accessed=moved, transcendentals=0),
        name=name,
    )(*ins)


def held(x):
    return pltpu.with_memory_space_constraint(x, pltpu.VMEM)


def shape(*dims, dtype=f32):
    return jax.ShapeDtypeStruct(dims, dtype)


CONTRACT_LAST = (((1,), (1,)), ((), ()))
CONTRACT_FIRST = (((0,), (0,)), ((), ()))


def log_add(a, b):
    top = jnp.maximum(a, b)
    return top + jnp.log2(jnp.exp2(a - top) + jnp.exp2(b - top))


def lane_blocks(x):
    return [x[:, k : k + 128] for k in range(0, x.shape[1], 128)]


def row_stat(logits):
    top = jnp.max(logits, axis=1, keepdims=True)
    total = jnp.sum(jnp.exp2(logits - top), axis=1, keepdims=True)
    lse = top + jnp.log2(total)
    return jnp.concatenate(lane_blocks(jnp.broadcast_to(lse, (lse.shape[0], 128)).T[0:1, :]), 0)


def column_step(logits, state):
    top = jnp.max(logits, axis=0, keepdims=True)
    if state is None:
        return top, jnp.sum(jnp.exp2(logits - top), axis=0, keepdims=True)
    new_top = jnp.maximum(state[0], top)
    total = state[1] * jnp.exp2(state[0] - new_top) + jnp.sum(jnp.exp2(logits - new_top), axis=0, keepdims=True)
    return new_top, total


def column_stat(state):
    return jnp.concatenate(lane_blocks(state[0] + jnp.log2(state[1])), 0)


def product(a, b):
    return lax.dot_general(a, b, CONTRACT_LAST, preferred_element_type=f32) * (logit_scale * log2e)


def place(first, mine, swapped, rows_ref, cols_ref):
    @pl.when(first)
    def _():
        for q in range(3):
            rows_ref[q * 256 : q * 256 + 256, :] = mine[q][0:256, :]
            cols_ref[q * 512 : q * 512 + 512, :] = swapped[q][...]

    @pl.when(jnp.logical_not(first))
    def _():
        for q in range(3):
            rows_ref[q * 256 : q * 256 + 256, :] = swapped[q][256:512, :]
            cols_ref[q * 512 : q * 512 + 512, :] = mine[q][...]


def near_kernel(core_ref, m0, m1, m2, packed_ref, rows_ref, cols_ref, logit_ref, row_out, col_out):
    swapped = [packed_ref.at[q * 512 : q * 512 + 512] for q in range(3)]
    place(core_ref[0] == 0, (m0, m1, m2), swapped, rows_ref, cols_ref)
    rows, state = [], None
    for q in range(3):
        part = slice(q * 256, q * 256 + 256)
        logit_ref[part, :] = product(rows_ref[part, :], cols_ref[...])
        logits = logit_ref[part, :]
        rows.append(row_stat(logits))
        state = column_step(logits, state)
    row_out[...] = jnp.concatenate(rows, 0)
    col_out[...] = column_stat(state)


def far_kernel(core_ref, *refs):
    mine, swapped = refs[0:3], refs[3:6]
    near_rows, near_cols, row_old, col_old, image_ref, text_ref = refs[6:12]
    rows_ref, cols_ref, *wide_refs = refs[12:17]
    tall_ref, send_ref, keep_ref = refs[17:20]
    first = core_ref[0] == 0
    place(first, mine, swapped, rows_ref, cols_ref)
    new, state = [], None
    for q, wide in enumerate(wide_refs):
        part = slice(q * 256, q * 256 + 256)
        wide[:, 0:1536] = product(rows_ref[part, :], near_cols[...])
        wide[:, 1536:3072] = product(rows_ref[part, :], cols_ref[...])
        logits = wide[...]
        new.append(row_stat(logits))
        state = column_step(logits, state)
    old, tall_state = [], None
    for q in range(3):
        part = slice(q * 256, q * 256 + 256)
        tall_ref[part, :] = product(near_rows[part, :], cols_ref[...])
        logits = tall_ref[part, :]
        old.append(row_stat(logits))
        tall_state = column_step(logits, tall_state)
    row = jnp.concatenate([log_add(row_old[...], jnp.concatenate(old, 0))] + new, 0)
    col = log_add(column_stat(state), jnp.concatenate([col_old[...], column_stat(tall_state)], 0))
    positive = logit_scale * jnp.sum(image_ref[...].astype(f32) * text_ref[...].astype(f32))
    extra = jnp.full((8, 128), positive, f32)
    blank = jnp.full((2, 128), lowest, f32)
    low_half = jnp.concatenate([x for g in range(6) for x in (row[2 * g : 2 * g + 2], blank)], 0)
    high_half = jnp.concatenate([x for g in range(6) for x in (blank, row[2 * g : 2 * g + 2])], 0)
    send_ref[0:24, :] = jnp.where(first, col, high_half)
    keep_ref[0:24, :] = jnp.where(first, low_half, col)
    send_ref[24:32, :] = extra
    keep_ref[24:32, :] = extra


def stack_kernel(core_ref, *refs):
    packed = len(refs) == 10
    for q in range(3):
        a, b, out = refs[q], refs[q + 3], refs[q + 6]
        rows = a.shape[0]
        out[0:rows, :] = a[...]
        out[rows : 2 * rows, :] = b[...]
        if packed:
            refs[9][q * 512 : q * 512 + rows, :] = a[...]
            refs[9][q * 512 + rows : q * 512 + 512, :] = b[...]


def gate_kernel(value_ref, token_ref, out_ref):
    pass


def after(value, token):
    return pl.pallas_call(
        gate_kernel,
        in_specs=[VMEM, VMEM],
        out_specs=VMEM,
        out_shape=pltpu.VMEM(value.shape, value.dtype),
        input_output_aliases={0: 0},
        compiler_params=pltpu.CompilerParams(vmem_limit_bytes=1 << 20),
        name="after",
    )(held(value), token)


def join_kernel(order, core_ref, mine_ref, got_ref, out_ref):
    got = got_ref[...]
    out_ref[0:24, :] = log_add(mine_ref[0:24, :], jnp.concatenate([got[k : k + 1, :] for k in order], 0))
    out_ref[24:32, :] = mine_ref[24:32, :] + got_ref[24:32, :]


def flip_order(dim):
    order = []
    for half, q, k in itertools.product(range(2), range(3), range(4)):
        j = (dim - q) % 3
        if j == 2:
            order.append((1 - half) * 12 + q * 4 + k)
        else:
            order.append(half * 12 + q * 4 + (k ^ (1 << j)))
    return order


def tile_lse(first, mine_ref, other_ref):
    mine, other = mine_ref[0:24, :], other_ref[0:24, :]
    row = jnp.where(first, mine, other)
    col = jnp.where(first, other, mine)
    row = [jnp.where(first, row[4 * g + b : 4 * g + b + 1], row[4 * g + b + 2 : 4 * g + b + 3]) for g in range(6) for b in range(2)]
    row = jnp.concatenate(row, 1) + 1.0
    col = jnp.concatenate([col[k : k + 1] for k in range(24)], 1) + 1.0
    return row, col


def coefficients(logits, row, col):
    n = logits.shape[0]
    row = jnp.broadcast_to(row, (128, n)).T[:, 0:1]
    return jnp.exp2(logits - row) + jnp.exp2(logits - col)


def total_of(terms):
    total = terms[0]
    for term in terms[1:]:
        total = total + term
    return logit_scale * total


def times(a, b):
    return jnp.dot(a, b, preferred_element_type=f32)


def transposed_times(a, b):
    return lax.dot_general(a, b, CONTRACT_FIRST, preferred_element_type=f32)


def far_coeff_kernel(core_ref, mine_ref, other_ref, *refs):
    tall_ref, *wide_refs = refs[0:4]
    near_cols, far_cols = refs[4:6]
    coeff_ref, *grad_refs = refs[6:10]
    loss_ref = refs[10]
    first = core_ref[0] == 0
    row, col = tile_lse(first, mine_ref, other_ref)
    loss_ref[...] = jnp.sum(other_ref[0:24, :]) * ln2 - jnp.where(first, 0.0, 2.0) * other_ref[24:32, :]
    for q in range(3):
        part = slice(768 + q * 256, 768 + q * 256 + 256)
        coeff_ref[part, :] = coefficients(wide_refs[q][...], row[:, part], col).astype(bf16)
        grad = [times(coeff_ref[part, 0:1536], near_cols[...]), times(coeff_ref[part, 1536:3072], far_cols[...])]
        grad_refs[q][...] = total_of(grad).astype(bf16)
        part = slice(q * 256, q * 256 + 256)
        coeff_ref[part, 1536:3072] = coefficients(tall_ref[part, :], row[:, part], col[:, 1536:3072]).astype(bf16)


def near_coeff_kernel(core_ref, mine_ref, other_ref, *refs):
    logit_ref, coeff_ref, near_cols, far_cols = refs[0:4]
    block_ref, *grad_refs = refs[7:11]
    own_ref = refs[11]
    first = core_ref[0] == 0
    row, col = tile_lse(first, mine_ref, other_ref)
    eye = lax.broadcasted_iota(jnp.int32, (128, 128), 0) == lax.broadcasted_iota(jnp.int32, (128, 128), 1)
    positive = jnp.where(jnp.logical_and(eye, first), 1.0, 0.0)
    for q in range(3):
        part = slice(q * 256, q * 256 + 256)
        coeffs = coefficients(logit_ref[part, :], row[:, part], col[:, 0:1536])
        block_ref[part, :] = coeffs.astype(bf16)
        own = slice(q * 512, q * 512 + 128)
        block_ref[q * 256 : q * 256 + 128, own] = (coeffs[0:128, own] - positive).astype(bf16)
        grad = total_of([times(block_ref[part, :], near_cols[...]), times(coeff_ref[part, 1536:3072], far_cols[...])])
        grad_refs[q][...] = grad.astype(bf16)
        own_ref[q * 128 : q * 128 + 128, :] = grad[0:128, :]


def text_grad(near_coeffs, far_coeffs, near_rows, far_rows):
    return total_of([transposed_times(near_coeffs, near_rows[...]), transposed_times(far_coeffs, far_rows[...])])


def far_text_kernel(q, core_ref, coeff_ref, near_rows, far_rows, image_ref, kept_ref, send_ref):
    first = core_ref[0] == 0
    here = slice(1536 + q * 512, 2048 + q * 512)
    text = text_grad(coeff_ref[0:768, here], coeff_ref[768:1536, here], near_rows, far_rows).astype(bf16)
    image = image_ref[...]
    kept_ref[0:256, :] = jnp.where(first, image, text[0:256])
    send_ref[0:256, :] = jnp.where(first, text[0:256], image)
    kept_ref[256:512, :] = text[256:512]
    send_ref[256:512, :] = text[256:512]


def near_text_kernel(q, core_ref, block_ref, coeff_ref, near_rows, far_rows, image_ref, base_ref, send_ref, own_ref):
    first = core_ref[0] == 0
    here = slice(q * 512, q * 512 + 512)
    text = text_grad(block_ref[:, here], coeff_ref[768:1536, here], near_rows, far_rows)
    image = image_ref[...].astype(f32)
    own_ref[...] = text[0:128]
    base_ref[0:128, :] = jnp.where(first, 0.0, text[0:128])
    base_ref[128:256, :] = jnp.where(first, image[128:256], text[128:256])
    base_ref[256:512, :] = jnp.where(first, 0.0, text[256:512])
    send_ref[0:128, :] = jnp.where(first, 0.0, image[0:128]).astype(bf16)
    send_ref[128:256, :] = jnp.where(first, text[128:256], image[128:256]).astype(bf16)
    send_ref[256:512, :] = text[256:512].astype(bf16)


def own_kernel(core_ref, image_ref, t0, t1, t2, early_image, early_text, kept_ref):
    for q, t in enumerate((t0, t1, t2)):
        rows, text_rows = slice(q * 64, q * 64 + 64), slice(192 + q * 64, 192 + q * 64 + 64)
        kept_ref[rows, :] = image_ref[q * 128 : q * 128 + 64, :]
        early_image[rows, :] = image_ref[q * 128 + 64 : q * 128 + 128, :]
        kept_ref[text_rows, :] = t[0:64, :]
        early_text[rows, :] = t[64:128, :]


def split_terms(x):
    high = x.astype(bf16)
    rest = x - high.astype(f32)
    middle = rest.astype(bf16)
    low = (rest - middle.astype(f32)).astype(bf16)
    pair = [jnp.concatenate([t, t], 0) for t in (high, middle, low)]
    return jnp.concatenate(pair + [jnp.zeros((16, 128), bf16)], 1)


def join_terms(ref, start):
    x = ref[start : start + 16, :].astype(f32)
    return (x[0:8, 0:128] + x[0:8, 128:256]) + x[0:8, 256:384]


def far_message_kernel(core_ref, mine_ref, got_ref, *refs):
    first = core_ref[0] == 0
    got = got_ref[...]
    both = (mine_ref[...].astype(f32) + got.astype(f32)).astype(bf16)
    refs[-1][0:256, :] = jnp.where(first, mine_ref[0:256, :], both[0:256])
    refs[-1][256:512, :] = jnp.where(first, got[0:256], both[256:512])
    if len(refs) == 2:
        refs[-1][512:528, :] = split_terms(refs[0][...])


def far_sum_kernel(core_ref, b0, b1, b2, r0, r1, r2, loss_ref, total_ref, loss_out):
    loss_out[...] = loss_ref[...] + join_terms(r0, 512)
    for q, (b, r) in enumerate(((b0, r0), (b1, r1), (b2, r2))):
        total_ref[q * 512 : q * 512 + 512, :] = b[...] + r[0:512, :].astype(f32)


def near_sum_kernel(core_ref, total_ref, g0, g1, g2, loss_ref, e0, e1, low_ref, s0, s1, s2):
    first = core_ref[0] == 0
    s0[256:272, :] = split_terms(loss_ref[...])
    for q, (g, s) in enumerate(((g0, s0), (g1, s1), (g2, s2))):
        at = q * 512
        got = g[...].astype(f32)
        low_ref[q * 256 : q * 256 + 256, :] = total_ref[at : at + 256, :] + jnp.where(first, 0.0, got[0:256])
        s[0:256, :] = (total_ref[at + 256 : at + 512, :] + jnp.where(first, got[0:256], got[256:512])).astype(bf16)


def half_sum_kernel(core_ref, low_ref, r0, r1, r2, loss_ref, out_ref, s0, s1, s2, loss_out):
    loss = loss_ref[...] + join_terms(r0, 256)
    loss_out[...] = loss
    s0[128:144, :] = split_terms(loss)
    for q, (r, s) in enumerate(((r0, s0), (r1, s1), (r2, s2))):
        total = low_ref[q * 256 : q * 256 + 256, :] + r[0:256, :].astype(f32)
        out_ref[q * 128 : q * 128 + 128, :] = total[0:128]
        s[0:128, :] = total[128:256].astype(bf16)


def last_sum_kernel(core_ref, low_ref, r0, r1, r2, loss_ref, keep_ref, send_ref):
    first = core_ref[0] == 0
    loss = loss_ref[...] + join_terms(r0, 128)
    keep_ref[192:200, :] = jnp.concatenate([loss] * 4, 1)
    send_ref[192:200, :] = jnp.concatenate([loss] * 4, 1)
    for q, r in enumerate((r0, r1, r2)):
        rows = slice(q * 64, q * 64 + 64)
        total = low_ref[q * 128 : q * 128 + 128, :] + r[0:128, :].astype(f32)
        keep_ref[rows, :] = jnp.where(first, total[0:64], total[64:128])
        send_ref[rows, :] = jnp.where(first, total[64:128], total[0:64])


def finish_kernel(count, core_ref, keep_ref, got_ref, kept_ref, early_image, early_text, image_out, text_out, loss_out):
    first = core_ref[0] == 0
    keep, got = keep_ref[0:192, :], got_ref[0:192, :]
    image_out[...] = jnp.where(first, keep, got) + jnp.where(first, kept_ref[0:192, :], early_image[...])
    text_out[...] = jnp.where(first, got, keep) + jnp.where(first, kept_ref[192:384, :], early_text[...])
    loss_out[...] = (keep_ref[192:193, 0:1] + got_ref[192:193, 0:1]) * (0.5 / count)


def pair_kernel(core_ref, image_hbm, text_hbm, image_got, text_got, o0, o1, o2, image_ref, text_ref, sems):
    copies = [
        pltpu.make_async_copy(image_hbm, image_ref, sems.at[0]),
        pltpu.make_async_copy(text_hbm, text_ref, sems.at[1]),
    ]
    for copy in copies:
        copy.start()
    for copy in copies:
        copy.wait()
    first = core_ref[0] == 0
    for q, out in enumerate((o0, o1, o2)):
        rows = slice(q * 64, q * 64 + 64)
        out[0:64, :] = jnp.where(first, image_ref[rows, :], text_got[rows, :])
        out[64:128, :] = jnp.where(first, image_got[rows, :], text_ref[rows, :])


def pair(core_id, image_emb, text_emb, image_got, text_got):
    rows, width = image_emb.shape
    anywhere = pl.BlockSpec(memory_space=pl.ANY)
    return pl.pallas_call(
        pair_kernel,
        in_specs=[SMEM, anywhere, anywhere, VMEM, VMEM],
        out_specs=[VMEM] * 3,
        out_shape=[shape(128, width, dtype=bf16)] * 3,
        scratch_shapes=[pltpu.VMEM((rows, width), bf16)] * 2 + [pltpu.SemaphoreType.DMA((2,))],
        compiler_params=pltpu.CompilerParams(vmem_limit_bytes=4 << 20),
        name="pair",
    )(
        core_id,
        pltpu.with_memory_space_constraint(image_emb, pltpu.HBM),
        pltpu.with_memory_space_constraint(text_emb, pltpu.HBM),
        image_got,
        text_got,
    )


def per_device(image_emb, text_emb):
    core_id = lax.axis_index("c").reshape(1).astype(jnp.int32)
    pair_rows, width = image_emb.shape
    count = pair_rows * 128

    got = [core_swap(image_emb), core_swap(text_emb)]
    near = pair(core_id, image_emb, text_emb, *got)
    for step in range(2):
        got = [flip_permute(near[q], q + step) for q in range(3)]
        outs = [shape(256 << step, width, dtype=bf16)] * 3 + [shape(1536, width, dtype=bf16)] * step
        near = call(stack_kernel, "stack", [core_id, *near, *got], outs, limit=2)
    *near, packed = near
    near_x = [core_swap(packed)]
    far = [flip_permute(near[q], q + 2) for q in range(3)]

    near_rows, near_cols, near_logits, row, col = call(
        near_kernel,
        "near",
        [core_id, *near, *near_x],
        [pltpu.VMEM((768, width), bf16), pltpu.VMEM((1536, width), bf16), pltpu.VMEM((768, 1536), f32)]
        + [shape(6, 128), shape(12, 128)],
        limit=10,
        flops=2 * 768 * 1536 * width,
    )
    far = [after(a, row) for a in far]
    far_x = [core_swap(a) for a in far]
    far_rows, far_cols, *logits, send, keep = call(
        far_kernel,
        "far",
        [core_id, *far, *far_x, held(near_rows), held(near_cols), row, col, image_emb, text_emb],
        [pltpu.VMEM((768, width), bf16), pltpu.VMEM((1536, width), bf16)]
        + [pltpu.VMEM((256, 3072), f32)] * 3
        + [pltpu.VMEM((768, 1536), f32), shape(32, 128), shape(32, 128)],
        limit=10,
        flops=2 * 768 * 4608 * width,
    )
    *wide_logits, tall_logits = logits

    mine = call(functools.partial(join_kernel, list(range(24))), "join", [core_id, keep, core_swap(send)], [shape(32, 128)], limit=2)[0]
    for dim in range(3):
        got = flip_permute(mine, dim)
        mine = call(functools.partial(join_kernel, flip_order(dim)), "join", [core_id, mine, got], [shape(32, 128)], limit=2)[0]
    other = core_swap(mine)

    held_rows = [held(near_rows), held(far_rows)]
    held_cols = [held(near_cols), held(far_cols)]
    coeffs, *far_images, loss = call(
        far_coeff_kernel,
        "far_coeffs",
        [core_id, mine, other, held(tall_logits), *[held(a) for a in wide_logits], *held_cols],
        [pltpu.VMEM((1536, 3072), bf16)] + [shape(256, width, dtype=bf16)] * 3 + [shape(8, 128)],
        limit=10,
        flops=2 * 768 * 3072 * width,
    )
    messages = []
    for q in range(3):
        kept, send = call(
            functools.partial(far_text_kernel, q),
            "far_text",
            [core_id, held(coeffs), *held_rows, far_images[q]],
            [shape(512, width, dtype=bf16)] * 2,
            limit=6,
            flops=2 * 1536 * 512 * width,
        )
        ins = [core_id, kept, core_swap(send)] + ([loss] if q == 0 else [])
        outs = [shape(528 if q == 0 else 512, width, dtype=bf16)]
        messages.append(call(far_message_kernel, "far_message", ins, outs)[0])
    got = [flip_permute(messages[q], q + 2) for q in range(3)]
    block, *near_images, own_image = call(
        near_coeff_kernel,
        "near_coeffs",
        [core_id, mine, other, held(near_logits), held(coeffs), *held_cols, *messages],
        [pltpu.VMEM((768, 1536), bf16)] + [shape(256, width, dtype=bf16)] * 3 + [shape(384, width)],
        limit=10,
        flops=2 * 768 * 3072 * width,
    )
    bases, near_got, owns = [], [], []
    for q in range(3):
        base, send, own = call(
            functools.partial(near_text_kernel, q),
            "near_text",
            [core_id, held(block), held(coeffs), *held_rows, near_images[q]],
            [shape(512, width), shape(512, width, dtype=bf16), shape(128, width)],
            limit=6,
            flops=2 * 1536 * 512 * width,
        )
        bases.append(base)
        near_got.append(core_swap(send))
        owns.append(own)
    *early, kept = call(
        own_kernel, "own", [core_id, own_image, *owns], [shape(192, width), shape(192, width), shape(384, width)]
    )
    early_got = [core_swap(a) for a in early]
    total, loss = call(far_sum_kernel, "far_sum", [core_id, *bases, *got, loss], [shape(1536, width), shape(8, 128)])
    low, *messages = call(
        near_sum_kernel,
        "near_sum",
        [core_id, total, *near_got, loss, *early_got],
        [shape(768, width)] + [shape(272 if q == 0 else 256, width, dtype=bf16) for q in range(3)],
    )
    got = [flip_permute(messages[q], q + 1) for q in range(3)]
    low, *messages, loss = call(
        half_sum_kernel,
        "half_sum",
        [core_id, low, *got, loss],
        [shape(384, width)] + [shape(144 if q == 0 else 128, width, dtype=bf16) for q in range(3)] + [shape(8, 128)],
    )
    got = [flip_permute(messages[q], q) for q in range(3)]
    keep, send = call(
        last_sum_kernel, "last_sum", [core_id, low, *got, loss], [shape(200, width), shape(200, width)]
    )
    grad_image, grad_text, loss = call(
        functools.partial(finish_kernel, count),
        "finish",
        [core_id, keep, core_swap(send), kept, *early_got],
        [shape(192, width), shape(192, width), shape(1, 1)],
    )
    return loss.reshape(()), grad_image, grad_text


def solution(mesh):
    fine = Mesh(mesh.devices.reshape(4, 4, 4, 2), AXES)
    return jax.shard_map(
        per_device,
        mesh=fine,
        in_specs=(P(AXES, None), P(AXES, None)),
        out_specs=(P(), P(AXES, None), P(AXES, None)),
        check_vma=False,
    )
```

```python
import functools
import itertools
import math

import jax
import jax.numpy as jnp
from jax import lax
from jax.experimental import pallas as pl
from jax.experimental.pallas import tpu as pltpu
from jax.sharding import Mesh, PartitionSpec as P


logit_scale = 10.0
log2e = 1.4426950408889634
ln2 = 0.6931471805599453
lowest = -1e30
f32 = jnp.float32
bf16 = jnp.bfloat16
AXES = ("z", "y", "x", "c")
SWAP = ((0, 1), (1, 0))
FLIPS = ((0, 0, 1), (0, 1, 0), (1, 0, 0))
IMAGE_PAIR = (1, 0, 3, 2)
TEXT_PAIR = (3, 2, 1, 0)
VMEM = pl.BlockSpec(memory_space=pltpu.VMEM)
SMEM = pl.BlockSpec(memory_space=pltpu.SMEM)


def role_pairs(flip):
    pairs = []
    for z, y, x in itertools.product(range(4), repeat=3):
        for core, pair in ((0, IMAGE_PAIR), (1, TEXT_PAIR)):
            target = [pair[v] if f else v for v, f in zip((z, y, x), flip)]
            source_id = ((z * 4 + y) * 4 + x) * 2 + core
            target_id = ((target[0] * 4 + target[1]) * 4 + target[2]) * 2 + core
            pairs.append((source_id, target_id))
    return pairs


ROLE_PAIRS = [role_pairs(flip) for flip in FLIPS]


def flip_permute(x, dim):
    return lax.ppermute(x, AXES, ROLE_PAIRS[dim % 3])


def core_swap(x):
    return lax.ppermute(x, "c", SWAP)


def call(kernel, name, ins, outs, scratch=(), limit=6, flops=0, moved=0):
    in_specs = [SMEM if i == 0 else VMEM for i in range(len(ins))]
    return pl.pallas_call(
        kernel,
        in_specs=in_specs,
        out_specs=[VMEM] * len(outs),
        out_shape=list(outs),
        scratch_shapes=list(scratch),
        compiler_params=pltpu.CompilerParams(vmem_limit_bytes=limit << 20),
        cost_estimate=pl.CostEstimate(flops=flops, bytes_accessed=moved, transcendentals=0),
        name=name,
    )(*ins)


def held(x):
    return pltpu.with_memory_space_constraint(x, pltpu.VMEM)


def shape(*dims, dtype=f32):
    return jax.ShapeDtypeStruct(dims, dtype)


CONTRACT_LAST = (((1,), (1,)), ((), ()))
CONTRACT_FIRST = (((0,), (0,)), ((), ()))


def log_add(a, b):
    top = jnp.maximum(a, b)
    return top + jnp.log2(jnp.exp2(a - top) + jnp.exp2(b - top))


def lane_blocks(x):
    return [x[:, k : k + 128] for k in range(0, x.shape[1], 128)]


def row_stat(logits):
    top = jnp.max(logits, axis=1, keepdims=True)
    total = jnp.sum(jnp.exp2(logits - top), axis=1, keepdims=True)
    lse = top + jnp.log2(total)
    return jnp.concatenate(lane_blocks(jnp.broadcast_to(lse, (lse.shape[0], 128)).T[0:1, :]), 0)


def column_step(logits, state):
    top = jnp.max(logits, axis=0, keepdims=True)
    if state is None:
        return top, jnp.sum(jnp.exp2(logits - top), axis=0, keepdims=True)
    new_top = jnp.maximum(state[0], top)
    total = state[1] * jnp.exp2(state[0] - new_top) + jnp.sum(jnp.exp2(logits - new_top), axis=0, keepdims=True)
    return new_top, total


def column_stat(state):
    return jnp.concatenate(lane_blocks(state[0] + jnp.log2(state[1])), 0)


def product(a, b):
    return lax.dot_general(a, b, CONTRACT_LAST, preferred_element_type=f32) * (logit_scale * log2e)


def place(first, mine, swapped, rows_ref, cols_ref):
    @pl.when(first)
    def _():
        for q in range(3):
            rows_ref[q * 256 : q * 256 + 256, :] = mine[q][0:256, :]
            cols_ref[q * 512 : q * 512 + 512, :] = swapped[q][...]

    @pl.when(jnp.logical_not(first))
    def _():
        for q in range(3):
            rows_ref[q * 256 : q * 256 + 256, :] = swapped[q][256:512, :]
            cols_ref[q * 512 : q * 512 + 512, :] = mine[q][...]


def near_kernel(core_ref, m0, m1, m2, packed_ref, rows_ref, cols_ref, logit_ref, row_out, col_out):
    swapped = [packed_ref.at[q * 512 : q * 512 + 512] for q in range(3)]
    place(core_ref[0] == 0, (m0, m1, m2), swapped, rows_ref, cols_ref)
    rows, state = [], None
    for q in range(3):
        part = slice(q * 256, q * 256 + 256)
        logit_ref[part, :] = product(rows_ref[part, :], cols_ref[...])
        logits = logit_ref[part, :]
        rows.append(row_stat(logits))
        state = column_step(logits, state)
    row_out[...] = jnp.concatenate(rows, 0)
    col_out[...] = column_stat(state)


def far_kernel(core_ref, *refs):
    mine, swapped = refs[0:3], refs[3:6]
    near_rows, near_cols, row_old, col_old, image_ref, text_ref = refs[6:12]
    rows_ref, cols_ref, *wide_refs = refs[12:17]
    tall_ref, send_ref, keep_ref = refs[17:20]
    first = core_ref[0] == 0
    place(first, mine, swapped, rows_ref, cols_ref)
    new, state = [], None
    for q, wide in enumerate(wide_refs):
        part = slice(q * 256, q * 256 + 256)
        wide[:, 0:1536] = product(rows_ref[part, :], near_cols[...])
        wide[:, 1536:3072] = product(rows_ref[part, :], cols_ref[...])
        logits = wide[...]
        new.append(row_stat(logits))
        state = column_step(logits, state)
    old, tall_state = [], None
    for q in range(3):
        part = slice(q * 256, q * 256 + 256)
        tall_ref[part, :] = product(near_rows[part, :], cols_ref[...])
        logits = tall_ref[part, :]
        old.append(row_stat(logits))
        tall_state = column_step(logits, tall_state)
    row = jnp.concatenate([log_add(row_old[...], jnp.concatenate(old, 0))] + new, 0)
    col = log_add(column_stat(state), jnp.concatenate([col_old[...], column_stat(tall_state)], 0))
    positive = logit_scale * jnp.sum(image_ref[...].astype(f32) * text_ref[...].astype(f32))
    extra = jnp.full((8, 128), positive, f32)
    blank = jnp.full((2, 128), lowest, f32)
    low_half = jnp.concatenate([x for g in range(6) for x in (row[2 * g : 2 * g + 2], blank)], 0)
    high_half = jnp.concatenate([x for g in range(6) for x in (blank, row[2 * g : 2 * g + 2])], 0)
    send_ref[0:24, :] = jnp.where(first, col, high_half)
    keep_ref[0:24, :] = jnp.where(first, low_half, col)
    send_ref[24:32, :] = extra
    keep_ref[24:32, :] = extra


def stack_kernel(core_ref, *refs):
    packed = len(refs) == 10
    for q in range(3):
        a, b, out = refs[q], refs[q + 3], refs[q + 6]
        rows = a.shape[0]
        out[0:rows, :] = a[...]
        out[rows : 2 * rows, :] = b[...]
        if packed:
            refs[9][q * 512 : q * 512 + rows, :] = a[...]
            refs[9][q * 512 + rows : q * 512 + 512, :] = b[...]


def gate_kernel(value_ref, token_ref, out_ref):
    pass


def after(value, token):
    return pl.pallas_call(
        gate_kernel,
        in_specs=[VMEM, VMEM],
        out_specs=VMEM,
        out_shape=pltpu.VMEM(value.shape, value.dtype),
        input_output_aliases={0: 0},
        compiler_params=pltpu.CompilerParams(vmem_limit_bytes=1 << 20),
        name="after",
    )(held(value), token)


def join_kernel(order, core_ref, mine_ref, got_ref, out_ref):
    got = got_ref[...]
    out_ref[0:24, :] = log_add(mine_ref[0:24, :], jnp.concatenate([got[k : k + 1, :] for k in order], 0))
    out_ref[24:32, :] = mine_ref[24:32, :] + got_ref[24:32, :]


def flip_order(dim):
    order = []
    for half, q, k in itertools.product(range(2), range(3), range(4)):
        j = (dim - q) % 3
        if j == 2:
            order.append((1 - half) * 12 + q * 4 + k)
        else:
            order.append(half * 12 + q * 4 + (k ^ (1 << j)))
    return order


def tile_lse(first, mine_ref, other_ref):
    mine, other = mine_ref[0:24, :], other_ref[0:24, :]
    row = jnp.where(first, mine, other)
    col = jnp.where(first, other, mine)
    row = [jnp.where(first, row[4 * g + b : 4 * g + b + 1], row[4 * g + b + 2 : 4 * g + b + 3]) for g in range(6) for b in range(2)]
    row = jnp.concatenate(row, 1) + 1.0
    col = jnp.concatenate([col[k : k + 1] for k in range(24)], 1) + 1.0
    return row, col


def coefficients(logits, row, col):
    n = logits.shape[0]
    row = jnp.broadcast_to(row, (128, n)).T[:, 0:1]
    return jnp.exp2(logits - row) + jnp.exp2(logits - col)


def total_of(terms):
    total = terms[0]
    for term in terms[1:]:
        total = total + term
    return logit_scale * total


def times(a, b):
    return jnp.dot(a, b, preferred_element_type=f32)


def transposed_times(a, b):
    return lax.dot_general(a, b, CONTRACT_FIRST, preferred_element_type=f32)


def coeff_kernel(core_ref, mine_ref, other_ref, *refs):
    near_ref, tall_ref, *wide_refs = refs[0:5]
    near_cols, far_cols = refs[5:7]
    coeff_ref, *grad_refs = refs[7:14]
    own_ref, loss_ref = refs[14:16]
    first = core_ref[0] == 0
    row, col = tile_lse(first, mine_ref, other_ref)
    loss_ref[...] = jnp.sum(other_ref[0:24, :]) * ln2 - jnp.where(first, 0.0, 2.0) * other_ref[24:32, :]
    eye = lax.broadcasted_iota(jnp.int32, (128, 128), 0) == lax.broadcasted_iota(jnp.int32, (128, 128), 1)
    positive = jnp.where(jnp.logical_and(eye, first), 1.0, 0.0)
    for g in range(6):
        part = slice(g * 256, g * 256 + 256)
        if g < 3:
            coeffs = coefficients(near_ref[part, :], row[:, part], col[:, 0:1536])
            coeff_ref[part, 0:1536] = coeffs.astype(bf16)
            own = slice(g * 512, g * 512 + 128)
            coeff_ref[g * 256 : g * 256 + 128, own] = (coeffs[0:128, own] - positive).astype(bf16)
            coeff_ref[part, 1536:3072] = coefficients(tall_ref[part, :], row[:, part], col[:, 1536:3072]).astype(bf16)
        else:
            coeff_ref[part, :] = coefficients(wide_refs[g - 3][...], row[:, part], col).astype(bf16)
        grad = total_of(
            [times(coeff_ref[part, 0:1536], near_cols[...]), times(coeff_ref[part, 1536:3072], far_cols[...])]
        )
        grad_refs[g][...] = grad.astype(bf16)
        if g < 3:
            own_ref[g * 128 : g * 128 + 128, :] = grad[0:128, :]


def text_grad(coeff_ref, near_rows, far_rows, start):
    here = slice(start, start + 512)
    return total_of(
        [
            transposed_times(coeff_ref[0:768, here], near_rows[...]),
            transposed_times(coeff_ref[768:1536, here], far_rows[...]),
        ]
    )


def far_text_kernel(q, core_ref, coeff_ref, near_rows, far_rows, image_ref, kept_ref, send_ref):
    first = core_ref[0] == 0
    text = text_grad(coeff_ref, near_rows, far_rows, 1536 + q * 512).astype(bf16)
    image = image_ref[...]
    kept_ref[0:256, :] = jnp.where(first, image, text[0:256])
    send_ref[0:256, :] = jnp.where(first, text[0:256], image)
    kept_ref[256:512, :] = text[256:512]
    send_ref[256:512, :] = text[256:512]


def near_text_kernel(q, core_ref, coeff_ref, near_rows, far_rows, image_ref, own_image, a0, a1, a2, base_ref, send_ref, own_ref):
    first = core_ref[0] == 0
    text = text_grad(coeff_ref, near_rows, far_rows, q * 512)
    image = image_ref[...].astype(f32)
    own_ref[0:128, :] = own_image[q * 128 : q * 128 + 128, :]
    own_ref[128:256, :] = text[0:128]
    base_ref[0:128, :] = jnp.where(first, 0.0, text[0:128])
    base_ref[128:256, :] = jnp.where(first, image[128:256], text[128:256])
    base_ref[256:512, :] = jnp.where(first, 0.0, text[256:512])
    send_ref[0:128, :] = jnp.where(first, 0.0, image[0:128]).astype(bf16)
    send_ref[128:256, :] = jnp.where(first, text[128:256], image[128:256]).astype(bf16)
    send_ref[256:512, :] = text[256:512].astype(bf16)


def split_terms(x):
    high = x.astype(bf16)
    rest = x - high.astype(f32)
    middle = rest.astype(bf16)
    low = (rest - middle.astype(f32)).astype(bf16)
    pair = [jnp.concatenate([t, t], 0) for t in (high, middle, low)]
    return jnp.concatenate(pair + [jnp.zeros((16, 128), bf16)], 1)


def join_terms(ref, start):
    x = ref[start : start + 16, :].astype(f32)
    return (x[0:8, 0:128] + x[0:8, 128:256]) + x[0:8, 256:384]


def far_message_kernel(core_ref, mine_ref, got_ref, *refs):
    first = core_ref[0] == 0
    got = got_ref[...]
    both = (mine_ref[...].astype(f32) + got.astype(f32)).astype(bf16)
    refs[-1][0:256, :] = jnp.where(first, mine_ref[0:256, :], both[0:256])
    refs[-1][256:512, :] = jnp.where(first, got[0:256], both[256:512])
    if len(refs) == 2:
        refs[-1][512:528, :] = split_terms(refs[0][...])


def far_sum_kernel(core_ref, base_ref, got_ref, *refs):
    total_ref = refs[0]
    if len(refs) == 3:
        loss_ref, total_ref, loss_out = refs
        loss_out[...] = loss_ref[...] + join_terms(got_ref, 512)
    total_ref[...] = base_ref[...] + got_ref[0:512, :].astype(f32)


def near_sum_kernel(core_ref, total_ref, got_ref, *refs):
    first = core_ref[0] == 0
    low_ref, send_ref = refs[-2:]
    if len(refs) == 3:
        send_ref[256:272, :] = split_terms(refs[0][...])
    got = got_ref[...].astype(f32)
    low_ref[...] = total_ref[0:256, :] + jnp.where(first, 0.0, got[0:256])
    send_ref[0:256, :] = (total_ref[256:512, :] + jnp.where(first, got[0:256], got[256:512])).astype(bf16)


def half_sum_kernel(core_ref, low_ref, got_ref, *refs):
    if len(refs) == 4:
        loss_ref, out_ref, send_ref, loss_out = refs
        loss = loss_ref[...] + join_terms(got_ref, 256)
        loss_out[...] = loss
        send_ref[128:144, :] = split_terms(loss)
    else:
        out_ref, send_ref = refs
    total = low_ref[...] + got_ref[0:256, :].astype(f32)
    out_ref[...] = total[0:128]
    send_ref[0:128, :] = total[128:256].astype(bf16)


def last_sum_kernel(core_ref, l0, l1, l2, r0, r1, r2, o0, o1, o2, loss_ref, keep_ref, send_ref):
    first = core_ref[0] == 0
    loss = loss_ref[...] + join_terms(r0, 128)
    keep_ref[384:392, :] = jnp.concatenate([loss] * 4, 1)
    send_ref[384:392, :] = jnp.concatenate([loss] * 4, 1)
    for q, (low, r, own) in enumerate(((l0, r0, o0), (l1, r1, o1), (l2, r2, o2))):
        rows, text_rows = slice(q * 64, q * 64 + 64), slice(192 + q * 64, 192 + q * 64 + 64)
        total = low[...] + r[0:128, :].astype(f32)
        keep_ref[rows, :] = jnp.where(first, total[0:64] + own[0:64, :], total[64:128])
        keep_ref[text_rows, :] = own[128:192, :]
        send_ref[rows, :] = jnp.where(first, total[64:128] + own[64:128, :], total[0:64])
        send_ref[text_rows, :] = own[192:256, :]


def finish_kernel(count, core_ref, keep_ref, got_ref, image_out, text_out, loss_out):
    first = core_ref[0] == 0
    image_out[...] = jnp.where(first, keep_ref[0:192, :], got_ref[0:192, :])
    text_out[...] = jnp.where(
        first, got_ref[0:192, :] + keep_ref[192:384, :], keep_ref[0:192, :] + got_ref[192:384, :]
    )
    loss_out[...] = (keep_ref[384:385, 0:1] + got_ref[384:385, 0:1]) * (0.5 / count)


def pair_kernel(core_ref, image_hbm, text_hbm, image_got, text_got, o0, o1, o2, image_ref, text_ref, sems):
    copies = [
        pltpu.make_async_copy(image_hbm, image_ref, sems.at[0]),
        pltpu.make_async_copy(text_hbm, text_ref, sems.at[1]),
    ]
    for copy in copies:
        copy.start()
    for copy in copies:
        copy.wait()
    first = core_ref[0] == 0
    for q, out in enumerate((o0, o1, o2)):
        rows = slice(q * 64, q * 64 + 64)
        out[0:64, :] = jnp.where(first, image_ref[rows, :], text_got[rows, :])
        out[64:128, :] = jnp.where(first, image_got[rows, :], text_ref[rows, :])


def pair(core_id, image_emb, text_emb, image_got, text_got):
    rows, width = image_emb.shape
    anywhere = pl.BlockSpec(memory_space=pl.ANY)
    return pl.pallas_call(
        pair_kernel,
        in_specs=[SMEM, anywhere, anywhere, VMEM, VMEM],
        out_specs=[VMEM] * 3,
        out_shape=[shape(128, width, dtype=bf16)] * 3,
        scratch_shapes=[pltpu.VMEM((rows, width), bf16)] * 2 + [pltpu.SemaphoreType.DMA((2,))],
        compiler_params=pltpu.CompilerParams(vmem_limit_bytes=4 << 20),
        name="pair",
    )(
        core_id,
        pltpu.with_memory_space_constraint(image_emb, pltpu.HBM),
        pltpu.with_memory_space_constraint(text_emb, pltpu.HBM),
        image_got,
        text_got,
    )


def per_device(image_emb, text_emb):
    core_id = lax.axis_index("c").reshape(1).astype(jnp.int32)
    pair_rows, width = image_emb.shape
    count = pair_rows * 128

    got = [core_swap(image_emb), core_swap(text_emb)]
    near = pair(core_id, image_emb, text_emb, *got)
    for step in range(2):
        got = [flip_permute(near[q], q + step) for q in range(3)]
        outs = [shape(256 << step, width, dtype=bf16)] * 3 + [shape(1536, width, dtype=bf16)] * step
        near = call(stack_kernel, "stack", [core_id, *near, *got], outs, limit=2)
    *near, packed = near
    near_x = [core_swap(packed)]
    far = [flip_permute(near[q], q + 2) for q in range(3)]

    near_rows, near_cols, near_logits, row, col = call(
        near_kernel,
        "near",
        [core_id, *near, *near_x],
        [pltpu.VMEM((768, width), bf16), pltpu.VMEM((1536, width), bf16), pltpu.VMEM((768, 1536), f32)]
        + [shape(6, 128), shape(12, 128)],
        limit=10,
        flops=2 * 768 * 1536 * width,
    )
    far = [after(a, row) for a in far]
    far_x = [core_swap(a) for a in far]
    far_rows, far_cols, *logits, send, keep = call(
        far_kernel,
        "far",
        [core_id, *far, *far_x, held(near_rows), held(near_cols), row, col, image_emb, text_emb],
        [pltpu.VMEM((768, width), bf16), pltpu.VMEM((1536, width), bf16)]
        + [pltpu.VMEM((256, 3072), f32)] * 3
        + [pltpu.VMEM((768, 1536), f32), shape(32, 128), shape(32, 128)],
        limit=10,
        flops=2 * 768 * 4608 * width,
    )
    *wide_logits, tall_logits = logits

    mine = call(functools.partial(join_kernel, list(range(24))), "join", [core_id, keep, core_swap(send)], [shape(32, 128)], limit=2)[0]
    for dim in range(3):
        got = flip_permute(mine, dim)
        mine = call(functools.partial(join_kernel, flip_order(dim)), "join", [core_id, mine, got], [shape(32, 128)], limit=2)[0]
    other = core_swap(mine)

    held_rows = [held(near_rows), held(far_rows)]
    coeffs, *image_grads, own_image, loss = call(
        coeff_kernel,
        "coeffs",
        [core_id, mine, other]
        + [held(a) for a in (near_logits, tall_logits, *wide_logits, near_cols, far_cols)],
        [pltpu.VMEM((1536, 3072), bf16)] + [shape(256, width, dtype=bf16)] * 6 + [shape(384, width), shape(8, 128)],
        limit=10,
        flops=2 * 1536 * 3072 * width,
    )
    messages = []
    for q in range(3):
        kept, send = call(
            functools.partial(far_text_kernel, q),
            "far_text",
            [core_id, held(coeffs), *held_rows, image_grads[3 + q]],
            [shape(512, width, dtype=bf16)] * 2,
            limit=6,
            flops=2 * 1536 * 512 * width,
        )
        ins = [core_id, kept, core_swap(send)] + ([loss] if q == 0 else [])
        outs = [shape(528 if q == 0 else 512, width, dtype=bf16)]
        messages.append(call(far_message_kernel, "far_message", ins, outs)[0])
    got = [flip_permute(messages[q], q + 2) for q in range(3)]
    bases, near_got, owns = [], [], []
    for q in range(3):
        base, send, own = call(
            functools.partial(near_text_kernel, q),
            "near_text",
            [core_id, held(coeffs), *held_rows, image_grads[q], own_image, *messages],
            [shape(512, width), shape(512, width, dtype=bf16), shape(256, width)],
            limit=6,
            flops=2 * 1536 * 512 * width,
        )
        bases.append(base)
        near_got.append(core_swap(send))
        owns.append(own)
    lows, last = [], []
    for q in range(3):
        extra = [loss] if q == 0 else []
        more = [shape(8, 128)] if q == 0 else []
        pad = 16 if q == 0 else 0
        total, *extra = call(
            far_sum_kernel, "far_sum", [core_id, bases[q], got[q], *extra], [shape(512, width), *more]
        )
        low, send = call(
            near_sum_kernel,
            "near_sum",
            [core_id, total, near_got[q], *extra],
            [shape(256, width), shape(256 + pad, width, dtype=bf16)],
        )
        low, send, *extra = call(
            half_sum_kernel,
            "half_sum",
            [core_id, low, flip_permute(send, q + 1), *extra],
            [shape(128, width), shape(128 + pad, width, dtype=bf16), *more],
        )
        lows.append(low)
        last.append(flip_permute(send, q))
        if q == 0:
            loss = extra[0]
    keep, send = call(
        last_sum_kernel, "last_sum", [core_id, *lows, *last, *owns, loss], [shape(392, width), shape(392, width)]
    )
    grad_image, grad_text, loss = call(
        functools.partial(finish_kernel, count),
        "finish",
        [core_id, keep, core_swap(send)],
        [shape(192, width), shape(192, width), shape(1, 1)],
    )
    return loss.reshape(()), grad_image, grad_text


def solution(mesh):
    fine = Mesh(mesh.devices.reshape(4, 4, 4, 2), AXES)
    return jax.shard_map(
        per_device,
        mesh=fine,
        in_specs=(P(AXES, None), P(AXES, None)),
        out_specs=(P(), P(AXES, None), P(AXES, None)),
        check_vma=False,
    )
```

```python
import functools
import itertools
import math

import jax
import jax.numpy as jnp
from jax import lax
from jax.experimental import pallas as pl
from jax.experimental.pallas import tpu as pltpu
from jax.sharding import Mesh, PartitionSpec as P


logit_scale = 10.0
log2e = 1.4426950408889634
ln2 = 0.6931471805599453
lowest = -1e30
f32 = jnp.float32
bf16 = jnp.bfloat16
AXES = ("z", "y", "x", "c")
SWAP = ((0, 1), (1, 0))
FLIPS = ((0, 0, 1), (0, 1, 0), (1, 0, 0))
IMAGE_PAIR = (1, 0, 3, 2)
TEXT_PAIR = (3, 2, 1, 0)
VMEM = pl.BlockSpec(memory_space=pltpu.VMEM)
SMEM = pl.BlockSpec(memory_space=pltpu.SMEM)


def role_pairs(flip):
    pairs = []
    for z, y, x in itertools.product(range(4), repeat=3):
        for core, pair in ((0, IMAGE_PAIR), (1, TEXT_PAIR)):
            target = [pair[v] if f else v for v, f in zip((z, y, x), flip)]
            source_id = ((z * 4 + y) * 4 + x) * 2 + core
            target_id = ((target[0] * 4 + target[1]) * 4 + target[2]) * 2 + core
            pairs.append((source_id, target_id))
    return pairs


ROLE_PAIRS = [role_pairs(flip) for flip in FLIPS]


def flip_permute(x, dim):
    return lax.ppermute(x, AXES, ROLE_PAIRS[dim % 3])


def core_swap(x):
    return lax.ppermute(x, "c", SWAP)


def call(kernel, name, ins, outs, scratch=(), limit=6, flops=0, moved=0):
    in_specs = [SMEM if i == 0 else VMEM for i in range(len(ins))]
    return pl.pallas_call(
        kernel,
        in_specs=in_specs,
        out_specs=[VMEM] * len(outs),
        out_shape=list(outs),
        scratch_shapes=list(scratch),
        compiler_params=pltpu.CompilerParams(vmem_limit_bytes=limit << 20),
        cost_estimate=pl.CostEstimate(flops=flops, bytes_accessed=moved, transcendentals=0),
        name=name,
    )(*ins)


def held(x):
    return pltpu.with_memory_space_constraint(x, pltpu.VMEM)


def shape(*dims, dtype=f32):
    return jax.ShapeDtypeStruct(dims, dtype)


CONTRACT_LAST = (((1,), (1,)), ((), ()))
CONTRACT_FIRST = (((0,), (0,)), ((), ()))


def log_add(a, b):
    top = jnp.maximum(a, b)
    return top + jnp.log2(jnp.exp2(a - top) + jnp.exp2(b - top))


def lane_blocks(x):
    return [x[:, k : k + 128] for k in range(0, x.shape[1], 128)]


def row_stat(logits):
    top = jnp.max(logits, axis=1, keepdims=True)
    total = jnp.sum(jnp.exp2(logits - top), axis=1, keepdims=True)
    lse = top + jnp.log2(total)
    return jnp.concatenate(lane_blocks(jnp.broadcast_to(lse, (lse.shape[0], 128)).T[0:1, :]), 0)


def column_step(logits, state):
    top = jnp.max(logits, axis=0, keepdims=True)
    if state is None:
        return top, jnp.sum(jnp.exp2(logits - top), axis=0, keepdims=True)
    new_top = jnp.maximum(state[0], top)
    total = state[1] * jnp.exp2(state[0] - new_top) + jnp.sum(jnp.exp2(logits - new_top), axis=0, keepdims=True)
    return new_top, total


def column_stat(state):
    return jnp.concatenate(lane_blocks(state[0] + jnp.log2(state[1])), 0)


def product(a, b):
    return lax.dot_general(a, b, CONTRACT_LAST, preferred_element_type=f32) * (logit_scale * log2e)


def place(first, mine, swapped, rows_ref, cols_ref):
    @pl.when(first)
    def _():
        for q in range(3):
            rows_ref[q * 256 : q * 256 + 256, :] = mine[q][0:256, :]
            cols_ref[q * 512 : q * 512 + 512, :] = swapped[q][...]

    @pl.when(jnp.logical_not(first))
    def _():
        for q in range(3):
            rows_ref[q * 256 : q * 256 + 256, :] = swapped[q][256:512, :]
            cols_ref[q * 512 : q * 512 + 512, :] = mine[q][...]


def near_kernel(core_ref, m0, m1, m2, x0, x1, x2, rows_ref, cols_ref, logit_ref, row_out, col_out):
    place(core_ref[0] == 0, (m0, m1, m2), (x0, x1, x2), rows_ref, cols_ref)
    rows, state = [], None
    for q in range(3):
        part = slice(q * 256, q * 256 + 256)
        logit_ref[part, :] = product(rows_ref[part, :], cols_ref[...])
        logits = logit_ref[part, :]
        rows.append(row_stat(logits))
        state = column_step(logits, state)
    row_out[...] = jnp.concatenate(rows, 0)
    col_out[...] = column_stat(state)


def far_kernel(core_ref, *refs):
    mine, swapped = refs[0:3], refs[3:6]
    near_rows, near_cols, row_old, col_old, image_ref, text_ref = refs[6:12]
    rows_ref, cols_ref, *wide_refs = refs[12:17]
    tall_ref, send_ref, keep_ref = refs[17:20]
    first = core_ref[0] == 0
    place(first, mine, swapped, rows_ref, cols_ref)
    new, state = [], None
    for q, wide in enumerate(wide_refs):
        part = slice(q * 256, q * 256 + 256)
        wide[:, 0:1536] = product(rows_ref[part, :], near_cols[...])
        wide[:, 1536:3072] = product(rows_ref[part, :], cols_ref[...])
        logits = wide[...]
        new.append(row_stat(logits))
        state = column_step(logits, state)
    old, tall_state = [], None
    for q in range(3):
        part = slice(q * 256, q * 256 + 256)
        tall_ref[part, :] = product(near_rows[part, :], cols_ref[...])
        logits = tall_ref[part, :]
        old.append(row_stat(logits))
        tall_state = column_step(logits, tall_state)
    row = jnp.concatenate([log_add(row_old[...], jnp.concatenate(old, 0))] + new, 0)
    col = log_add(column_stat(state), jnp.concatenate([col_old[...], column_stat(tall_state)], 0))
    positive = logit_scale * jnp.sum(image_ref[...].astype(f32) * text_ref[...].astype(f32))
    extra = jnp.full((8, 128), positive, f32)
    blank = jnp.full((2, 128), lowest, f32)
    low_half = jnp.concatenate([x for g in range(6) for x in (row[2 * g : 2 * g + 2], blank)], 0)
    high_half = jnp.concatenate([x for g in range(6) for x in (blank, row[2 * g : 2 * g + 2])], 0)
    send_ref[0:24, :] = jnp.where(first, col, high_half)
    keep_ref[0:24, :] = jnp.where(first, low_half, col)
    send_ref[24:32, :] = extra
    keep_ref[24:32, :] = extra


def stack_kernel(core_ref, *refs):
    for q in range(3):
        a, b, out = refs[q], refs[q + 3], refs[q + 6]
        rows = a.shape[0]
        out[0:rows, :] = a[...]
        out[rows : 2 * rows, :] = b[...]


def join_rows_kernel(core_ref, *refs):
    at = 0
    for ref in refs[:-1]:
        rows = ref.shape[0]
        refs[-1][at : at + rows, :] = ref[...]
        at += rows


def join_rows(core_id, parts):
    rows, width = sum(a.shape[0] for a in parts), parts[0].shape[1]
    return call(join_rows_kernel, "join_rows", [core_id, *parts], [shape(rows, width, dtype=bf16)], limit=2)[0]


def gate_kernel(value_ref, token_ref, out_ref):
    pass


def after(value, token):
    return pl.pallas_call(
        gate_kernel,
        in_specs=[VMEM, VMEM],
        out_specs=VMEM,
        out_shape=pltpu.VMEM(value.shape, value.dtype),
        input_output_aliases={0: 0},
        compiler_params=pltpu.CompilerParams(vmem_limit_bytes=1 << 20),
        name="after",
    )(held(value), token)


def join_kernel(order, core_ref, mine_ref, got_ref, out_ref):
    got = got_ref[...]
    out_ref[0:24, :] = log_add(mine_ref[0:24, :], jnp.concatenate([got[k : k + 1, :] for k in order], 0))
    out_ref[24:32, :] = mine_ref[24:32, :] + got_ref[24:32, :]


def flip_order(dim):
    order = []
    for half, q, k in itertools.product(range(2), range(3), range(4)):
        j = (dim - q) % 3
        if j == 2:
            order.append((1 - half) * 12 + q * 4 + k)
        else:
            order.append(half * 12 + q * 4 + (k ^ (1 << j)))
    return order


def tile_lse(first, mine_ref, other_ref):
    mine, other = mine_ref[0:24, :], other_ref[0:24, :]
    row = jnp.where(first, mine, other)
    col = jnp.where(first, other, mine)
    row = [jnp.where(first, row[4 * g + b : 4 * g + b + 1], row[4 * g + b + 2 : 4 * g + b + 3]) for g in range(6) for b in range(2)]
    row = jnp.concatenate(row, 1) + 1.0
    col = jnp.concatenate([col[k : k + 1] for k in range(24)], 1) + 1.0
    return row, col


def coefficients(logits, row, col):
    n = logits.shape[0]
    row = jnp.broadcast_to(row, (128, n)).T[:, 0:1]
    return jnp.exp2(logits - row) + jnp.exp2(logits - col)


def total_of(terms):
    total = terms[0]
    for term in terms[1:]:
        total = total + term
    return logit_scale * total


def times(a, b):
    return jnp.dot(a, b, preferred_element_type=f32)


def transposed_times(a, b):
    return lax.dot_general(a, b, CONTRACT_FIRST, preferred_element_type=f32)


def coeff_kernel(core_ref, mine_ref, other_ref, *refs):
    near_ref, tall_ref, *wide_refs = refs[0:5]
    near_cols, far_cols = refs[5:7]
    coeff_ref, *grad_refs = refs[7:14]
    own_ref, loss_ref = refs[14:16]
    first = core_ref[0] == 0
    row, col = tile_lse(first, mine_ref, other_ref)
    loss_ref[...] = jnp.sum(other_ref[0:24, :]) * ln2 - jnp.where(first, 0.0, 2.0) * other_ref[24:32, :]
    eye = lax.broadcasted_iota(jnp.int32, (128, 128), 0) == lax.broadcasted_iota(jnp.int32, (128, 128), 1)
    positive = jnp.where(jnp.logical_and(eye, first), 1.0, 0.0)
    for g in range(6):
        part = slice(g * 256, g * 256 + 256)
        if g < 3:
            coeffs = coefficients(near_ref[part, :], row[:, part], col[:, 0:1536])
            coeff_ref[part, 0:1536] = coeffs.astype(bf16)
            own = slice(g * 512, g * 512 + 128)
            coeff_ref[g * 256 : g * 256 + 128, own] = (coeffs[0:128, own] - positive).astype(bf16)
            coeff_ref[part, 1536:3072] = coefficients(tall_ref[part, :], row[:, part], col[:, 1536:3072]).astype(bf16)
        else:
            coeff_ref[part, :] = coefficients(wide_refs[g - 3][...], row[:, part], col).astype(bf16)
        grad = total_of(
            [times(coeff_ref[part, 0:1536], near_cols[...]), times(coeff_ref[part, 1536:3072], far_cols[...])]
        )
        grad_refs[g][...] = grad.astype(bf16)
        if g < 3:
            own_ref[g * 128 : g * 128 + 128, :] = grad[0:128, :]


def text_grad(coeff_ref, near_rows, far_rows, start):
    here = slice(start, start + 512)
    return total_of(
        [
            transposed_times(coeff_ref[0:768, here], near_rows[...]),
            transposed_times(coeff_ref[768:1536, here], far_rows[...]),
        ]
    )


def far_text_kernel(q, core_ref, coeff_ref, near_rows, far_rows, image_ref, kept_ref, send_ref):
    first = core_ref[0] == 0
    text = text_grad(coeff_ref, near_rows, far_rows, 1536 + q * 512).astype(bf16)
    image = image_ref[...]
    kept_ref[0:256, :] = jnp.where(first, image, text[0:256])
    send_ref[0:256, :] = jnp.where(first, text[0:256], image)
    kept_ref[256:512, :] = text[256:512]
    send_ref[256:512, :] = text[256:512]


def near_text_kernel(q, core_ref, coeff_ref, near_rows, far_rows, image_ref, own_image, a0, a1, a2, base_ref, send_ref, own_ref):
    first = core_ref[0] == 0
    text = text_grad(coeff_ref, near_rows, far_rows, q * 512)
    image = image_ref[...].astype(f32)
    own_ref[0:128, :] = own_image[q * 128 : q * 128 + 128, :]
    own_ref[128:256, :] = text[0:128]
    base_ref[0:128, :] = jnp.where(first, 0.0, text[0:128])
    base_ref[128:256, :] = jnp.where(first, image[128:256], text[128:256])
    base_ref[256:512, :] = jnp.where(first, 0.0, text[256:512])
    send_ref[0:128, :] = jnp.where(first, 0.0, image[0:128]).astype(bf16)
    send_ref[128:256, :] = jnp.where(first, text[128:256], image[128:256]).astype(bf16)
    send_ref[256:512, :] = text[256:512].astype(bf16)


def split_terms(x):
    high = x.astype(bf16)
    rest = x - high.astype(f32)
    middle = rest.astype(bf16)
    low = (rest - middle.astype(f32)).astype(bf16)
    pair = [jnp.concatenate([t, t], 0) for t in (high, middle, low)]
    return jnp.concatenate(pair + [jnp.zeros((16, 128), bf16)], 1)


def join_terms(ref, start):
    x = ref[start : start + 16, :].astype(f32)
    return (x[0:8, 0:128] + x[0:8, 128:256]) + x[0:8, 256:384]


def far_message_kernel(core_ref, mine_ref, got_ref, *refs):
    first = core_ref[0] == 0
    got = got_ref[...]
    both = (mine_ref[...].astype(f32) + got.astype(f32)).astype(bf16)
    refs[-1][0:256, :] = jnp.where(first, mine_ref[0:256, :], both[0:256])
    refs[-1][256:512, :] = jnp.where(first, got[0:256], both[256:512])
    if len(refs) == 2:
        refs[-1][512:528, :] = split_terms(refs[0][...])


def far_sum_kernel(core_ref, base_ref, got_ref, *refs):
    total_ref = refs[0]
    if len(refs) == 3:
        loss_ref, total_ref, loss_out = refs
        loss_out[...] = loss_ref[...] + join_terms(got_ref, 512)
    total_ref[...] = base_ref[...] + got_ref[0:512, :].astype(f32)


def near_sum_kernel(core_ref, total_ref, got_ref, *refs):
    first = core_ref[0] == 0
    low_ref, send_ref = refs[-2:]
    if len(refs) == 3:
        send_ref[256:272, :] = split_terms(refs[0][...])
    got = got_ref[...].astype(f32)
    low_ref[...] = total_ref[0:256, :] + jnp.where(first, 0.0, got[0:256])
    send_ref[0:256, :] = (total_ref[256:512, :] + jnp.where(first, got[0:256], got[256:512])).astype(bf16)


def half_sum_kernel(core_ref, low_ref, got_ref, *refs):
    if len(refs) == 4:
        loss_ref, out_ref, send_ref, loss_out = refs
        loss = loss_ref[...] + join_terms(got_ref, 256)
        loss_out[...] = loss
        send_ref[128:144, :] = split_terms(loss)
    else:
        out_ref, send_ref = refs
    total = low_ref[...] + got_ref[0:256, :].astype(f32)
    out_ref[...] = total[0:128]
    send_ref[0:128, :] = total[128:256].astype(bf16)


def last_sum_kernel(core_ref, l0, l1, l2, r0, r1, r2, o0, o1, o2, loss_ref, keep_ref, send_ref):
    first = core_ref[0] == 0
    loss = loss_ref[...] + join_terms(r0, 128)
    keep_ref[384:392, :] = jnp.concatenate([loss] * 4, 1)
    send_ref[384:392, :] = jnp.concatenate([loss] * 4, 1)
    for q, (low, r, own) in enumerate(((l0, r0, o0), (l1, r1, o1), (l2, r2, o2))):
        rows, text_rows = slice(q * 64, q * 64 + 64), slice(192 + q * 64, 192 + q * 64 + 64)
        total = low[...] + r[0:128, :].astype(f32)
        keep_ref[rows, :] = jnp.where(first, total[0:64] + own[0:64, :], total[64:128])
        keep_ref[text_rows, :] = own[128:192, :]
        send_ref[rows, :] = jnp.where(first, total[64:128] + own[64:128, :], total[0:64])
        send_ref[text_rows, :] = own[192:256, :]


def finish_kernel(count, core_ref, keep_ref, got_ref, image_out, text_out, loss_out):
    first = core_ref[0] == 0
    image_out[...] = jnp.where(first, keep_ref[0:192, :], got_ref[0:192, :])
    text_out[...] = jnp.where(
        first, got_ref[0:192, :] + keep_ref[192:384, :], keep_ref[0:192, :] + got_ref[192:384, :]
    )
    loss_out[...] = (keep_ref[384:385, 0:1] + got_ref[384:385, 0:1]) * (0.5 / count)


def pair_kernel(core_ref, image_hbm, text_hbm, image_got, text_got, o0, o1, o2, image_ref, text_ref, sems):
    copies = [
        pltpu.make_async_copy(image_hbm, image_ref, sems.at[0]),
        pltpu.make_async_copy(text_hbm, text_ref, sems.at[1]),
    ]
    for copy in copies:
        copy.start()
    for copy in copies:
        copy.wait()
    first = core_ref[0] == 0
    for q, out in enumerate((o0, o1, o2)):
        rows = slice(q * 64, q * 64 + 64)
        out[0:64, :] = jnp.where(first, image_ref[rows, :], text_got[rows, :])
        out[64:128, :] = jnp.where(first, image_got[rows, :], text_ref[rows, :])


def pair(core_id, image_emb, text_emb, image_got, text_got):
    rows, width = image_emb.shape
    anywhere = pl.BlockSpec(memory_space=pl.ANY)
    return pl.pallas_call(
        pair_kernel,
        in_specs=[SMEM, anywhere, anywhere, VMEM, VMEM],
        out_specs=[VMEM] * 3,
        out_shape=[shape(128, width, dtype=bf16)] * 3,
        scratch_shapes=[pltpu.VMEM((rows, width), bf16)] * 2 + [pltpu.SemaphoreType.DMA((2,))],
        compiler_params=pltpu.CompilerParams(vmem_limit_bytes=4 << 20),
        name="pair",
    )(
        core_id,
        pltpu.with_memory_space_constraint(image_emb, pltpu.HBM),
        pltpu.with_memory_space_constraint(text_emb, pltpu.HBM),
        image_got,
        text_got,
    )


def per_device(image_emb, text_emb):
    core_id = lax.axis_index("c").reshape(1).astype(jnp.int32)
    pair_rows, width = image_emb.shape
    count = pair_rows * 128

    got = [core_swap(image_emb), core_swap(text_emb)]
    near = pair(core_id, image_emb, text_emb, *got)
    got = [flip_permute(near[q], q) for q in range(3)]
    near = call(stack_kernel, "stack", [core_id, *near, *got], [shape(256, width, dtype=bf16)] * 3, limit=2)
    near = [join_rows(core_id, [near[q], flip_permute(near[q], q + 1)]) for q in range(3)]
    near_x = [core_swap(a) for a in near]
    far = [flip_permute(near[q], q + 2) for q in range(3)]

    near_rows, near_cols, near_logits, row, col = call(
        near_kernel,
        "near",
        [core_id, *near, *near_x],
        [pltpu.VMEM((768, width), bf16), pltpu.VMEM((1536, width), bf16), pltpu.VMEM((768, 1536), f32)]
        + [shape(6, 128), shape(12, 128)],
        limit=10,
        flops=2 * 768 * 1536 * width,
    )
    far_x = [core_swap(a) for a in far]
    far_rows, far_cols, *logits, send, keep = call(
        far_kernel,
        "far",
        [core_id, *far, *far_x, held(near_rows), held(near_cols), row, col, image_emb, text_emb],
        [pltpu.VMEM((768, width), bf16), pltpu.VMEM((1536, width), bf16)]
        + [pltpu.VMEM((256, 3072), f32)] * 3
        + [pltpu.VMEM((768, 1536), f32), shape(32, 128), shape(32, 128)],
        limit=10,
        flops=2 * 768 * 4608 * width,
    )
    *wide_logits, tall_logits = logits

    mine = call(functools.partial(join_kernel, list(range(24))), "join", [core_id, keep, core_swap(send)], [shape(32, 128)], limit=2)[0]
    for dim in range(3):
        got = flip_permute(mine, dim)
        mine = call(functools.partial(join_kernel, flip_order(dim)), "join", [core_id, mine, got], [shape(32, 128)], limit=2)[0]
    other = core_swap(mine)

    held_rows = [held(near_rows), held(far_rows)]
    coeffs, *image_grads, own_image, loss = call(
        coeff_kernel,
        "coeffs",
        [core_id, mine, other]
        + [held(a) for a in (near_logits, tall_logits, *wide_logits, near_cols, far_cols)],
        [pltpu.VMEM((1536, 3072), bf16)] + [shape(256, width, dtype=bf16)] * 6 + [shape(384, width), shape(8, 128)],
        limit=10,
        flops=2 * 1536 * 3072 * width,
    )
    messages = []
    for q in range(3):
        kept, send = call(
            functools.partial(far_text_kernel, q),
            "far_text",
            [core_id, held(coeffs), *held_rows, image_grads[3 + q]],
            [shape(512, width, dtype=bf16)] * 2,
            limit=6,
            flops=2 * 1536 * 512 * width,
        )
        ins = [core_id, kept, core_swap(send)] + ([loss] if q == 0 else [])
        outs = [shape(528 if q == 0 else 512, width, dtype=bf16)]
        messages.append(call(far_message_kernel, "far_message", ins, outs)[0])
    got = [flip_permute(messages[q], q + 2) for q in range(3)]
    bases, near_got, owns = [], [], []
    for q in range(3):
        base, send, own = call(
            functools.partial(near_text_kernel, q),
            "near_text",
            [core_id, held(coeffs), *held_rows, image_grads[q], own_image, *messages],
            [shape(512, width), shape(512, width, dtype=bf16), shape(256, width)],
            limit=6,
            flops=2 * 1536 * 512 * width,
        )
        bases.append(base)
        near_got.append(core_swap(send))
        owns.append(own)
    lows, last = [], []
    for q in range(3):
        extra = [loss] if q == 0 else []
        more = [shape(8, 128)] if q == 0 else []
        pad = 16 if q == 0 else 0
        total, *extra = call(
            far_sum_kernel, "far_sum", [core_id, bases[q], got[q], *extra], [shape(512, width), *more]
        )
        low, send = call(
            near_sum_kernel,
            "near_sum",
            [core_id, total, near_got[q], *extra],
            [shape(256, width), shape(256 + pad, width, dtype=bf16)],
        )
        low, send, *extra = call(
            half_sum_kernel,
            "half_sum",
            [core_id, low, flip_permute(send, q + 1), *extra],
            [shape(128, width), shape(128 + pad, width, dtype=bf16), *more],
        )
        lows.append(low)
        last.append(flip_permute(send, q))
        if q == 0:
            loss = extra[0]
    keep, send = call(
        last_sum_kernel, "last_sum", [core_id, *lows, *last, *owns, loss], [shape(392, width), shape(392, width)]
    )
    grad_image, grad_text, loss = call(
        functools.partial(finish_kernel, count),
        "finish",
        [core_id, keep, core_swap(send)],
        [shape(192, width), shape(192, width), shape(1, 1)],
    )
    return loss.reshape(()), grad_image, grad_text


def solution(mesh):
    fine = Mesh(mesh.devices.reshape(4, 4, 4, 2), AXES)
    return jax.shard_map(
        per_device,
        mesh=fine,
        in_specs=(P(AXES, None), P(AXES, None)),
        out_specs=(P(), P(AXES, None), P(AXES, None)),
        check_vma=False,
    )
```

```python
import functools
import itertools
import math

import jax
import jax.numpy as jnp
from jax import lax
from jax.experimental import pallas as pl
from jax.experimental.pallas import tpu as pltpu
from jax.sharding import Mesh, PartitionSpec as P


logit_scale = 10.0
log2e = 1.4426950408889634
ln2 = 0.6931471805599453
lowest = -1e30
f32 = jnp.float32
bf16 = jnp.bfloat16
AXES = ("z", "y", "x", "c")
SWAP = ((0, 1), (1, 0))
FLIPS = ((0, 0, 1), (0, 1, 0), (1, 0, 0))
IMAGE_PAIR = (1, 0, 3, 2)
TEXT_PAIR = (3, 2, 1, 0)
VMEM = pl.BlockSpec(memory_space=pltpu.VMEM)
SMEM = pl.BlockSpec(memory_space=pltpu.SMEM)


def role_pairs(flip):
    pairs = []
    for z, y, x in itertools.product(range(4), repeat=3):
        for core, pair in ((0, IMAGE_PAIR), (1, TEXT_PAIR)):
            target = [pair[v] if f else v for v, f in zip((z, y, x), flip)]
            source_id = ((z * 4 + y) * 4 + x) * 2 + core
            target_id = ((target[0] * 4 + target[1]) * 4 + target[2]) * 2 + core
            pairs.append((source_id, target_id))
    return pairs


ROLE_PAIRS = [role_pairs(flip) for flip in FLIPS]


def flip_permute(x, dim):
    return lax.ppermute(x, AXES, ROLE_PAIRS[dim % 3])


def core_swap(x):
    return lax.ppermute(x, "c", SWAP)


def call(kernel, name, ins, outs, scratch=(), limit=6, flops=0, moved=0):
    in_specs = [SMEM if i == 0 else VMEM for i in range(len(ins))]
    return pl.pallas_call(
        kernel,
        in_specs=in_specs,
        out_specs=[VMEM] * len(outs),
        out_shape=list(outs),
        scratch_shapes=list(scratch),
        compiler_params=pltpu.CompilerParams(vmem_limit_bytes=limit << 20),
        cost_estimate=pl.CostEstimate(flops=flops, bytes_accessed=moved, transcendentals=0),
        name=name,
    )(*ins)


def held(x):
    return pltpu.with_memory_space_constraint(x, pltpu.VMEM)


def shape(*dims, dtype=f32):
    return jax.ShapeDtypeStruct(dims, dtype)


CONTRACT_LAST = (((1,), (1,)), ((), ()))
CONTRACT_FIRST = (((0,), (0,)), ((), ()))


def log_add(a, b):
    top = jnp.maximum(a, b)
    return top + jnp.log2(jnp.exp2(a - top) + jnp.exp2(b - top))


def lane_blocks(x):
    return [x[:, k : k + 128] for k in range(0, x.shape[1], 128)]


def row_stat(logits):
    top = jnp.max(logits, axis=1, keepdims=True)
    total = jnp.sum(jnp.exp2(logits - top), axis=1, keepdims=True)
    lse = top + jnp.log2(total)
    return jnp.concatenate(lane_blocks(jnp.broadcast_to(lse, (lse.shape[0], 128)).T[0:1, :]), 0)


def column_step(logits, state):
    top = jnp.max(logits, axis=0, keepdims=True)
    if state is None:
        return top, jnp.sum(jnp.exp2(logits - top), axis=0, keepdims=True)
    new_top = jnp.maximum(state[0], top)
    total = state[1] * jnp.exp2(state[0] - new_top) + jnp.sum(jnp.exp2(logits - new_top), axis=0, keepdims=True)
    return new_top, total


def column_stat(state):
    return jnp.concatenate(lane_blocks(state[0] + jnp.log2(state[1])), 0)


def product(a, b):
    return lax.dot_general(a, b, CONTRACT_LAST, preferred_element_type=f32) * (logit_scale * log2e)


def place(first, mine, swapped, rows_ref, cols_ref):
    @pl.when(first)
    def _():
        for q in range(3):
            rows_ref[q * 256 : q * 256 + 256, :] = mine[q][0:256, :]
            cols_ref[q * 512 : q * 512 + 512, :] = swapped[q][...]

    @pl.when(jnp.logical_not(first))
    def _():
        for q in range(3):
            rows_ref[q * 256 : q * 256 + 256, :] = swapped[q][256:512, :]
            cols_ref[q * 512 : q * 512 + 512, :] = mine[q][...]


def near_kernel(core_ref, m0, m1, m2, x0, x1, x2, rows_ref, cols_ref, logit_ref, row_out, col_out):
    place(core_ref[0] == 0, (m0, m1, m2), (x0, x1, x2), rows_ref, cols_ref)
    rows, state = [], None
    for q in range(3):
        part = slice(q * 256, q * 256 + 256)
        logit_ref[part, :] = product(rows_ref[part, :], cols_ref[...])
        logits = logit_ref[part, :]
        rows.append(row_stat(logits))
        state = column_step(logits, state)
    row_out[...] = jnp.concatenate(rows, 0)
    col_out[...] = column_stat(state)


def far_kernel(core_ref, *refs):
    mine, swapped = refs[0:3], refs[3:6]
    near_rows, near_cols, row_old, col_old, image_ref, text_ref = refs[6:12]
    rows_ref, cols_ref, *wide_refs = refs[12:17]
    tall_ref, send_ref, keep_ref = refs[17:20]
    first = core_ref[0] == 0
    place(first, mine, swapped, rows_ref, cols_ref)
    new, state = [], None
    for q, wide in enumerate(wide_refs):
        part = slice(q * 256, q * 256 + 256)
        wide[:, 0:1536] = product(rows_ref[part, :], near_cols[...])
        wide[:, 1536:3072] = product(rows_ref[part, :], cols_ref[...])
        logits = wide[...]
        new.append(row_stat(logits))
        state = column_step(logits, state)
    old, tall_state = [], None
    for q in range(3):
        part = slice(q * 256, q * 256 + 256)
        tall_ref[part, :] = product(near_rows[part, :], cols_ref[...])
        logits = tall_ref[part, :]
        old.append(row_stat(logits))
        tall_state = column_step(logits, tall_state)
    row = jnp.concatenate([log_add(row_old[...], jnp.concatenate(old, 0))] + new, 0)
    col = log_add(column_stat(state), jnp.concatenate([col_old[...], column_stat(tall_state)], 0))
    positive = logit_scale * jnp.sum(image_ref[...].astype(f32) * text_ref[...].astype(f32))
    extra = jnp.full((8, 128), positive, f32)
    blank = jnp.full((2, 128), lowest, f32)
    low_half = jnp.concatenate([x for g in range(6) for x in (row[2 * g : 2 * g + 2], blank)], 0)
    high_half = jnp.concatenate([x for g in range(6) for x in (blank, row[2 * g : 2 * g + 2])], 0)
    send_ref[0:24, :] = jnp.where(first, col, high_half)
    keep_ref[0:24, :] = jnp.where(first, low_half, col)
    send_ref[24:32, :] = extra
    keep_ref[24:32, :] = extra


def stack_kernel(core_ref, *refs):
    for q in range(3):
        a, b, out = refs[q], refs[q + 3], refs[q + 6]
        rows = a.shape[0]
        out[0:rows, :] = a[...]
        out[rows : 2 * rows, :] = b[...]


def join_rows_kernel(core_ref, *refs):
    at = 0
    for ref in refs[:-1]:
        rows = ref.shape[0]
        refs[-1][at : at + rows, :] = ref[...]
        at += rows


def join_rows(core_id, parts):
    rows, width = sum(a.shape[0] for a in parts), parts[0].shape[1]
    return call(join_rows_kernel, "join_rows", [core_id, *parts], [shape(rows, width, dtype=bf16)], limit=2)[0]


def gate_kernel(value_ref, token_ref, out_ref):
    pass


def after(value, token):
    return pl.pallas_call(
        gate_kernel,
        in_specs=[VMEM, VMEM],
        out_specs=VMEM,
        out_shape=pltpu.VMEM(value.shape, value.dtype),
        input_output_aliases={0: 0},
        compiler_params=pltpu.CompilerParams(vmem_limit_bytes=1 << 20),
        name="after",
    )(held(value), token)


def join_kernel(order, core_ref, mine_ref, got_ref, out_ref):
    got = got_ref[...]
    out_ref[0:24, :] = log_add(mine_ref[0:24, :], jnp.concatenate([got[k : k + 1, :] for k in order], 0))
    out_ref[24:32, :] = mine_ref[24:32, :] + got_ref[24:32, :]


def flip_order(dim):
    order = []
    for half, q, k in itertools.product(range(2), range(3), range(4)):
        j = (dim - q) % 3
        if j == 2:
            order.append((1 - half) * 12 + q * 4 + k)
        else:
            order.append(half * 12 + q * 4 + (k ^ (1 << j)))
    return order


def tile_lse(first, mine_ref, other_ref):
    mine, other = mine_ref[0:24, :], other_ref[0:24, :]
    row = jnp.where(first, mine, other)
    col = jnp.where(first, other, mine)
    row = [jnp.where(first, row[4 * g + b : 4 * g + b + 1], row[4 * g + b + 2 : 4 * g + b + 3]) for g in range(6) for b in range(2)]
    row = jnp.concatenate(row, 1) + 1.0
    col = jnp.concatenate([col[k : k + 1] for k in range(24)], 1) + 1.0
    return row, col


def coefficients(logits, row, col):
    n = logits.shape[0]
    row = jnp.broadcast_to(row, (128, n)).T[:, 0:1]
    return jnp.exp2(logits - row) + jnp.exp2(logits - col)


def total_of(terms):
    total = terms[0]
    for term in terms[1:]:
        total = total + term
    return logit_scale * total


def times(a, b):
    return jnp.dot(a, b, preferred_element_type=f32)


def transposed_times(a, b):
    return lax.dot_general(a, b, CONTRACT_FIRST, preferred_element_type=f32)


def coeff_kernel(core_ref, mine_ref, other_ref, *refs):
    near_ref, tall_ref, *wide_refs = refs[0:5]
    near_cols, far_cols = refs[5:7]
    coeff_ref, *grad_refs = refs[7:14]
    own_ref, loss_ref = refs[14:16]
    first = core_ref[0] == 0
    row, col = tile_lse(first, mine_ref, other_ref)
    loss_ref[...] = jnp.sum(other_ref[0:24, :]) * ln2 - jnp.where(first, 0.0, 2.0) * other_ref[24:32, :]
    eye = lax.broadcasted_iota(jnp.int32, (128, 128), 0) == lax.broadcasted_iota(jnp.int32, (128, 128), 1)
    positive = jnp.where(jnp.logical_and(eye, first), 1.0, 0.0)
    for g in range(6):
        part = slice(g * 256, g * 256 + 256)
        if g < 3:
            coeffs = coefficients(near_ref[part, :], row[:, part], col[:, 0:1536])
            coeff_ref[part, 0:1536] = coeffs.astype(bf16)
            own = slice(g * 512, g * 512 + 128)
            coeff_ref[g * 256 : g * 256 + 128, own] = (coeffs[0:128, own] - positive).astype(bf16)
            coeff_ref[part, 1536:3072] = coefficients(tall_ref[part, :], row[:, part], col[:, 1536:3072]).astype(bf16)
        else:
            coeff_ref[part, :] = coefficients(wide_refs[g - 3][...], row[:, part], col).astype(bf16)
        grad = total_of(
            [times(coeff_ref[part, 0:1536], near_cols[...]), times(coeff_ref[part, 1536:3072], far_cols[...])]
        )
        grad_refs[g][...] = grad.astype(bf16)
        if g < 3:
            own_ref[g * 128 : g * 128 + 128, :] = grad[0:128, :]


def text_grad(coeff_ref, near_rows, far_rows, start):
    here = slice(start, start + 512)
    return total_of(
        [
            transposed_times(coeff_ref[0:768, here], near_rows[...]),
            transposed_times(coeff_ref[768:1536, here], far_rows[...]),
        ]
    )


def far_text_kernel(q, core_ref, coeff_ref, near_rows, far_rows, image_ref, kept_ref, send_ref):
    first = core_ref[0] == 0
    text = text_grad(coeff_ref, near_rows, far_rows, 1536 + q * 512).astype(bf16)
    image = image_ref[...]
    kept_ref[0:256, :] = jnp.where(first, image, text[0:256])
    send_ref[0:256, :] = jnp.where(first, text[0:256], image)
    kept_ref[256:512, :] = text[256:512]
    send_ref[256:512, :] = text[256:512]


def near_text_kernel(q, core_ref, coeff_ref, near_rows, far_rows, image_ref, own_image, a0, a1, a2, base_ref, send_ref, own_ref):
    first = core_ref[0] == 0
    text = text_grad(coeff_ref, near_rows, far_rows, q * 512)
    image = image_ref[...].astype(f32)
    own_ref[0:128, :] = own_image[q * 128 : q * 128 + 128, :]
    own_ref[128:256, :] = text[0:128]
    base_ref[0:128, :] = jnp.where(first, 0.0, text[0:128])
    base_ref[128:256, :] = jnp.where(first, image[128:256], text[128:256])
    base_ref[256:512, :] = jnp.where(first, 0.0, text[256:512])
    send_ref[0:128, :] = jnp.where(first, 0.0, image[0:128]).astype(bf16)
    send_ref[128:256, :] = jnp.where(first, text[128:256], image[128:256]).astype(bf16)
    send_ref[256:512, :] = text[256:512].astype(bf16)


def split_terms(x):
    high = x.astype(bf16)
    rest = x - high.astype(f32)
    middle = rest.astype(bf16)
    low = (rest - middle.astype(f32)).astype(bf16)
    pair = [jnp.concatenate([t, t], 0) for t in (high, middle, low)]
    return jnp.concatenate(pair + [jnp.zeros((16, 128), bf16)], 1)


def join_terms(ref, start):
    x = ref[start : start + 16, :].astype(f32)
    return (x[0:8, 0:128] + x[0:8, 128:256]) + x[0:8, 256:384]


def far_message_kernel(core_ref, mine_ref, got_ref, *refs):
    first = core_ref[0] == 0
    got = got_ref[...]
    both = (mine_ref[...].astype(f32) + got.astype(f32)).astype(bf16)
    refs[-1][0:256, :] = jnp.where(first, mine_ref[0:256, :], both[0:256])
    refs[-1][256:512, :] = jnp.where(first, got[0:256], both[256:512])
    if len(refs) == 2:
        refs[-1][512:528, :] = split_terms(refs[0][...])


def far_sum_kernel(core_ref, base_ref, got_ref, *refs):
    total_ref = refs[0]
    if len(refs) == 3:
        loss_ref, total_ref, loss_out = refs
        loss_out[...] = loss_ref[...] + join_terms(got_ref, 512)
    total_ref[...] = base_ref[...] + got_ref[0:512, :].astype(f32)


def near_sum_kernel(core_ref, total_ref, got_ref, *refs):
    first = core_ref[0] == 0
    low_ref, send_ref = refs[-2:]
    if len(refs) == 3:
        send_ref[256:272, :] = split_terms(refs[0][...])
    got = got_ref[...].astype(f32)
    low_ref[...] = total_ref[0:256, :] + jnp.where(first, 0.0, got[0:256])
    send_ref[0:256, :] = (total_ref[256:512, :] + jnp.where(first, got[0:256], got[256:512])).astype(bf16)


def half_sum_kernel(core_ref, low_ref, got_ref, *refs):
    if len(refs) == 4:
        loss_ref, out_ref, send_ref, loss_out = refs
        loss = loss_ref[...] + join_terms(got_ref, 256)
        loss_out[...] = loss
        send_ref[128:144, :] = split_terms(loss)
    else:
        out_ref, send_ref = refs
    total = low_ref[...] + got_ref[0:256, :].astype(f32)
    out_ref[...] = total[0:128]
    send_ref[0:128, :] = total[128:256].astype(bf16)


def last_sum_kernel(core_ref, l0, l1, l2, r0, r1, r2, o0, o1, o2, loss_ref, keep_ref, send_ref):
    first = core_ref[0] == 0
    loss = loss_ref[...] + join_terms(r0, 128)
    keep_ref[384:392, :] = jnp.concatenate([loss] * 4, 1)
    send_ref[384:392, :] = jnp.concatenate([loss] * 4, 1)
    for q, (low, r, own) in enumerate(((l0, r0, o0), (l1, r1, o1), (l2, r2, o2))):
        rows, text_rows = slice(q * 64, q * 64 + 64), slice(192 + q * 64, 192 + q * 64 + 64)
        total = low[...] + r[0:128, :].astype(f32)
        keep_ref[rows, :] = jnp.where(first, total[0:64] + own[0:64, :], total[64:128])
        keep_ref[text_rows, :] = own[128:192, :]
        send_ref[rows, :] = jnp.where(first, total[64:128] + own[64:128, :], total[0:64])
        send_ref[text_rows, :] = own[192:256, :]


def finish_kernel(count, core_ref, keep_ref, got_ref, image_out, text_out, loss_out):
    first = core_ref[0] == 0
    image_out[...] = jnp.where(first, keep_ref[0:192, :], got_ref[0:192, :])
    text_out[...] = jnp.where(
        first, got_ref[0:192, :] + keep_ref[192:384, :], keep_ref[0:192, :] + got_ref[192:384, :]
    )
    loss_out[...] = (keep_ref[384:385, 0:1] + got_ref[384:385, 0:1]) * (0.5 / count)


def pair_kernel(core_ref, image_hbm, text_hbm, image_got, text_got, o0, o1, o2, own_ref, sem):
    first = core_ref[0] == 0

    @pl.when(first)
    def _():
        copy = pltpu.make_async_copy(image_hbm, own_ref, sem)
        copy.start()
        copy.wait()

    @pl.when(jnp.logical_not(first))
    def _():
        copy = pltpu.make_async_copy(text_hbm, own_ref, sem)
        copy.start()
        copy.wait()

    for q, out in enumerate((o0, o1, o2)):
        rows = slice(q * 64, q * 64 + 64)
        out[0:64, :] = jnp.where(first, own_ref[rows, :], text_got[rows, :])
        out[64:128, :] = jnp.where(first, image_got[rows, :], own_ref[rows, :])


def pair(core_id, image_emb, text_emb, image_got, text_got):
    rows, width = image_emb.shape
    anywhere = pl.BlockSpec(memory_space=pl.ANY)
    return pl.pallas_call(
        pair_kernel,
        in_specs=[SMEM, anywhere, anywhere, VMEM, VMEM],
        out_specs=[VMEM] * 3,
        out_shape=[shape(128, width, dtype=bf16)] * 3,
        scratch_shapes=[pltpu.VMEM((rows, width), bf16), pltpu.SemaphoreType.DMA],
        compiler_params=pltpu.CompilerParams(vmem_limit_bytes=4 << 20),
        name="pair",
    )(
        core_id,
        pltpu.with_memory_space_constraint(image_emb, pltpu.HBM),
        pltpu.with_memory_space_constraint(text_emb, pltpu.HBM),
        image_got,
        text_got,
    )


def per_device(image_emb, text_emb):
    core_id = lax.axis_index("c").reshape(1).astype(jnp.int32)
    pair_rows, width = image_emb.shape
    count = pair_rows * 128

    got = [core_swap(image_emb), core_swap(text_emb)]
    near = pair(core_id, image_emb, text_emb, *got)
    got = [flip_permute(near[q], q) for q in range(3)]
    near = call(stack_kernel, "stack", [core_id, *near, *got], [shape(256, width, dtype=bf16)] * 3, limit=2)
    near = [join_rows(core_id, [near[q], flip_permute(near[q], q + 1)]) for q in range(3)]
    near_x = [core_swap(a) for a in near]
    far = [flip_permute(near[q], q + 2) for q in range(3)]

    near_rows, near_cols, near_logits, row, col = call(
        near_kernel,
        "near",
        [core_id, *near, *near_x],
        [pltpu.VMEM((768, width), bf16), pltpu.VMEM((1536, width), bf16), pltpu.VMEM((768, 1536), f32)]
        + [shape(6, 128), shape(12, 128)],
        limit=10,
        flops=2 * 768 * 1536 * width,
    )
    far_x = [core_swap(a) for a in far]
    far_rows, far_cols, *logits, send, keep = call(
        far_kernel,
        "far",
        [core_id, *far, *far_x, held(near_rows), held(near_cols), row, col, image_emb, text_emb],
        [pltpu.VMEM((768, width), bf16), pltpu.VMEM((1536, width), bf16)]
        + [pltpu.VMEM((256, 3072), f32)] * 3
        + [pltpu.VMEM((768, 1536), f32), shape(32, 128), shape(32, 128)],
        limit=10,
        flops=2 * 768 * 4608 * width,
    )
    *wide_logits, tall_logits = logits

    mine = call(functools.partial(join_kernel, list(range(24))), "join", [core_id, keep, core_swap(send)], [shape(32, 128)], limit=2)[0]
    for dim in range(3):
        got = flip_permute(mine, dim)
        mine = call(functools.partial(join_kernel, flip_order(dim)), "join", [core_id, mine, got], [shape(32, 128)], limit=2)[0]
    other = core_swap(mine)

    held_rows = [held(near_rows), held(far_rows)]
    coeffs, *image_grads, own_image, loss = call(
        coeff_kernel,
        "coeffs",
        [core_id, mine, other]
        + [held(a) for a in (near_logits, tall_logits, *wide_logits, near_cols, far_cols)],
        [pltpu.VMEM((1536, 3072), bf16)] + [shape(256, width, dtype=bf16)] * 6 + [shape(384, width), shape(8, 128)],
        limit=10,
        flops=2 * 1536 * 3072 * width,
    )
    messages = []
    for q in range(3):
        kept, send = call(
            functools.partial(far_text_kernel, q),
            "far_text",
            [core_id, held(coeffs), *held_rows, image_grads[3 + q]],
            [shape(512, width, dtype=bf16)] * 2,
            limit=6,
            flops=2 * 1536 * 512 * width,
        )
        ins = [core_id, kept, core_swap(send)] + ([loss] if q == 0 else [])
        outs = [shape(528 if q == 0 else 512, width, dtype=bf16)]
        messages.append(call(far_message_kernel, "far_message", ins, outs)[0])
    got = [flip_permute(messages[q], q + 2) for q in range(3)]
    bases, near_got, owns = [], [], []
    for q in range(3):
        base, send, own = call(
            functools.partial(near_text_kernel, q),
            "near_text",
            [core_id, held(coeffs), *held_rows, image_grads[q], own_image, *messages],
            [shape(512, width), shape(512, width, dtype=bf16), shape(256, width)],
            limit=6,
            flops=2 * 1536 * 512 * width,
        )
        bases.append(base)
        near_got.append(core_swap(send))
        owns.append(own)
    lows, last = [], []
    for q in range(3):
        extra = [loss] if q == 0 else []
        more = [shape(8, 128)] if q == 0 else []
        pad = 16 if q == 0 else 0
        total, *extra = call(
            far_sum_kernel, "far_sum", [core_id, bases[q], got[q], *extra], [shape(512, width), *more]
        )
        low, send = call(
            near_sum_kernel,
            "near_sum",
            [core_id, total, near_got[q], *extra],
            [shape(256, width), shape(256 + pad, width, dtype=bf16)],
        )
        low, send, *extra = call(
            half_sum_kernel,
            "half_sum",
            [core_id, low, flip_permute(send, q + 1), *extra],
            [shape(128, width), shape(128 + pad, width, dtype=bf16), *more],
        )
        lows.append(low)
        last.append(flip_permute(send, q))
        if q == 0:
            loss = extra[0]
    keep, send = call(
        last_sum_kernel, "last_sum", [core_id, *lows, *last, *owns, loss], [shape(392, width), shape(392, width)]
    )
    grad_image, grad_text, loss = call(
        functools.partial(finish_kernel, count),
        "finish",
        [core_id, keep, core_swap(send)],
        [shape(192, width), shape(192, width), shape(1, 1)],
    )
    return loss.reshape(()), grad_image, grad_text


def solution(mesh):
    fine = Mesh(mesh.devices.reshape(4, 4, 4, 2), AXES)
    return jax.shard_map(
        per_device,
        mesh=fine,
        in_specs=(P(AXES, None), P(AXES, None)),
        out_specs=(P(), P(AXES, None), P(AXES, None)),
        check_vma=False,
    )
```
